128 devices in a mesh: tm: 4 (over x_lo, core), height: 32 (over x_hi, y, z).
Axes of the slice: x: 4 (x_hi: 2, x_lo: 2; x = x_hi * 2 + x_lo), y: 4, z: 4, core: 2. Of those that a mesh axis runs over, the one named last changes fastest.
Arguments:
- hidden: bfloat16 [12, 64, 48, 3072], P(None, 'height', 'tm'), may hold values from -6 to 6
- mod_scale: float32 [3072], replicated, may hold values from -2.5 to 2.5
- mod_shift: float32 [3072], replicated, may hold values from -4 to 4
- w_out: bfloat16 [3072, 64], replicated, may hold values from -0.109375 to 0.109375
- w_in: bfloat16 [3, 3, 3, 16, 512], replicated, may hold values from -0.3125 to 0.3125
- w_section: bfloat16 [3, 3, 3, 512, 512], replicated, may hold values from -0.0546875 to 0.0546875
- section_grad: bfloat16 [12, 128, 96, 512], P('tm', 'height'), may hold values from -6 to 6
Outputs:
- grad_hidden: bfloat16 [12, 64, 48, 3072], P(None, 'height', 'tm')
- grad_out_weight: float32 [3072, 64], P(('tm', 'height'))
The draws below stay inside these ranges and needn't reach their ends.
All inputs are finite; a program needn't handle non-finite values.
Results may differ from the reference program's by a relative error of at most 0.015.
Values may be sent and summed in bfloat16 or wider, within the bound.
No kernel may reach another device: no remote copies, remote signals or barrier semaphores. Data moves between devices by JAX's collectives and lax.ppermute only.
A program may use at most 128 MiB of HBM per device.

```python
import math
import jax
import jax.numpy as jnp
from jax import lax

D = 3072
C = 512
LAT = 16
LW = 96
FRAMES = 12
LH = 128


def spiked(array, key, source, target, blocks, factor):
    owner, partner = [(jnp.arange(array.shape[dim]) // (array.shape[dim] // blocks)).reshape([-1 if axis == dim else 1 for axis in range(array.ndim)]) for dim in (source, target)]
    chosen = jax.random.permutation(key, blocks)[partner]
    strong = (owner == chosen) | (owner == (partner + blocks // 2) % blocks)
    return jnp.where(strong, factor * array, array)


def block_scale(stream_key, extent, shards, smallest, top_value):
    factor_of, own = 1.0, jax.random.fold_in(stream_key, 6)
    for axis_at, blocks in shards:
        heights = jnp.exp(jax.random.uniform(jax.random.fold_in(own, axis_at), (blocks,), jnp.float32, smallest / len(shards), top_value / len(shards)))
        factor_of = factor_of * jnp.repeat(heights, extent[axis_at] // blocks).reshape([-1 if axis == axis_at else 1 for axis in range(len(extent))])
    return factor_of


def bell_draw(key, dims, width, most, cuts=(), kind=jnp.bfloat16):
    array = width * jax.random.normal(key, dims, jnp.float32)
    if cuts:
        array = array * block_scale(key, dims, cuts, -0.22, 0.18)
    return jnp.clip(array, -most, most).astype(kind)


def bell_draw_with(stream_key, shape, deviation, limit, shards, heavy, held_as=jnp.bfloat16):
    result = deviation * jax.random.normal(stream_key, shape, jnp.float32)
    if shards:
        result = result * block_scale(stream_key, shape, shards, -0.22, 0.18)
    return jnp.clip(spiked(result, jax.random.fold_in(stream_key, 3), *heavy), -limit, limit).astype(held_as)


def setup_inputs(seed: int = 0) -> dict:
    key_list = jax.random.split(jax.random.key(seed), 8)
    hidden = bell_draw_with(key_list[0], (FRAMES, LH // 2, LW // 2, D), 1.0, 6.0, ((1, 32), (2, 4)), (1, 3, 32, 2.75))
    mod_scale = bell_draw(key_list[1], (D,), 0.5, 2.5, (), jnp.float32)
    mod_shift = bell_draw(key_list[2], (D,), 1.0, 4.0, (), jnp.float32)
    w_out = bell_draw(key_list[3], (D, 4 * LAT), D ** -0.5, 0.109375)
    w_in = bell_draw(key_list[4], (3, 3, 3, LAT, C), (27 * LAT) ** -0.5, 0.3125)
    w_section = bell_draw(key_list[5], (3, 3, 3, C, C), (27 * C) ** -0.5, 0.0546875)
    section_grad = bell_draw(key_list[6], (FRAMES, LH, LW, C), 1.0, 6.0, ((0, 4), (1, 32)))
    return dict(hidden=hidden, mod_scale=mod_scale, mod_shift=mod_shift, w_out=w_out, w_in=w_in, w_section=w_section, section_grad=section_grad)


epsilon = 1e-05

def modulate(hidden, mod_scale, mod_shift):
    values = hidden.astype(jnp.float32)
    center = lax.optimization_barrier(jnp.mean(values, axis=-1, keepdims=True))
    spread = lax.optimization_barrier(jnp.mean((values - center) * (values - center), axis=-1, keepdims=True))
    inverse = lax.rsqrt(spread + epsilon)
    normed = (values - center) * inverse
    modulated = (normed * (1.0 + mod_scale) + mod_shift).astype(jnp.bfloat16)
    return (normed, inverse, modulated)

def to_grid(tokens):
    frame_count, row_count, col_count, token_width = tokens.shape
    lat_width = token_width // 4
    blocks = tokens.reshape(frame_count, row_count, col_count, 2, 2, lat_width)
    blocks = jnp.transpose(blocks, (0, 1, 3, 2, 4, 5))
    return blocks.reshape(frame_count, 2 * row_count, 2 * col_count, lat_width)

def to_tokens(field):
    frame_count, row_count, col_count, lat_width = field.shape
    blocks = field.reshape(frame_count, row_count // 2, 2, col_count // 2, 2, lat_width)
    blocks = jnp.transpose(blocks, (0, 1, 3, 2, 4, 5))
    return blocks.reshape(frame_count, row_count // 2, col_count // 2, 4 * lat_width)

def input_conv(latent_win, w_in, row_count, col_count):
    pieces = []
    for tap_time in range(3):
        for tap_row in range(3):
            for tap_col in range(3):
                pieces.append(latent_win[tap_time, tap_row:tap_row + row_count, tap_col:tap_col + col_count])
    stacked = jnp.concatenate(pieces, axis=-1)
    flat_weight = w_in.reshape(-1, w_in.shape[-1])
    preact = jnp.dot(stacked.reshape(row_count * col_count, -1), flat_weight, preferred_element_type=jnp.float32)
    return preact.reshape(row_count, col_count, -1)

def section_back(grad_win, w_section, row_count, col_count):
    channels = w_section.shape[3]
    running = jnp.zeros((row_count * col_count, channels), jnp.float32)
    for tap_time in range(3):
        for tap_row in range(3):
            pieces = [grad_win[2 - tap_time, 2 - tap_row:2 - tap_row + row_count, 2 - tap_col:2 - tap_col + col_count] for tap_col in range(3)]
            window = jnp.concatenate(pieces, axis=-1).reshape(row_count * col_count, -1)
            turned = jnp.transpose(w_section[tap_time, tap_row], (0, 2, 1)).reshape(-1, channels)
            running = running + jnp.dot(window, turned, preferred_element_type=jnp.float32)
    return running.reshape(row_count, col_count, channels)

def silu_slope(preact):
    squash = jax.nn.sigmoid(preact)
    return squash * (1.0 + preact * (1.0 - squash))

def spread_back(act_grad, w_in):
    row_count, col_count, channels = act_grad.shape
    lat_width = w_in.shape[3]
    flat_weight = w_in.reshape(-1, channels)
    tap_terms = lax.dot_general(act_grad.reshape(row_count * col_count, channels), flat_weight, (((1,), (1,)), ((), ())), preferred_element_type=jnp.float32)
    tap_terms = tap_terms.reshape(row_count, col_count, 3, 3, 3, lat_width)
    placed_terms = jnp.zeros((3, row_count + 2, col_count + 2, lat_width), jnp.float32)
    for tap_time in range(3):
        for tap_row in range(3):
            for tap_col in range(3):
                placed_terms = placed_terms.at[tap_time, tap_row:tap_row + row_count, tap_col:tap_col + col_count].add(tap_terms[:, :, tap_time, tap_row, tap_col])
    return placed_terms

def norm_back(mod_grad, normed, inverse, mod_scale):
    scaled = mod_grad * (1.0 + mod_scale)
    first_mean = lax.optimization_barrier(jnp.mean(scaled, axis=-1, keepdims=True))
    second_mean = lax.optimization_barrier(jnp.mean(scaled * normed, axis=-1, keepdims=True))
    return ((scaled - first_mean - normed * second_mean) * inverse).astype(jnp.bfloat16)

def reference(hidden, mod_scale, mod_shift, w_out, w_in, w_section, section_grad):
    normed, inverse, modulated = modulate(hidden, mod_scale, mod_shift)
    model_width = hidden.shape[-1]
    flat_mod = modulated.reshape(-1, model_width)
    latent_tokens = jnp.dot(flat_mod, w_out, preferred_element_type=jnp.float32).astype(jnp.bfloat16)
    latent = to_grid(latent_tokens.reshape(hidden.shape[:3] + (w_out.shape[1],)))
    frame_count, row_count, col_count, lat_width = latent.shape
    latent_pad = jnp.pad(latent, ((2, 0), (1, 1), (1, 1), (0, 0)))
    grad_pad = jnp.pad(section_grad, ((0, 2), (1, 1), (1, 1), (0, 0)))

    def one_frame(frame_index):
        latent_win = lax.dynamic_slice_in_dim(latent_pad, frame_index, 3, 0)
        grad_win = lax.dynamic_slice_in_dim(grad_pad, frame_index, 3, 0)
        preact = input_conv(latent_win, w_in, row_count, col_count)
        back_grad = section_back(grad_win, w_section, row_count, col_count)
        act_grad = (back_grad * silu_slope(preact)).astype(jnp.bfloat16)
        return spread_back(act_grad, w_in)
    shares = lax.map(one_frame, jnp.arange(frame_count, dtype=jnp.int32))
    summed_pad = jnp.zeros((frame_count + 2, row_count + 2, col_count + 2, lat_width), jnp.float32)
    for tap_time in range(3):
        summed_pad = summed_pad.at[tap_time:tap_time + frame_count].add(shares[:, tap_time])
    latent_grad = summed_pad[2:, 1:-1, 1:-1]
    token_grad = to_tokens(latent_grad).astype(jnp.bfloat16)
    flat_grad = token_grad.reshape(-1, token_grad.shape[-1])
    mod_grad = lax.dot_general(flat_grad, w_out, (((1,), (1,)), ((), ())), preferred_element_type=jnp.float32)
    grad_hidden = norm_back(mod_grad.reshape(hidden.shape), normed, inverse, mod_scale)
    weight_grad = lax.dot_general(flat_mod, flat_grad, (((0,), (0,)), ((), ())), preferred_element_type=jnp.float32)
    grad_out_weight = weight_grad / math.sqrt(flat_mod.shape[0])
    return (grad_hidden, grad_out_weight)
```

```python
import math

import jax
import jax.numpy as jnp
from jax import lax
from jax.sharding import PartitionSpec as P

epsilon = 1e-05


def padded(block, sides, width):
    for axis, dim in sides:
        count = lax.axis_size(axis)
        forward = [(i, i + 1) for i in range(count - 1)]
        backward = [(target, source) for source, target in forward]
        low = lax.ppermute(
            lax.slice_in_dim(block, block.shape[dim] - width, None, axis=dim), axis, forward
        )
        high = lax.ppermute(lax.slice_in_dim(block, 0, width, axis=dim), axis, backward)
        block = jnp.concatenate([low, block, high], axis=dim)
    return block


def modulate(hidden, mod_scale, mod_shift):
    values = hidden.astype(jnp.float32)
    center = jnp.mean(values, axis=-1, keepdims=True)
    spread = jnp.mean((values - center) * (values - center), axis=-1, keepdims=True)
    inverse = lax.rsqrt(spread + epsilon)
    normed = (values - center) * inverse
    modulated = (normed * (1.0 + mod_scale) + mod_shift).astype(jnp.bfloat16)
    return (normed, inverse, modulated)


def to_grid(tokens):
    frame_count, row_count, col_count, token_width = tokens.shape
    lat_width = token_width // 4
    blocks = tokens.reshape(frame_count, row_count, col_count, 2, 2, lat_width)
    blocks = jnp.transpose(blocks, (0, 1, 3, 2, 4, 5))
    return blocks.reshape(frame_count, 2 * row_count, 2 * col_count, lat_width)


def to_tokens(field):
    frame_count, row_count, col_count, lat_width = field.shape
    blocks = field.reshape(frame_count, row_count // 2, 2, col_count // 2, 2, lat_width)
    blocks = jnp.transpose(blocks, (0, 1, 3, 2, 4, 5))
    return blocks.reshape(frame_count, row_count // 2, col_count // 2, 4 * lat_width)


def input_conv(latent_win, w_in, row_count, col_count):
    pieces = []
    for tap_time in range(3):
        for tap_row in range(3):
            for tap_col in range(3):
                pieces.append(
                    latent_win[
                        tap_time, tap_row : tap_row + row_count, tap_col : tap_col + col_count
                    ]
                )
    stacked = jnp.concatenate(pieces, axis=-1)
    flat_weight = w_in.reshape(-1, w_in.shape[-1])
    preact = jnp.dot(
        stacked.reshape(row_count * col_count, -1), flat_weight, preferred_element_type=jnp.float32
    )
    return preact.reshape(row_count, col_count, -1)


def section_back(grad_win, w_section, row_count, col_count):
    channels = w_section.shape[3]
    running = jnp.zeros((row_count * col_count, channels), jnp.float32)
    for tap_time in range(3):
        for tap_row in range(3):
            pieces = [
                grad_win[
                    2 - tap_time,
                    2 - tap_row : 2 - tap_row + row_count,
                    2 - tap_col : 2 - tap_col + col_count,
                ]
                for tap_col in range(3)
            ]
            window = jnp.concatenate(pieces, axis=-1).reshape(row_count * col_count, -1)
            turned = jnp.transpose(w_section[tap_time, tap_row], (0, 2, 1)).reshape(-1, channels)
            running = running + jnp.dot(window, turned, preferred_element_type=jnp.float32)
    return running.reshape(row_count, col_count, channels)


def silu_slope(preact):
    squash = jax.nn.sigmoid(preact)
    return squash * (1.0 + preact * (1.0 - squash))


def spread_back(act_grad, w_in):
    row_count, col_count, channels = act_grad.shape
    lat_width = w_in.shape[3]
    flat_weight = w_in.reshape(-1, channels)
    tap_terms = lax.dot_general(
        act_grad.reshape(row_count * col_count, channels),
        flat_weight,
        (((1,), (1,)), ((), ())),
        preferred_element_type=jnp.float32,
    )
    tap_terms = tap_terms.reshape(row_count, col_count, 3, 3, 3, lat_width)
    placed_terms = jnp.zeros((3, row_count + 2, col_count + 2, lat_width), jnp.float32)
    for tap_time in range(3):
        for tap_row in range(3):
            for tap_col in range(3):
                placed_terms = placed_terms.at[
                    tap_time, tap_row : tap_row + row_count, tap_col : tap_col + col_count
                ].add(tap_terms[:, :, tap_time, tap_row, tap_col])
    return placed_terms


def norm_back(mod_grad, normed, inverse, mod_scale):
    scaled = mod_grad * (1.0 + mod_scale)
    first_mean = jnp.mean(scaled, axis=-1, keepdims=True)
    second_mean = jnp.mean(scaled * normed, axis=-1, keepdims=True)
    return ((scaled - first_mean - normed * second_mean) * inverse).astype(jnp.bfloat16)


def shards(hidden, mod_scale, mod_shift, w_out, w_in, w_section, section_grad):
    normed, inverse, modulated = modulate(hidden, mod_scale, mod_shift)
    frame_count, token_rows, token_cols, model_width = hidden.shape
    token_width = w_out.shape[1]
    lat_width = w_in.shape[3]
    frame_block = section_grad.shape[0]
    row_count = section_grad.shape[1]
    flat_mod = modulated.reshape(-1, model_width)
    latent_tokens = jnp.dot(flat_mod, w_out, preferred_element_type=jnp.float32).astype(
        jnp.bfloat16
    )
    latent_part = to_grid(latent_tokens.reshape(frame_count, token_rows, token_cols, token_width))
    col_count = section_grad.shape[2]
    groups = lax.axis_size("tm")
    latent_pad = jnp.pad(latent_part, ((2, 0), (0, 0), (0, 0), (0, 0)))
    latent_send = jnp.stack(
        [latent_pad[frame_block * j : frame_block * j + frame_block + 2] for j in range(groups)]
    )
    latent_got = lax.all_to_all(latent_send, "tm", 0, 0, tiled=True)
    latent_back = jnp.transpose(latent_got, (1, 2, 0, 3, 4)).reshape(
        frame_block + 2, row_count, col_count, lat_width
    )
    frames_next = lax.ppermute(section_grad[:2], "tm", [(i + 1, i) for i in range(groups - 1)])
    grad_ahead = jnp.concatenate([section_grad, frames_next], axis=0)
    combined = jnp.concatenate([latent_back, grad_ahead], axis=-1)
    rimmed = padded(combined, (("height", 1),), 1)
    widened = jnp.pad(rimmed, ((0, 0), (0, 0), (1, 1), (0, 0)))
    latent_win = widened[..., :lat_width]
    grad_win = widened[..., lat_width:]
    holder = jnp.zeros((frame_block + 2, row_count + 2, col_count, lat_width), jnp.float32)
    for local_frame in range(frame_block):
        preact = input_conv(latent_win[local_frame : local_frame + 3], w_in, row_count, col_count)
        back_grad = section_back(
            grad_win[local_frame : local_frame + 3], w_section, row_count, col_count
        )
        act_grad = (back_grad * silu_slope(preact)).astype(jnp.bfloat16)
        holder = holder.at[local_frame : local_frame + 3].add(
            spread_back(act_grad, w_in)[:, :, 1:-1]
        )
    col_block = col_count // groups
    shares = holder.astype(jnp.bfloat16).reshape(
        frame_block + 2, row_count + 2, groups, col_block, lat_width
    )
    shares = lax.all_to_all(jnp.transpose(shares, (2, 0, 1, 3, 4)), "tm", 0, 0, tiled=True)
    shares = shares.astype(jnp.float32)
    summed = sum(
        jnp.pad(
            shares[j],
            (
                (frame_block * j, frame_count - frame_block * (j + 1)),
                (0, 0),
                (0, 0),
                (0, 0),
            ),
        )
        for j in range(groups)
    )[2:]
    edged = padded(summed.astype(jnp.bfloat16), (("height", 1),), 1).astype(summed.dtype)
    latent_grad = summed[:, 1 : row_count + 1]
    latent_grad = latent_grad.at[:, 0].add(edged[:, 0])
    latent_grad = latent_grad.at[:, row_count - 1].add(edged[:, row_count + 3])
    token_grad = to_tokens(latent_grad).astype(jnp.bfloat16)
    flat_grad = token_grad.reshape(-1, token_width)
    mod_grad = lax.dot_general(
        flat_grad, w_out, (((1,), (1,)), ((), ())), preferred_element_type=jnp.float32
    )
    grad_hidden = norm_back(mod_grad.reshape(hidden.shape), normed, inverse, mod_scale)
    device_count = lax.axis_size("tm") * lax.axis_size("height")
    total_tokens = flat_mod.shape[0] * device_count
    weight_part = lax.dot_general(
        flat_mod, flat_grad, (((0,), (0,)), ((), ())), preferred_element_type=jnp.float32
    )
    pieces = weight_part.astype(jnp.bfloat16).reshape(device_count, -1, 2 * token_width)
    pieces = lax.all_to_all(pieces, ("tm", "height"), 0, 0, tiled=True)
    weight_part = jnp.sum(pieces.astype(jnp.float32), axis=0).reshape(-1, token_width)
    grad_out_weight = weight_part / math.sqrt(total_tokens)
    return (grad_hidden, grad_out_weight)


def solution(mesh):
    placed = (P(None, "height", "tm", None), P(), P(), P(), P(), P(), P("tm", "height", None, None))
    return jax.shard_map(
        shards,
        mesh=mesh,
        in_specs=placed,
        out_specs=(P(None, "height", "tm", None), P(("tm", "height"), None)),
        check_vma=False,
    )
```

```python
import functools
import math

import jax
import jax.numpy as jnp
from jax import lax
from jax.experimental import pallas as pl
from jax.experimental.pallas import tpu as pltpu
from jax.sharding import PartitionSpec as P

epsilon = 1e-05
slots = 16
lanes = 128
f32 = jnp.float32
bf16 = jnp.bfloat16
anywhere = pl.BlockSpec(memory_space=pl.ANY)
whole = pl.BlockSpec(memory_space=pltpu.VMEM)


def params(mib, *semantics):
    return pltpu.CompilerParams(
        vmem_limit_bytes=mib * 2**20, dimension_semantics=semantics or None
    )


def dot(lhs, rhs):
    return jnp.dot(lhs, rhs, preferred_element_type=f32)


def dot_turned(lhs, rhs):
    return lax.dot_general(lhs, rhs, (((1,), (1,)), ((), ())), preferred_element_type=f32)


def cut_kernel(grad, ahead, first, last, corner_first, corner_last, sems):
    rows = grad.shape[1]
    pieces = (
        (grad.at[0:2], ahead),
        (grad.at[:, 0:1], first),
        (grad.at[:, rows - 1 : rows], last),
        (grad.at[0:2, 0:1], corner_first),
        (grad.at[0:2, rows - 1 : rows], corner_last),
    )
    copies = [pltpu.make_async_copy(src, dst, sems.at[n]) for n, (src, dst) in enumerate(pieces)]
    for copy in copies:
        copy.start()
    for copy in copies:
        copy.wait()


def cut_halos(grad):
    frames, rows, cols, channels = grad.shape
    shapes = ((2, rows), (frames, 1), (frames, 1), (2, 1), (2, 1))
    return pl.pallas_call(
        cut_kernel,
        out_shape=[jax.ShapeDtypeStruct(s + (cols, channels), grad.dtype) for s in shapes],
        in_specs=[anywhere],
        out_specs=[anywhere] * 5,
        scratch_shapes=[pltpu.SemaphoreType.DMA((5,))],
        name="cut_halos",
    )(grad)


def normalise(values):
    center = jnp.mean(values, axis=-1, keepdims=True)
    shifted = values - center
    spread = jnp.mean(shifted * shifted, axis=-1, keepdims=True)
    inverse = lax.rsqrt(spread + epsilon)
    return shifted * inverse, inverse


def modulate_kernel(hidden, scale, shift, w_out, modulated, send):
    step = pl.program_id(0)
    frames, token_rows, tokens, width = hidden.shape
    gain = 1.0 + scale[...]
    blank = jnp.zeros((slots - tokens, width), f32)
    for frame in range(frames):
        for row in range(token_rows):
            normed, _ = normalise(hidden[frame, row].astype(f32))
            value = jnp.concatenate([normed * gain + shift[...], blank], axis=0)
            modulated[frame, row] = value.astype(bf16)
    flat = modulated[...].reshape(frames * token_rows * slots, width)
    latent = dot(flat, w_out[...]).astype(bf16)
    latent = latent.reshape(frames, token_rows, slots, latent.shape[-1])
    paired = jnp.concatenate([latent[:, 0], latent[:, 1]], axis=-1)
    for frame in range(frames):
        send[step, frame + 2] = paired[frame]

    @pl.when(step == 0)
    def _():
        send[0, 0:2] = jnp.zeros_like(send[0, 0:2])

    @pl.when(step < pl.num_programs(0) - 1)
    def _():
        for frame in range(1, frames):
            send[step + 1, frame - 1] = paired[frame]


def modulate(hidden, mod_scale, mod_shift, w_out, groups):
    frames, token_rows, tokens, width = hidden.shape
    block = frames // groups
    token_width = w_out.shape[1]
    held = lambda *dims: pl.BlockSpec(dims, lambda g: (0,) * len(dims))
    return pl.pallas_call(
        modulate_kernel,
        grid=(groups,),
        out_shape=[
            jax.ShapeDtypeStruct((frames, token_rows, slots, width), bf16),
            jax.ShapeDtypeStruct((groups, block + 2, slots, 2 * token_width), bf16),
        ],
        in_specs=[
            pl.BlockSpec((block, token_rows, tokens, width), lambda g: (g, 0, 0, 0)),
            held(1, width),
            held(1, width),
            held(width, token_width),
        ],
        out_specs=[
            pl.BlockSpec((block, token_rows, slots, width), lambda g: (g, 0, 0, 0)),
            held(groups, block + 2, slots, 2 * token_width),
        ],
        compiler_params=params(40, "arbitrary"),
        cost_estimate=pl.CostEstimate(
            flops=2 * frames * 2 * slots * width * token_width,
            bytes_accessed=8 * frames * slots * width,
            transcendentals=0,
        ),
        name="modulate",
    )(hidden, mod_scale.reshape(1, -1), mod_shift.reshape(1, -1), w_out)


def column_shifts(value):
    cols, channels = value.shape
    wide = value.astype(f32)
    place = lax.broadcasted_iota(jnp.int32, (cols, channels), 0)
    nxt = jnp.where(place == cols - 1, 0.0, pltpu.roll(wide, cols - 1, 0))
    prv = jnp.where(place == 0, 0.0, pltpu.roll(wide, 1, 0))
    return nxt.astype(bf16), prv.astype(bf16)


def tap_of(step):
    turn = step % 3
    return 2 - step // 3, jnp.where(turn == 0, 1, jnp.where(turn == 1, 0, 2))


taps = [(2 - n // 3, (1, 0, 2)[n % 3]) for n in range(9)]


def weight_matrix(w_section):
    return jnp.concatenate([w_section[0, 0, kx] for kx in range(3)], axis=-1)


def flat(value):
    return value.reshape(-1, value.shape[-1])


def own_kernel(grad, w_section, total, shifts):
    step = pl.program_id(0)
    frames, rows, cols, channels = grad.shape

    @pl.when(step == 0)
    def _():
        for frame in range(frames):
            for row in range(rows):
                shifts[0, frame, row], shifts[1, frame, row] = column_shifts(grad[frame, row])

    for n, (kt, ky) in enumerate(taps):

        @pl.when(step == n)
        def _(n=n, kt=kt, ky=ky):
            lo, hi = max(0, ky - 1), rows + min(0, ky - 1)
            src = slice(2 - kt, frames), slice(lo + 1 - ky, hi + 1 - ky)
            window = jnp.concatenate(
                [flat(shifts[(0,) + src]), flat(grad[src]), flat(shifts[(1,) + src])], axis=-1
            )
            part = dot_turned(window, weight_matrix(w_section))
            for lane in range(channels // lanes):
                value = part[:, lane * lanes : (lane + 1) * lanes]
                value = value.reshape(kt + 1, hi - lo, cols, lanes)
                if n == 0:
                    total[lane] = value
                else:
                    total[lane, 0 : kt + 1, lo:hi] += value


def own_part(grad, w_section):
    frames, rows, cols, channels = grad.shape
    return pl.pallas_call(
        own_kernel,
        grid=(9,),
        out_shape=jax.ShapeDtypeStruct((channels // lanes, frames, rows, cols, lanes), f32),
        in_specs=[
            pl.BlockSpec(grad.shape, lambda n: (0, 0, 0, 0)),
            pl.BlockSpec((1, 1, 3, channels, channels), lambda n: tap_of(n) + (0, 0, 0)),
        ],
        out_specs=pl.BlockSpec(
            (channels // lanes, frames, rows, cols, lanes), lambda n: (0, 0, 0, 0, 0)
        ),
        scratch_shapes=[pltpu.VMEM((2,) + grad.shape, bf16)],
        compiler_params=params(48, "arbitrary"),
        cost_estimate=pl.CostEstimate(
            flops=2 * 15 * grad.size * channels,
            bytes_accessed=2 * w_section.size,
            transcendentals=0,
        ),
        name="own_part",
    )(grad, w_section)


def rest_kernel(
    own,
    grad_ahead,
    above,
    below,
    above_ahead,
    below_ahead,
    w_section,
    latent,
    latent_above,
    latent_below,
    w_in,
    centre_out,
    up_out,
    down_out,
    total,
    far,
    near,
    tokens,
    windows,
    patches,
    spread,
):
    step = pl.program_id(0)
    blocks, frames, rows, cols, _ = own.shape
    groups, depth, _, pair = latent.shape
    width = pair // 2
    block = cols // (2 * groups)
    half = cols // 2

    @pl.when(step == 0)
    def _():
        total[...] = own[...]
        for frame in range(2):
            for row in range(rows + 2):
                if row == 0:
                    value = above_ahead[frame, 0]
                elif row == rows + 1:
                    value = below_ahead[frame, 0]
                else:
                    value = grad_ahead[frame, row - 1]
                far[1, frame, row] = value
                far[0, frame, row], far[2, frame, row] = column_shifts(value)
        for frame in range(frames):
            for side, ref in ((0, above), (1, below)):
                value = ref[frame, 0]
                near[1, side, frame] = value
                near[0, side, frame], near[2, side, frame] = column_shifts(value)

    for n, (kt, ky) in enumerate(taps):
        if (kt, ky) == (2, 1):
            continue

        @pl.when(step == n - 1)
        def _(kt=kt, ky=ky):
            pieces, places = [], []
            if kt < 2:
                src = slice(0, 2 - kt), slice(2 - ky, 2 - ky + rows)
                pieces.append([far[(kx,) + src] for kx in range(3)])
                places.append((slice(kt + 1, frames), slice(0, rows)))
            if ky != 1:
                side = 0 if ky == 2 else 1
                edge = 0 if ky == 2 else rows - 1
                pieces.append([near[kx, side, 2 - kt : frames] for kx in range(3)])
                places.append((slice(0, kt + 1), slice(edge, edge + 1)))
            window = jnp.concatenate(
                [jnp.concatenate([flat(v) for v in piece], axis=-1) for piece in pieces], axis=0
            )
            part = dot_turned(window, weight_matrix(w_section))
            at = 0
            for place in places:
                shape = [cut.stop - cut.start for cut in place] + [cols, lanes]
                count = shape[0] * shape[1] * cols
                for lane in range(blocks):
                    value = part[at : at + count, lane * lanes : (lane + 1) * lanes]
                    total[(lane,) + place] += value.reshape(shape)
                at += count

    @pl.when(step == pl.num_programs(0) - 1)
    def _():
        tokens[...] = jnp.zeros_like(tokens)
        for src in range(groups):
            at = slice(8 + src * block, 8 + (src + 1) * block)
            for frame in range(depth):
                value = latent[src, frame].astype(f32)[:block]
                tokens[frame, 1, at] = value[:, :width]
                tokens[frame, 2, at] = value[:, width:]
                tokens[frame, 0, at] = latent_above[src, frame].astype(f32)[:block, width:]
                tokens[frame, 3, at] = latent_below[src, frame].astype(f32)[:block, :width]
        for q in range(2):
            left = tokens[:, :, 7 + q : 7 + q + half]
            right = tokens[:, :, 8 + q : 8 + q + half]
            windows[q] = jnp.concatenate([left, right], axis=-1).astype(bf16)
        patches[...] = jnp.zeros_like(patches)
        lat = width // 4
        for p in range(2):
            for q in range(2):
                for kt in range(3):
                    for a in range(2):
                        for b in range(2):
                            for pp in range(2):
                                for qq in range(2):
                                    ky, kx = p - 1 + 2 * a + pp, q - 1 + 2 * b + qq
                                    if not (0 <= ky < 3 and 0 <= kx < 3):
                                        continue
                                    at = (kt * 2 + a) * pair + b * width + (2 * pp + qq) * lat
                                    patches[2 * p + q, at : at + lat] = w_in[kt, ky, kx]
        spread[...] = jnp.zeros_like(spread)
        for p in range(2):
            for q in range(2):
                window = jnp.concatenate(
                    [
                        flat(windows[q, kt : kt + frames, p + a : p + a + rows // 2])
                        for kt in range(3)
                        for a in range(2)
                    ],
                    axis=-1,
                )
                weight = patches[2 * p + q]
                pre = dot(window, weight)
                back = jnp.concatenate(
                    [
                        jnp.concatenate(
                            [
                                total[lane, frame, 2 * row + p, pl.ds(q, half, stride=2), :]
                                for lane in range(blocks)
                            ],
                            axis=-1,
                        )
                        for frame in range(frames)
                        for row in range(rows // 2)
                    ],
                    axis=0,
                )
                gate = jax.nn.sigmoid(pre)
                act_grad = (back * (gate * (1.0 + pre * (1.0 - gate)))).astype(bf16)
                terms = dot_turned(act_grad, weight)
                for kt in range(3):
                    for a in range(2):
                        at = (kt * 2 + a) * pair
                        spread[kt : kt + frames, p + a : p + a + rows // 2, q : q + half] += terms[
                            :, at : at + pair
                        ].reshape(frames, rows // 2, half, pair)
        centre_out[...] = jnp.zeros_like(centre_out)
        up_out[...] = jnp.zeros_like(up_out)
        down_out[...] = jnp.zeros_like(down_out)
        grid = spread[:, :, 1 : half + 1, :width] + spread[:, :, 0:half, width:]
        tokens[:, :, 0:half] = grid
        for dst in range(groups):
            for frame in range(depth):
                value = [
                    tokens[frame, row, dst * block : (dst + 1) * block] for row in range(4)
                ]
                none = jnp.zeros_like(value[0])
                centre_out[dst, frame, 0:block] = jnp.concatenate([value[1], value[2]], axis=-1)
                up_out[dst, frame, 0:block] = jnp.concatenate([none, value[0]], axis=-1)
                down_out[dst, frame, 0:block] = jnp.concatenate([value[3], none], axis=-1)


def rest_part(own, halos, w_section, latents, w_in):
    blocks, frames, rows, cols, _ = own.shape
    channels = blocks * lanes
    groups, depth, _, pair = latents[0].shape
    held = lambda value: pl.BlockSpec(value.shape, lambda n: (0,) * value.ndim)
    out = jax.ShapeDtypeStruct(latents[0].shape, f32)
    return pl.pallas_call(
        rest_kernel,
        grid=(8,),
        out_shape=[out] * 3,
        in_specs=[held(own)]
        + [held(value) for value in halos]
        + [pl.BlockSpec((1, 1, 3, channels, channels), lambda n: tap_of(n + 1) + (0, 0, 0))]
        + [held(value) for value in latents]
        + [held(w_in)],
        out_specs=[held(out)] * 3,
        scratch_shapes=[
            pltpu.VMEM(own.shape, f32),
            pltpu.VMEM((3, 2, rows + 2, cols, channels), bf16),
            pltpu.VMEM((3, 2, frames, cols, channels), bf16),
            pltpu.VMEM((depth, rows // 2 + 2, 72, pair // 2), f32),
            pltpu.VMEM((2, depth, rows // 2 + 2, cols // 2, pair), bf16),
            pltpu.VMEM((4, 6 * pair, channels), bf16),
            pltpu.VMEM((depth, rows // 2 + 2, cols // 2 + 8, pair), f32),
        ],
        compiler_params=params(56, "arbitrary"),
        cost_estimate=pl.CostEstimate(
            flops=2 * 16 * own.size * channels,
            bytes_accessed=2 * w_section.size,
            transcendentals=2 * own.size,
        ),
        name="rest_part",
    )(own, *halos, w_section, *latents, w_in)


def weight_kernel(shares, modulated, token_grad, send, field):
    groups, depth, _, pair = shares.shape
    width = pair // 2
    frames, token_rows = modulated.shape[:2]
    model = modulated.shape[-1]
    field[...] = jnp.zeros_like(field)
    for src in range(groups):
        at = src * (frames // groups)
        field[at : at + depth] += shares[src].astype(f32)
    values = field[2 : 2 + frames]
    token_grad[:, 0] = values[:, :, :width].astype(bf16)
    token_grad[:, 1] = values[:, :, width:].astype(bf16)
    turned = jnp.transpose(token_grad[...].reshape(-1, width).astype(f32)).astype(bf16)
    weight = dot(turned, modulated[...].reshape(-1, model))
    half = model // (2 * groups)
    for dst in range(groups):
        at = 2 * half * dst
        stacked = jnp.concatenate(
            [weight[:, at : at + half], weight[:, at + half : at + 2 * half]], axis=0
        )
        send[dst] = jnp.transpose(stacked).astype(bf16)


def weight_terms(shares, modulated):
    groups, depth, _, pair = shares.shape
    frames, token_rows, _, model = modulated.shape
    return pl.pallas_call(
        weight_kernel,
        out_shape=[
            jax.ShapeDtypeStruct((frames, token_rows, slots, pair // 2), bf16),
            jax.ShapeDtypeStruct((groups, model // (2 * groups), pair), bf16),
        ],
        in_specs=[whole] * 2,
        out_specs=[whole] * 2,
        scratch_shapes=[pltpu.VMEM((frames + 2, slots, pair), f32)],
        compiler_params=params(40),
        name="weight_terms",
    )(shares, modulated)


def middle_kernel(got, send):
    total = jnp.sum(got[...].astype(f32), axis=0)
    count, rows, width = send.shape
    total = total.reshape(count // 2, rows, 2 * width).astype(bf16)
    send[0 : count // 2] = total[:, :, :width]
    send[count // 2 :] = total[:, :, width:]


def middle_sum(got, count):
    groups, depth, pair = got.shape
    return pl.pallas_call(
        middle_kernel,
        out_shape=jax.ShapeDtypeStruct((count, 2 * depth // count, pair // 2), bf16),
        in_specs=[whole],
        out_specs=whole,
        compiler_params=params(24),
        name="middle_sum",
    )(got)


def hidden_kernel(hidden, token_grad, scale, w_out, grad_hidden):
    frames, token_rows, tokens, width = hidden.shape
    gain = 1.0 + scale[...]
    flat_grad = token_grad[...].reshape(-1, token_grad.shape[-1])
    mod_grad = dot_turned(flat_grad, w_out[...])
    for frame in range(frames):
        for row in range(token_rows):
            at = (frame * token_rows + row) * slots
            scaled = mod_grad[at : at + tokens] * gain
            normed, inverse = normalise(hidden[frame, row].astype(f32))
            first = jnp.mean(scaled, axis=-1, keepdims=True)
            second = jnp.mean(scaled * normed, axis=-1, keepdims=True)
            value = (scaled - first - normed * second) * inverse
            grad_hidden[frame, row] = value.astype(bf16)


def hidden_grad(hidden, token_grad, mod_scale, w_out):
    frames, token_rows, tokens, width = hidden.shape
    token_width = w_out.shape[1]
    block = 2
    return pl.pallas_call(
        hidden_kernel,
        grid=(frames // block,),
        out_shape=jax.ShapeDtypeStruct(hidden.shape, bf16),
        in_specs=[
            pl.BlockSpec((block, token_rows, tokens, width), lambda g: (g, 0, 0, 0)),
            pl.BlockSpec((block, token_rows, slots, token_width), lambda g: (g, 0, 0, 0)),
            pl.BlockSpec((1, width), lambda g: (0, 0)),
            pl.BlockSpec((width, token_width), lambda g: (0, 0)),
        ],
        out_specs=pl.BlockSpec((block, token_rows, tokens, width), lambda g: (g, 0, 0, 0)),
        compiler_params=params(40, "arbitrary"),
        cost_estimate=pl.CostEstimate(
            flops=2 * frames * 2 * slots * width * token_width,
            bytes_accessed=8 * frames * slots * width,
            transcendentals=0,
        ),
        name="hidden_grad",
    )(hidden, token_grad, mod_scale.reshape(1, -1), w_out)


def shards(hidden, mod_scale, mod_shift, w_out, w_in, w_section, section_grad):
    groups, strips = lax.axis_size("tm"), lax.axis_size("height")
    up = [(i + 1, i) for i in range(strips - 1)]
    down = [(i, i + 1) for i in range(strips - 1)]

    ahead, first, last, corner_first, corner_last = cut_halos(section_grad)
    earlier = [(g + 1, g) for g in range(groups - 1)]
    cross = lambda steps: [
        (g * strips + a, h * strips + b) for g, h in earlier for a, b in steps
    ]
    grad_ahead = lax.ppermute(ahead, "tm", earlier)
    below = lax.ppermute(first, "height", up)
    above = lax.ppermute(last, "height", down)
    below_ahead = lax.ppermute(corner_first, ("tm", "height"), cross(up))
    above_ahead = lax.ppermute(corner_last, ("tm", "height"), cross(down))

    modulated, latent_send = modulate(hidden, mod_scale, mod_shift, w_out, groups)
    latent = lax.all_to_all(latent_send, "tm", 0, 0, tiled=True)
    latent_below = lax.ppermute(latent, "height", up)
    latent_above = lax.ppermute(latent, "height", down)

    own = own_part(section_grad, w_section)
    centre, to_above, to_below = rest_part(
        own,
        (grad_ahead, above, below, above_ahead, below_ahead),
        w_section,
        (latent, latent_above, latent_below),
        w_in,
    )
    from_below = lax.ppermute(to_above.astype(bf16), "height", up)
    from_above = lax.ppermute(to_below.astype(bf16), "height", down)
    centre = centre + from_below.astype(f32) + from_above.astype(f32)
    shares = lax.all_to_all(centre.astype(bf16), "tm", 0, 0, tiled=True)

    token_grad, send = weight_terms(shares, modulated)
    got = lax.all_to_all(send, "tm", 0, 0, tiled=True)
    grad_hidden = hidden_grad(hidden, token_grad, mod_scale, w_out)
    pieces = lax.all_to_all(middle_sum(got, strips), "height", 0, 0, tiled=True)
    total_tokens = math.prod(hidden.shape[:3]) * groups * strips
    grad_out_weight = jnp.sum(pieces.astype(f32), axis=0) / math.sqrt(total_tokens)
    return (grad_hidden, grad_out_weight)


def solution(mesh):
    placed = (P(None, "height", "tm", None), P(), P(), P(), P(), P(), P("tm", "height", None, None))
    return jax.shard_map(
        shards,
        mesh=mesh,
        in_specs=placed,
        out_specs=(P(None, "height", "tm", None), P(("tm", "height"), None)),
        check_vma=False,
    )
```

```python
import functools
import math

import jax
import jax.numpy as jnp
from jax import lax
from jax.experimental import pallas as pl
from jax.experimental.pallas import tpu as pltpu
from jax.sharding import PartitionSpec as P

epsilon = 1e-05
slots = 16
lanes = 128
f32 = jnp.float32
bf16 = jnp.bfloat16
whole = pl.BlockSpec(memory_space=pltpu.VMEM)


def params(mib, *semantics):
    return pltpu.CompilerParams(
        vmem_limit_bytes=mib * 2**20, dimension_semantics=semantics or None
    )


def dot(lhs, rhs):
    return jnp.dot(lhs, rhs, preferred_element_type=f32)


def dot_turned(lhs, rhs):
    return lax.dot_general(lhs, rhs, (((1,), (1,)), ((), ())), preferred_element_type=f32)


def normalise(values):
    center = jnp.mean(values, axis=-1, keepdims=True)
    shifted = values - center
    spread = jnp.mean(shifted * shifted, axis=-1, keepdims=True)
    inverse = lax.rsqrt(spread + epsilon)
    return shifted * inverse, inverse


def modulate_kernel(hidden, scale, shift, w_out, modulated, send):
    step = pl.program_id(0)
    frames, token_rows, tokens, width = hidden.shape
    gain = 1.0 + scale[...]
    blank = jnp.zeros((slots - tokens, width), f32)
    for frame in range(frames):
        for row in range(token_rows):
            normed, _ = normalise(hidden[frame, row].astype(f32))
            value = jnp.concatenate([normed * gain + shift[...], blank], axis=0)
            modulated[frame, row] = value.astype(bf16)
    flat = modulated[...].reshape(frames * token_rows * slots, width)
    latent = dot_turned(flat, w_out[...]).astype(bf16)
    latent = latent.reshape(frames, token_rows, slots, latent.shape[-1])
    paired = jnp.concatenate([latent[:, 0], latent[:, 1]], axis=-1)
    for frame in range(frames):
        send[step, frame + 2] = paired[frame]

    @pl.when(step == 0)
    def _():
        send[0, 0:2] = jnp.zeros_like(send[0, 0:2])

    @pl.when(step < pl.num_programs(0) - 1)
    def _():
        for frame in range(1, frames):
            send[step + 1, frame - 1] = paired[frame]


def modulate(hidden, mod_scale, mod_shift, w_out, groups):
    frames, token_rows, tokens, width = hidden.shape
    block = frames // groups
    token_width = w_out.shape[0]
    held = lambda *dims: pl.BlockSpec(dims, lambda g: (0,) * len(dims))
    return pl.pallas_call(
        modulate_kernel,
        grid=(groups,),
        out_shape=[
            jax.ShapeDtypeStruct((frames, token_rows, slots, width), bf16),
            jax.ShapeDtypeStruct((groups, block + 2, slots, 2 * token_width), bf16),
        ],
        in_specs=[
            pl.BlockSpec((block, token_rows, tokens, width), lambda g: (g, 0, 0, 0)),
            held(1, width),
            held(1, width),
            held(token_width, width),
        ],
        out_specs=[
            pl.BlockSpec((block, token_rows, slots, width), lambda g: (g, 0, 0, 0)),
            held(groups, block + 2, slots, 2 * token_width),
        ],
        compiler_params=params(20, "arbitrary"),
        cost_estimate=pl.CostEstimate(
            flops=2 * frames * 2 * slots * width * token_width,
            bytes_accessed=8 * frames * slots * width,
            transcendentals=0,
        ),
        name="modulate",
    )(hidden, mod_scale.reshape(1, -1), mod_shift.reshape(1, -1), w_out)


def column_shifts(value):
    cols, channels = value.shape
    wide = value.astype(f32)
    place = lax.broadcasted_iota(jnp.int32, (cols, channels), 0)
    nxt = jnp.where(place == cols - 1, 0.0, pltpu.roll(wide, cols - 1, 0))
    prv = jnp.where(place == 0, 0.0, pltpu.roll(wide, 1, 0))
    return nxt.astype(bf16), prv.astype(bf16)


def tap_of(step):
    turn = step % 3
    return 2 - step // 3, jnp.where(turn == 0, 1, jnp.where(turn == 1, 0, 2))


taps = [(2 - n // 3, (1, 0, 2)[n % 3]) for n in range(9)]


def flat(value):
    return value.reshape(-1, value.shape[-1])


def pack_kernel(places, own_near, own_far, ahead_near, ahead_far, latent, near, far):
    channels = own_near.shape[-1]
    for own, ahead, out in ((own_near, ahead_near, near), (own_far, ahead_far, far)):
        front = flat(own[...])
        back = flat(ahead[...])
        out[0 : front.shape[0]] = front
        out[front.shape[0] : front.shape[0] + back.shape[0]] = back
        at = front.shape[0] + back.shape[0]
        tail = flat(latent[...])
        count = tail.shape[0] * lanes // channels
        for lane in range(channels // lanes):
            out[at : at + count, lane * lanes : (lane + 1) * lanes] = tail[
                lane * count : (lane + 1) * count
            ]


def pack_rows(places, grad, grad_ahead, latent):
    frames, rows, cols, channels = grad.shape
    total = (frames + 2) * cols + latent.size // channels
    out = jax.ShapeDtypeStruct((total, channels), bf16)
    near = lambda n, at: (0, at[0], 0, 0)
    far = lambda n, at: (0, at[1], 0, 0)
    return pl.pallas_call(
        pack_kernel,
        grid_spec=pltpu.PrefetchScalarGridSpec(
            num_scalar_prefetch=1,
            grid=(1,),
            in_specs=[
                pl.BlockSpec((frames, 1, cols, channels), near),
                pl.BlockSpec((frames, 1, cols, channels), far),
                pl.BlockSpec((2, 1, cols, channels), near),
                pl.BlockSpec((2, 1, cols, channels), far),
                pl.BlockSpec(latent.shape, lambda n, at: (0, 0, 0, 0)),
            ],
            out_specs=[pl.BlockSpec(out.shape, lambda n, at: (0, 0))] * 2,
        ),
        out_shape=[out] * 2,
        compiler_params=params(16, "arbitrary"),
        name="pack_rows",
    )(places, grad, grad, grad_ahead, grad_ahead, latent)


def own_kernel(grad, w_section, total, turned, shifts):
    step = pl.program_id(0)
    frames, rows, cols, channels = grad.shape
    for kx in range(3):
        turned[0, 0, kx] = jnp.transpose(w_section[0, 0, kx])

    @pl.when(step == 0)
    def _():
        for frame in range(frames):
            for row in range(rows):
                shifts[0, frame, row], shifts[1, frame, row] = column_shifts(grad[frame, row])

    for n, (kt, ky) in enumerate(taps):

        @pl.when(step == n)
        def _(n=n, kt=kt, ky=ky):
            lo, hi = max(0, ky - 1), rows + min(0, ky - 1)
            src = slice(2 - kt, frames), slice(lo + 1 - ky, hi + 1 - ky)
            window = jnp.concatenate(
                [flat(shifts[(0,) + src]), flat(grad[src]), flat(shifts[(1,) + src])], axis=-1
            )
            part = dot(window, flat(turned[0, 0]))
            for lane in range(channels // lanes):
                value = part[:, lane * lanes : (lane + 1) * lanes]
                value = value.reshape(kt + 1, hi - lo, cols, lanes)
                if n == 0:
                    total[lane] = value
                else:
                    total[lane, 0 : kt + 1, lo:hi] += value


def own_part(grad, w_section):
    frames, rows, cols, channels = grad.shape
    return pl.pallas_call(
        own_kernel,
        grid=(9,),
        out_shape=[
            jax.ShapeDtypeStruct((channels // lanes, frames, rows, cols, lanes), f32),
            jax.ShapeDtypeStruct(w_section.shape, bf16),
        ],
        in_specs=[
            pl.BlockSpec(grad.shape, lambda n: (0, 0, 0, 0)),
            pl.BlockSpec((1, 1, 3, channels, channels), lambda n: tap_of(n) + (0, 0, 0)),
        ],
        out_specs=[
            pl.BlockSpec((channels // lanes, frames, rows, cols, lanes), lambda n: (0,) * 5),
            pl.BlockSpec((1, 1, 3, channels, channels), lambda n: tap_of(n) + (0, 0, 0)),
        ],
        scratch_shapes=[pltpu.VMEM((2,) + grad.shape, bf16)],
        compiler_params=params(52, "arbitrary"),
        cost_estimate=pl.CostEstimate(
            flops=2 * 15 * grad.size * channels,
            bytes_accessed=2 * w_section.size,
            transcendentals=0,
        ),
        name="own_part",
    )(grad, w_section)


def rest_kernel(
    places,
    own,
    grad_ahead,
    near_rows,
    far_rows,
    turned,
    latent,
    w_in,
    centre_out,
    near_out,
    far_out,
    total,
    far,
    near,
    tokens,
    windows,
    patches,
    spread,
):
    even = places[0] != 0
    step = pl.program_id(0)
    blocks, frames, rows, cols, _ = own.shape
    channels = blocks * lanes
    groups, depth, _, pair = latent.shape
    width = pair // 2
    block = cols // (2 * groups)
    half = cols // 2

    @pl.when(step == 0)
    def _():
        total[...] = own[...]
        for frame in range(frames + 2):
            at = slice(frame * cols, (frame + 1) * cols)
            ends = near_rows[at], far_rows[at]
            for side in range(2):
                value = jnp.where(even == (side == 1), ends[0], ends[1])
                shifted = column_shifts(value)
                if frame < frames:
                    near[1, side, frame] = value
                    near[0, side, frame], near[2, side, frame] = shifted
                else:
                    row = side * (rows + 1)
                    far[1, frame - frames, row] = value
                    far[0, frame - frames, row], far[2, frame - frames, row] = shifted
        for frame in range(2):
            for row in range(rows):
                value = grad_ahead[frame, row]
                far[1, frame, row + 1] = value
                far[0, frame, row + 1], far[2, frame, row + 1] = column_shifts(value)

    for n, (kt, ky) in enumerate(taps):
        if (kt, ky) == (2, 1):
            continue

        @pl.when(step == n - 1)
        def _(kt=kt, ky=ky):
            pieces, places = [], []
            if kt < 2:
                src = slice(0, 2 - kt), slice(2 - ky, 2 - ky + rows)
                pieces.append([far[(kx,) + src] for kx in range(3)])
                places.append((slice(kt + 1, frames), slice(0, rows)))
            if ky != 1:
                side = 0 if ky == 2 else 1
                edge = 0 if ky == 2 else rows - 1
                pieces.append([near[kx, side, 2 - kt : frames] for kx in range(3)])
                places.append((slice(0, kt + 1), slice(edge, edge + 1)))
            window = jnp.concatenate(
                [jnp.concatenate([flat(v) for v in piece], axis=-1) for piece in pieces], axis=0
            )
            part = dot(window, flat(turned[0, 0]))
            at = 0
            for place in places:
                shape = [cut.stop - cut.start for cut in place] + [cols, lanes]
                count = shape[0] * shape[1] * cols
                for lane in range(blocks):
                    value = part[at : at + count, lane * lanes : (lane + 1) * lanes]
                    total[(lane,) + place] += value.reshape(shape)
                at += count

    @pl.when(step == pl.num_programs(0) - 1)
    def _():
        tokens[...] = jnp.zeros_like(tokens)
        for src in range(groups):
            at = slice(8 + src * block, 8 + (src + 1) * block)
            for frame in range(depth):
                value = latent[src, frame].astype(f32)[:block]
                tokens[frame, 1, at] = value[:, :width]
                tokens[frame, 2, at] = value[:, width:]
                row = (src * depth + frame) * slots
                count = groups * depth * slots * lanes // channels
                lane = row // count * lanes
                row = (frames + 2) * cols + row % count
                ends = [
                    rows_of[row : row + slots, lane : lane + lanes].astype(f32)[:block]
                    for rows_of in (near_rows, far_rows)
                ]
                tokens[frame, 0, at] = jnp.where(even, ends[1], ends[0])[:, width:]
                tokens[frame, 3, at] = jnp.where(even, ends[0], ends[1])[:, :width]
        for q in range(2):
            left = tokens[:, :, 7 + q : 7 + q + half]
            right = tokens[:, :, 8 + q : 8 + q + half]
            windows[q] = jnp.concatenate([left, right], axis=-1).astype(bf16)
        patches[...] = jnp.zeros_like(patches)
        lat = width // 4
        for p in range(2):
            for q in range(2):
                for kt in range(3):
                    for a in range(2):
                        for b in range(2):
                            for pp in range(2):
                                for qq in range(2):
                                    ky, kx = p - 1 + 2 * a + pp, q - 1 + 2 * b + qq
                                    if not (0 <= ky < 3 and 0 <= kx < 3):
                                        continue
                                    at = (kt * 2 + a) * pair + b * width + (2 * pp + qq) * lat
                                    patches[2 * p + q, at : at + lat] = w_in[kt, ky, kx]
        spread[...] = jnp.zeros_like(spread)
        for p in range(2):
            for q in range(2):
                window = jnp.concatenate(
                    [
                        flat(windows[q, kt : kt + frames, p + a : p + a + rows // 2])
                        for kt in range(3)
                        for a in range(2)
                    ],
                    axis=-1,
                )
                weight = patches[2 * p + q]
                pre = dot(window, weight)
                back = jnp.concatenate(
                    [
                        jnp.concatenate(
                            [
                                total[lane, frame, 2 * row + p, pl.ds(q, half, stride=2), :]
                                for lane in range(blocks)
                            ],
                            axis=-1,
                        )
                        for frame in range(frames)
                        for row in range(rows // 2)
                    ],
                    axis=0,
                )
                gate = jax.nn.sigmoid(pre)
                act_grad = (back * (gate * (1.0 + pre * (1.0 - gate)))).astype(bf16)
                terms = dot_turned(act_grad, weight)
                for kt in range(3):
                    for a in range(2):
                        at = (kt * 2 + a) * pair
                        spread[kt : kt + frames, p + a : p + a + rows // 2, q : q + half] += terms[
                            :, at : at + pair
                        ].reshape(frames, rows // 2, half, pair)
        centre_out[...] = jnp.zeros_like(centre_out)
        near_out[...] = jnp.zeros_like(near_out)
        far_out[...] = jnp.zeros_like(far_out)
        grid = spread[:, :, 1 : half + 1, :width] + spread[:, :, 0:half, width:]
        tokens[:, :, 0:half] = grid
        for dst in range(groups):
            for frame in range(depth):
                value = [
                    tokens[frame, row, dst * block : (dst + 1) * block] for row in range(4)
                ]
                none = jnp.zeros_like(value[0])
                centre = jnp.concatenate([value[1], value[2]], axis=-1)
                up = jnp.concatenate([none, value[0]], axis=-1)
                down = jnp.concatenate([value[3], none], axis=-1)
                fill = jnp.zeros((slots - block, 2 * width), f32)
                padded = lambda v: jnp.concatenate([v, fill], axis=0).astype(bf16)
                centre_out[dst, frame] = padded(centre)
                near_out[dst, frame] = padded(jnp.where(even, down, up))
                far_out[dst, frame] = padded(jnp.where(even, up, down))


def rest_part(places, own, grad_ahead, near_rows, far_rows, turned, latent, w_in):
    blocks, frames, rows, cols, _ = own.shape
    channels = blocks * lanes
    groups, depth, _, pair = latent.shape
    held = lambda value: pl.BlockSpec(
        value.shape, lambda n, at: (0,) * len(value.shape), pipeline_mode=pl.Buffered(1)
    )
    out = jax.ShapeDtypeStruct(latent.shape, bf16)
    return pl.pallas_call(
        rest_kernel,
        out_shape=[out] * 3,
        grid_spec=pltpu.PrefetchScalarGridSpec(
            num_scalar_prefetch=1,
            grid=(8,),
            in_specs=[
                held(own),
                pl.BlockSpec((2, rows, cols, channels), lambda n, at: (0, 0, 0, 0)),
                held(near_rows),
                held(far_rows),
                pl.BlockSpec(
                    (1, 1, 3, channels, channels), lambda n, at: tap_of(n + 1) + (0, 0, 0)
                ),
                held(latent),
                held(w_in),
            ],
            out_specs=[held(out)] * 3,
            scratch_shapes=[
                pltpu.VMEM(own.shape, f32),
                pltpu.VMEM((3, 2, rows + 2, cols, channels), bf16),
                pltpu.VMEM((3, 2, frames, cols, channels), bf16),
                pltpu.VMEM((depth, rows // 2 + 2, 72, pair // 2), f32),
                pltpu.VMEM((2, depth, rows // 2 + 2, cols // 2, pair), bf16),
                pltpu.VMEM((4, 6 * pair, channels), bf16),
                pltpu.VMEM((depth, rows // 2 + 2, cols // 2 + 8, pair), f32),
            ],
        ),
        compiler_params=params(52, "arbitrary"),
        cost_estimate=pl.CostEstimate(
            flops=2 * 16 * own.size * channels,
            bytes_accessed=2 * turned.size,
            transcendentals=2 * own.size,
        ),
        name="rest_part",
    )(places, own, grad_ahead, near_rows, far_rows, turned, latent, w_in)


def weight_kernel(shares, modulated, token_grad, send, field):
    groups, depth, _, pair = shares.shape
    width = pair // 2
    frames, token_rows = modulated.shape[:2]
    model = modulated.shape[-1]
    field[...] = jnp.zeros_like(field)
    for src in range(groups):
        at = src * (frames // groups)
        field[at : at + depth] += shares[src].astype(f32)
    values = field[2 : 2 + frames]
    token_grad[:, 0] = values[:, :, :width].astype(bf16)
    token_grad[:, 1] = values[:, :, width:].astype(bf16)
    turned = jnp.transpose(token_grad[...].reshape(-1, width).astype(f32)).astype(bf16)
    weight = dot(turned, modulated[...].reshape(-1, model))
    half = model // (2 * groups)
    for dst in range(groups):
        at = 2 * half * dst
        stacked = jnp.concatenate(
            [weight[:, at : at + half], weight[:, at + half : at + 2 * half]], axis=0
        )
        send[dst] = jnp.transpose(stacked).astype(bf16)


def weight_terms(shares, modulated):
    groups, depth, _, pair = shares.shape
    frames, token_rows, _, model = modulated.shape
    return pl.pallas_call(
        weight_kernel,
        out_shape=[
            jax.ShapeDtypeStruct((frames, token_rows, slots, pair // 2), bf16),
            jax.ShapeDtypeStruct((groups, model // (2 * groups), pair), bf16),
        ],
        in_specs=[whole] * 2,
        out_specs=[whole] * 2,
        scratch_shapes=[pltpu.VMEM((frames + 2, slots, pair), f32)],
        compiler_params=params(24),
        name="weight_terms",
    )(shares, modulated)


def middle_kernel(got, send):
    total = jnp.sum(got[...].astype(f32), axis=0)
    count, rows, width = send.shape
    total = total.reshape(count // 2, rows, 2 * width).astype(bf16)
    send[0 : count // 2] = total[:, :, :width]
    send[count // 2 :] = total[:, :, width:]


def middle_sum(got, count):
    groups, depth, pair = got.shape
    return pl.pallas_call(
        middle_kernel,
        out_shape=jax.ShapeDtypeStruct((count, 2 * depth // count, pair // 2), bf16),
        in_specs=[whole],
        out_specs=whole,
        compiler_params=params(24),
        name="middle_sum",
    )(got)


def hidden_kernel(hidden, token_grad, scale, w_out, grad_hidden):
    frames, token_rows, tokens, width = hidden.shape
    gain = 1.0 + scale[...]
    flat_grad = token_grad[...].reshape(-1, token_grad.shape[-1])
    mod_grad = dot(flat_grad, w_out[...])
    for frame in range(frames):
        for row in range(token_rows):
            at = (frame * token_rows + row) * slots
            scaled = mod_grad[at : at + tokens] * gain
            normed, inverse = normalise(hidden[frame, row].astype(f32))
            first = jnp.mean(scaled, axis=-1, keepdims=True)
            second = jnp.mean(scaled * normed, axis=-1, keepdims=True)
            value = (scaled - first - normed * second) * inverse
            grad_hidden[frame, row] = value.astype(bf16)


def hidden_grad(hidden, token_grad, mod_scale, w_out):
    frames, token_rows, tokens, width = hidden.shape
    token_width = w_out.shape[0]
    block = 2
    return pl.pallas_call(
        hidden_kernel,
        grid=(frames // block,),
        out_shape=jax.ShapeDtypeStruct(hidden.shape, bf16),
        in_specs=[
            pl.BlockSpec((block, token_rows, tokens, width), lambda g: (g, 0, 0, 0)),
            pl.BlockSpec((block, token_rows, slots, token_width), lambda g: (g, 0, 0, 0)),
            pl.BlockSpec((1, width), lambda g: (0, 0)),
            pl.BlockSpec((token_width, width), lambda g: (0, 0)),
        ],
        out_specs=pl.BlockSpec((block, token_rows, tokens, width), lambda g: (g, 0, 0, 0)),
        compiler_params=params(20, "arbitrary"),
        cost_estimate=pl.CostEstimate(
            flops=2 * frames * 2 * slots * width * token_width,
            bytes_accessed=8 * frames * slots * width,
            transcendentals=0,
        ),
        name="hidden_grad",
    )(hidden, token_grad, mod_scale.reshape(1, -1), w_out)


def shards(hidden, mod_scale, mod_shift, w_out, w_in, w_section, section_grad):
    groups, strips = lax.axis_size("tm"), lax.axis_size("height")
    rows = section_grad.shape[1]
    swap = lambda a, b: [(a, b), (b, a)]
    near = sum([swap(i, i + 1) for i in range(0, strips - 1, 2)], [])
    far = sum([swap(i, i + 1) for i in range(1, strips - 1, 2)], [])
    odd = lax.rem(lax.axis_index("height"), 2)
    places = jnp.stack([(1 - odd) * (rows - 1), odd * (rows - 1)]).astype(jnp.int32)
    w_out = jnp.transpose(w_out)

    grad_ahead = lax.ppermute(section_grad, "tm", [(g + 1, g) for g in range(groups - 1)])
    modulated, latent_send = modulate(hidden, mod_scale, mod_shift, w_out, groups)
    latent = lax.all_to_all(latent_send, "tm", 0, 0, tiled=True)
    near_send, far_send = pack_rows(places, section_grad, grad_ahead, latent)
    far_rows = lax.ppermute(far_send, "height", far)
    near_rows = lax.ppermute(near_send, "height", near)

    own, turned = own_part(section_grad, w_section)
    centre, near_share, far_share = rest_part(
        places, own, grad_ahead, near_rows, far_rows, turned, latent, w_in
    )
    far_share = lax.ppermute(far_share, "height", far)
    near_share = lax.ppermute(near_share, "height", near)
    centre = centre.astype(f32) + near_share.astype(f32) + far_share.astype(f32)
    shares = lax.all_to_all(centre.astype(bf16), "tm", 0, 0, tiled=True)

    token_grad, send = weight_terms(shares, modulated)
    got = lax.all_to_all(send, "tm", 0, 0, tiled=True)
    grad_hidden = hidden_grad(hidden, token_grad, mod_scale, w_out)
    pieces = lax.all_to_all(middle_sum(got, strips), "height", 0, 0, tiled=True)
    total_tokens = math.prod(hidden.shape[:3]) * groups * strips
    grad_out_weight = jnp.sum(pieces.astype(f32), axis=0) / math.sqrt(total_tokens)
    return (grad_hidden, grad_out_weight)


def solution(mesh):
    placed = (P(None, "height", "tm", None), P(), P(), P(), P(), P(), P("tm", "height", None, None))
    return jax.shard_map(
        shards,
        mesh=mesh,
        in_specs=placed,
        out_specs=(P(None, "height", "tm", None), P(("tm", "height"), None)),
        check_vma=False,
    )
```

```python
import functools
import math

import jax
import jax.numpy as jnp
from jax import lax
from jax.experimental import pallas as pl
from jax.experimental.pallas import tpu as pltpu
from jax.sharding import PartitionSpec as P

epsilon = 1e-05
slots = 16
lanes = 128
f32 = jnp.float32
bf16 = jnp.bfloat16
whole = pl.BlockSpec(memory_space=pltpu.VMEM)


def params(mib):
    return pltpu.CompilerParams(vmem_limit_bytes=mib * 2**20)


def dot(lhs, rhs):
    return jnp.dot(lhs, rhs, preferred_element_type=f32)


def dot_turned(lhs, rhs):
    return lax.dot_general(lhs, rhs, (((1,), (1,)), ((), ())), preferred_element_type=f32)


def normalise(values):
    center = jnp.mean(values, axis=-1, keepdims=True)
    shifted = values - center
    spread = jnp.mean(shifted * shifted, axis=-1, keepdims=True)
    inverse = lax.rsqrt(spread + epsilon)
    return shifted * inverse, inverse


def modulate_kernel(hidden, scale, shift, w_out, modulated, send):
    groups, depth = send.shape[:2]
    block = depth - 2
    _, token_rows, tokens, width = hidden.shape
    gain = 1.0 + scale[...]
    blank = jnp.zeros((slots - tokens, width), f32)
    send[0, 0:2] = jnp.zeros_like(send[0, 0:2])

    def share(step, carry):
        for frame in range(block):
            for row in range(token_rows):
                normed, _ = normalise(hidden[step * block + frame, row].astype(f32))
                value = jnp.concatenate([normed * gain + shift[...], blank], axis=0)
                modulated[step * block + frame, row] = value.astype(bf16)
        rows = modulated[pl.ds(step * block, block)].reshape(-1, width)
        latent = dot_turned(rows, w_out[...]).astype(bf16)
        latent = latent.reshape(block, token_rows, slots, latent.shape[-1])
        paired = jnp.concatenate([latent[:, 0], latent[:, 1]], axis=-1)
        for frame in range(block):
            send[step, frame + 2] = paired[frame]

        @pl.when(step < groups - 1)
        def _():
            for frame in range(1, block):
                send[step + 1, frame - 1] = paired[frame]

        return carry

    lax.fori_loop(0, groups, share, 0)


def modulate(hidden, mod_scale, mod_shift, w_out, groups):
    frames, token_rows, tokens, width = hidden.shape
    token_width = w_out.shape[0]
    return pl.pallas_call(
        modulate_kernel,
        out_shape=[
            jax.ShapeDtypeStruct((frames, token_rows, slots, width), bf16),
            jax.ShapeDtypeStruct((groups, frames // groups + 2, slots, 2 * token_width), bf16),
        ],
        in_specs=[whole] * 4,
        out_specs=[whole] * 2,
        compiler_params=params(8),
        cost_estimate=pl.CostEstimate(
            flops=2 * frames * 2 * slots * width * token_width,
            bytes_accessed=8 * frames * slots * width,
            transcendentals=0,
        ),
        name="modulate",
    )(hidden, mod_scale.reshape(1, -1), mod_shift.reshape(1, -1), w_out)


def column_shifts(value):
    cols, channels = value.shape
    wide = value.astype(f32)
    place = lax.broadcasted_iota(jnp.int32, (cols, channels), 0)
    nxt = jnp.where(place == cols - 1, 0.0, pltpu.roll(wide, cols - 1, 0))
    prv = jnp.where(place == 0, 0.0, pltpu.roll(wide, 1, 0))
    return nxt.astype(bf16), prv.astype(bf16)


taps = [(2 - n // 3, (1, 0, 2)[n % 3]) for n in range(9)]


def flat(value):
    return value.reshape(-1, value.shape[-1])


def weight_matrix(w_section, kt, ky):
    return jnp.concatenate([w_section[kt, ky, kx] for kx in range(3)], axis=-1)


def pack_kernel(places, grad, grad_ahead, latent, near, far):
    frames, _, cols, channels = grad.shape
    for side, out in ((0, near), (1, far)):
        row = places[side]
        for frame in range(frames):
            out[frame * cols : (frame + 1) * cols] = grad[frame, row]
        for frame in range(2):
            at = (frames + frame) * cols
            out[at : at + cols] = grad_ahead[frame, row]
        at = (frames + 2) * cols
        tail = flat(latent[...])
        count = tail.shape[0] * lanes // channels
        for lane in range(channels // lanes):
            out[at : at + count, lane * lanes : (lane + 1) * lanes] = tail[
                lane * count : (lane + 1) * count
            ]


def pack_rows(places, grad, grad_ahead, latent):
    frames, rows, cols, channels = grad.shape
    total = (frames + 2) * cols + latent.size // channels
    return pl.pallas_call(
        pack_kernel,
        in_specs=[pl.BlockSpec(memory_space=pltpu.SMEM)] + [whole] * 3,
        out_specs=[whole] * 2,
        out_shape=[jax.ShapeDtypeStruct((total, channels), bf16)] * 2,
        compiler_params=params(4),
        name="pack_rows",
    )(places, grad, grad_ahead, latent)


def own_kernel(grad, w_section, total, held, shifts, sems):
    frames, rows, cols, channels = grad.shape
    copies = [
        pltpu.make_async_copy(w_section.at[kt, ky], held.at[kt, ky], sems.at[n])
        for n, (kt, ky) in enumerate(taps)
    ]
    for copy in copies:
        copy.start()
    for frame in range(frames):
        for row in range(rows):
            shifts[0, frame, row], shifts[1, frame, row] = column_shifts(grad[frame, row])
    for n, (kt, ky) in enumerate(taps):
        lo, hi = max(0, ky - 1), rows + min(0, ky - 1)
        src = slice(2 - kt, frames), slice(lo + 1 - ky, hi + 1 - ky)
        window = jnp.concatenate(
            [flat(shifts[(0,) + src]), flat(grad[src]), flat(shifts[(1,) + src])], axis=-1
        )
        copies[n].wait()
        part = dot_turned(window, weight_matrix(held, kt, ky))
        for lane in range(channels // lanes):
            value = part[:, lane * lanes : (lane + 1) * lanes]
            value = value.reshape(kt + 1, hi - lo, cols, lanes)
            if n == 0:
                total[lane] = value
            else:
                total[lane, 0 : kt + 1, lo:hi] += value


def own_part(grad, w_section):
    frames, rows, cols, channels = grad.shape
    return pl.pallas_call(
        own_kernel,
        out_shape=[
            jax.ShapeDtypeStruct((channels // lanes, frames, rows, cols, lanes), f32),
            jax.ShapeDtypeStruct(w_section.shape, bf16),
        ],
        in_specs=[whole, pl.BlockSpec(memory_space=pltpu.HBM)],
        out_specs=[whole] * 2,
        scratch_shapes=[
            pltpu.VMEM((2,) + grad.shape, bf16),
            pltpu.SemaphoreType.DMA((len(taps),)),
        ],
        compiler_params=params(24),
        cost_estimate=pl.CostEstimate(
            flops=2 * 15 * grad.size * channels,
            bytes_accessed=2 * w_section.size,
            transcendentals=0,
        ),
        name="own_part",
    )(grad, w_section)


def rest_kernel(
    places,
    own,
    grad_ahead,
    near_rows,
    far_rows,
    w_section,
    latent,
    w_in,
    centre_out,
    near_out,
    far_out,
    total,
    far,
    near,
    tokens,
    windows,
    patches,
    spread,
):
    even = places[0] != 0
    blocks, frames, rows, cols, _ = own.shape
    channels = blocks * lanes
    groups, depth, _, pair = latent.shape
    width = pair // 2
    block = cols // (2 * groups)
    half = cols // 2
    total[...] = own[...]
    for frame in range(frames + 2):
        at = slice(frame * cols, (frame + 1) * cols)
        ends = near_rows[at], far_rows[at]
        for side in range(2):
            value = jnp.where(even == (side == 1), ends[0], ends[1])
            shifted = column_shifts(value)
            if frame < frames:
                near[1, side, frame] = value
                near[0, side, frame], near[2, side, frame] = shifted
            else:
                row = side * (rows + 1)
                far[1, frame - frames, row] = value
                far[0, frame - frames, row], far[2, frame - frames, row] = shifted
    for frame in range(2):
        for row in range(rows):
            value = grad_ahead[frame, row]
            far[1, frame, row + 1] = value
            far[0, frame, row + 1], far[2, frame, row + 1] = column_shifts(value)

    for n, (kt, ky) in enumerate(taps):
        if (kt, ky) == (2, 1):
            continue
        pieces, places = [], []
        if kt < 2:
            src = slice(0, 2 - kt), slice(2 - ky, 2 - ky + rows)
            pieces.append([far[(kx,) + src] for kx in range(3)])
            places.append((slice(kt + 1, frames), slice(0, rows)))
        if ky != 1:
            side = 0 if ky == 2 else 1
            edge = 0 if ky == 2 else rows - 1
            pieces.append([near[kx, side, 2 - kt : frames] for kx in range(3)])
            places.append((slice(0, kt + 1), slice(edge, edge + 1)))
        window = jnp.concatenate(
            [jnp.concatenate([flat(v) for v in piece], axis=-1) for piece in pieces], axis=0
        )
        part = dot_turned(window, weight_matrix(w_section, kt, ky))
        at = 0
        for place in places:
            shape = [cut.stop - cut.start for cut in place] + [cols, lanes]
            count = shape[0] * shape[1] * cols
            for lane in range(blocks):
                value = part[at : at + count, lane * lanes : (lane + 1) * lanes]
                total[(lane,) + place] += value.reshape(shape)
            at += count
    tokens[...] = jnp.zeros_like(tokens)
    for src in range(groups):
        at = slice(8 + src * block, 8 + (src + 1) * block)
        for frame in range(depth):
            value = latent[src, frame].astype(f32)[:block]
            tokens[frame, 1, at] = value[:, :width]
            tokens[frame, 2, at] = value[:, width:]
            row = (src * depth + frame) * slots
            count = groups * depth * slots * lanes // channels
            lane = row // count * lanes
            row = (frames + 2) * cols + row % count
            ends = [
                rows_of[row : row + slots, lane : lane + lanes].astype(f32)[:block]
                for rows_of in (near_rows, far_rows)
            ]
            tokens[frame, 0, at] = jnp.where(even, ends[1], ends[0])[:, width:]
            tokens[frame, 3, at] = jnp.where(even, ends[0], ends[1])[:, :width]
    for q in range(2):
        left = tokens[:, :, 7 + q : 7 + q + half]
        right = tokens[:, :, 8 + q : 8 + q + half]
        windows[q] = jnp.concatenate([left, right], axis=-1).astype(bf16)
    patches[...] = jnp.zeros_like(patches)
    lat = width // 4
    for p in range(2):
        for q in range(2):
            for kt in range(3):
                for a in range(2):
                    for b in range(2):
                        for pp in range(2):
                            for qq in range(2):
                                ky, kx = p - 1 + 2 * a + pp, q - 1 + 2 * b + qq
                                if not (0 <= ky < 3 and 0 <= kx < 3):
                                    continue
                                at = (kt * 2 + a) * pair + b * width + (2 * pp + qq) * lat
                                patches[2 * p + q, at : at + lat] = w_in[kt, ky, kx]
    spread[...] = jnp.zeros_like(spread)
    for p in range(2):
        for q in range(2):
            window = jnp.concatenate(
                [
                    flat(windows[q, kt : kt + frames, p + a : p + a + rows // 2])
                    for kt in range(3)
                    for a in range(2)
                ],
                axis=-1,
            )
            weight = patches[2 * p + q]
            pre = dot(window, weight)
            back = jnp.concatenate(
                [
                    jnp.concatenate(
                        [
                            total[lane, frame, 2 * row + p, pl.ds(q, half, stride=2), :]
                            for lane in range(blocks)
                        ],
                        axis=-1,
                    )
                    for frame in range(frames)
                    for row in range(rows // 2)
                ],
                axis=0,
            )
            gate = jax.nn.sigmoid(pre)
            act_grad = (back * (gate * (1.0 + pre * (1.0 - gate)))).astype(bf16)
            terms = dot_turned(act_grad, weight)
            for kt in range(3):
                for a in range(2):
                    at = (kt * 2 + a) * pair
                    spread[kt : kt + frames, p + a : p + a + rows // 2, q : q + half] += terms[
                        :, at : at + pair
                    ].reshape(frames, rows // 2, half, pair)
    centre_out[...] = jnp.zeros_like(centre_out)
    near_out[...] = jnp.zeros_like(near_out)
    far_out[...] = jnp.zeros_like(far_out)
    grid = spread[:, :, 1 : half + 1, :width] + spread[:, :, 0:half, width:]
    tokens[:, :, 0:half] = grid
    for dst in range(groups):
        for frame in range(depth):
            value = [
                tokens[frame, row, dst * block : (dst + 1) * block] for row in range(4)
            ]
            none = jnp.zeros_like(value[0])
            centre = jnp.concatenate([value[1], value[2]], axis=-1)
            up = jnp.concatenate([none, value[0]], axis=-1)
            down = jnp.concatenate([value[3], none], axis=-1)
            fill = jnp.zeros((slots - block, 2 * width), f32)
            padded = lambda v: jnp.concatenate([v, fill], axis=0).astype(bf16)
            centre_out[dst, frame] = padded(centre)
            near_out[dst, frame] = padded(jnp.where(even, down, up))
            far_out[dst, frame] = padded(jnp.where(even, up, down))


def rest_part(places, own, grad_ahead, near_rows, far_rows, w_section, latent, w_in):
    blocks, frames, rows, cols, _ = own.shape
    channels = blocks * lanes
    groups, depth, _, pair = latent.shape
    out = jax.ShapeDtypeStruct(latent.shape, bf16)
    return pl.pallas_call(
        rest_kernel,
        out_shape=[out] * 3,
        in_specs=[pl.BlockSpec(memory_space=pltpu.SMEM)] + [whole] * 7,
        out_specs=[whole] * 3,
        scratch_shapes=[
            pltpu.VMEM(own.shape, f32),
            pltpu.VMEM((3, 2, rows + 2, cols, channels), bf16),
            pltpu.VMEM((3, 2, frames, cols, channels), bf16),
            pltpu.VMEM((depth, rows // 2 + 2, 72, pair // 2), f32),
            pltpu.VMEM((2, depth, rows // 2 + 2, cols // 2, pair), bf16),
            pltpu.VMEM((4, 6 * pair, channels), bf16),
            pltpu.VMEM((depth, rows // 2 + 2, cols // 2 + 8, pair), f32),
        ],
        compiler_params=params(24),
        cost_estimate=pl.CostEstimate(
            flops=2 * 16 * own.size * channels,
            bytes_accessed=2 * w_section.size,
            transcendentals=2 * own.size,
        ),
        name="rest_part",
    )(places, own, grad_ahead, near_rows, far_rows, w_section, latent, w_in)


def weight_kernel(shares, modulated, token_grad, send, field):
    groups, depth, _, pair = shares.shape
    width = pair // 2
    frames, token_rows = modulated.shape[:2]
    model = modulated.shape[-1]
    field[...] = jnp.zeros_like(field)
    for src in range(groups):
        at = src * (frames // groups)
        field[at : at + depth] += shares[src].astype(f32)
    values = field[2 : 2 + frames]
    token_grad[:, 0] = values[:, :, :width].astype(bf16)
    token_grad[:, 1] = values[:, :, width:].astype(bf16)
    turned = jnp.transpose(token_grad[...].reshape(-1, width).astype(f32)).astype(bf16)
    weight = dot(turned, modulated[...].reshape(-1, model))
    half = model // (2 * groups)
    for dst in range(groups):
        at = 2 * half * dst
        stacked = jnp.concatenate(
            [weight[:, at : at + half], weight[:, at + half : at + 2 * half]], axis=0
        )
        send[dst] = jnp.transpose(stacked).astype(bf16)


def weight_terms(shares, modulated):
    groups, depth, _, pair = shares.shape
    frames, token_rows, _, model = modulated.shape
    return pl.pallas_call(
        weight_kernel,
        out_shape=[
            jax.ShapeDtypeStruct((frames, token_rows, slots, pair // 2), bf16),
            jax.ShapeDtypeStruct((groups, model // (2 * groups), pair), bf16),
        ],
        in_specs=[whole] * 2,
        out_specs=[whole] * 2,
        scratch_shapes=[pltpu.VMEM((frames + 2, slots, pair), f32)],
        compiler_params=params(12),
        name="weight_terms",
    )(shares, modulated)


def middle_kernel(got, send):
    total = jnp.sum(got[...].astype(f32), axis=0)
    count, rows, width = send.shape
    total = total.reshape(count // 2, rows, 2 * width).astype(bf16)
    send[0 : count // 2] = total[:, :, :width]
    send[count // 2 :] = total[:, :, width:]


def middle_sum(got, count):
    groups, depth, pair = got.shape
    return pl.pallas_call(
        middle_kernel,
        out_shape=jax.ShapeDtypeStruct((count, 2 * depth // count, pair // 2), bf16),
        in_specs=[whole],
        out_specs=whole,
        compiler_params=params(4),
        name="middle_sum",
    )(got)


def hidden_kernel(hidden, token_grad, scale, w_out, grad_hidden):
    frames, token_rows, tokens, width = hidden.shape
    gain = 1.0 + scale[...]
    block = 3

    def share(step, carry):
        rows = token_grad[pl.ds(step * block, block)].reshape(-1, token_grad.shape[-1])
        mod_grad = dot(rows, w_out[...])
        for frame in range(block):
            for row in range(token_rows):
                at = (frame * token_rows + row) * slots
                scaled = mod_grad[at : at + tokens] * gain
                normed, inverse = normalise(hidden[step * block + frame, row].astype(f32))
                first = jnp.mean(scaled, axis=-1, keepdims=True)
                second = jnp.mean(scaled * normed, axis=-1, keepdims=True)
                value = (scaled - first - normed * second) * inverse
                grad_hidden[step * block + frame, row] = value.astype(bf16)
        return carry

    lax.fori_loop(0, frames // block, share, 0)


def hidden_grad(hidden, token_grad, mod_scale, w_out):
    frames, token_rows, tokens, width = hidden.shape
    return pl.pallas_call(
        hidden_kernel,
        out_shape=jax.ShapeDtypeStruct(hidden.shape, bf16),
        in_specs=[whole] * 4,
        out_specs=whole,
        compiler_params=params(8),
        cost_estimate=pl.CostEstimate(
            flops=2 * frames * 2 * slots * width * w_out.shape[0],
            bytes_accessed=8 * frames * slots * width,
            transcendentals=0,
        ),
        name="hidden_grad",
    )(hidden, token_grad, mod_scale.reshape(1, -1), w_out)


def shards(hidden, mod_scale, mod_shift, w_out, w_in, w_section, section_grad):
    groups, strips = lax.axis_size("tm"), lax.axis_size("height")
    rows = section_grad.shape[1]
    swap = lambda a, b: [(a, b), (b, a)]
    near = sum([swap(i, i + 1) for i in range(0, strips - 1, 2)], [])
    far = sum([swap(i, i + 1) for i in range(1, strips - 1, 2)], [])
    odd = lax.rem(lax.axis_index("height"), 2)
    places = jnp.stack([(1 - odd) * (rows - 1), odd * (rows - 1)]).astype(jnp.int32)
    w_out = jnp.transpose(w_out)

    grad_ahead = lax.ppermute(section_grad, "tm", [(g + 1, g) for g in range(groups - 1)])
    modulated, latent_send = modulate(hidden, mod_scale, mod_shift, w_out, groups)
    latent = lax.all_to_all(latent_send, "tm", 0, 0, tiled=True)
    near_send, far_send = pack_rows(places, section_grad, grad_ahead, latent)
    far_rows = lax.ppermute(far_send, "height", far)
    near_rows = lax.ppermute(near_send, "height", near)

    own, held = own_part(section_grad, w_section)
    centre, near_share, far_share = rest_part(
        places, own, grad_ahead, near_rows, far_rows, held, latent, w_in
    )
    far_share = lax.ppermute(far_share, "height", far)
    near_share = lax.ppermute(near_share, "height", near)
    centre = centre.astype(f32) + near_share.astype(f32) + far_share.astype(f32)
    shares = lax.all_to_all(centre.astype(bf16), "tm", 0, 0, tiled=True)

    token_grad, send = weight_terms(shares, modulated)
    got = lax.all_to_all(send, "tm", 0, 0, tiled=True)
    grad_hidden = hidden_grad(hidden, token_grad, mod_scale, w_out)
    got, grad_hidden = lax.optimization_barrier((got, grad_hidden))
    pieces = lax.all_to_all(middle_sum(got, strips), "height", 0, 0, tiled=True)
    total_tokens = math.prod(hidden.shape[:3]) * groups * strips
    grad_out_weight = jnp.sum(pieces.astype(f32), axis=0) / math.sqrt(total_tokens)
    return (grad_hidden, grad_out_weight)


def solution(mesh):
    placed = (P(None, "height", "tm", None), P(), P(), P(), P(), P(), P("tm", "height", None, None))
    return jax.shard_map(
        shards,
        mesh=mesh,
        in_specs=placed,
        out_specs=(P(None, "height", "tm", None), P(("tm", "height"), None)),
        check_vma=False,
    )
```

```python
import functools
import math

import jax
import jax.numpy as jnp
from jax import lax
from jax.experimental import pallas as pl
from jax.experimental.pallas import tpu as pltpu
from jax.sharding import PartitionSpec as P

epsilon = 1e-05
slots = 16
lanes = 128
f32 = jnp.float32
bf16 = jnp.bfloat16
whole = pl.BlockSpec(memory_space=pltpu.VMEM)
scalars = pl.BlockSpec(memory_space=pltpu.SMEM)
far_off = pl.BlockSpec(memory_space=pltpu.HBM)
early = 2


def params(mib):
    return pltpu.CompilerParams(vmem_limit_bytes=int(mib * 2**20))


def dot(lhs, rhs):
    return jnp.dot(lhs, rhs, preferred_element_type=f32)


def dot_turned(lhs, rhs):
    return lax.dot_general(lhs, rhs, (((1,), (1,)), ((), ())), preferred_element_type=f32)


def normalise(values):
    center = jnp.mean(values, axis=-1, keepdims=True)
    shifted = values - center
    spread = jnp.mean(shifted * shifted, axis=-1, keepdims=True)
    inverse = lax.rsqrt(spread + epsilon)
    return shifted * inverse, inverse


def fetch_kernel(grad, ahead, last, sems):
    copies = [
        pltpu.make_async_copy(grad.at[0:2], ahead, sems.at[0]),
        pltpu.make_async_copy(grad.at[2:3], last, sems.at[1]),
    ]
    for copy in copies:
        copy.start()
    for copy in copies:
        copy.wait()


def fetch(grad):
    return pl.pallas_call(
        fetch_kernel,
        out_shape=[
            jax.ShapeDtypeStruct((2,) + grad.shape[1:], bf16),
            jax.ShapeDtypeStruct((1,) + grad.shape[1:], bf16),
        ],
        in_specs=[far_off],
        out_specs=[whole] * 2,
        scratch_shapes=[pltpu.SemaphoreType.DMA((2,))],
        compiler_params=params(4),
        name="fetch",
    )(grad)


def modulate_kernel(
    hidden, scale, shift, w_out, w_section, modulated, latent, held, rows, sems, out_sems
):
    frames, token_rows, tokens, width = hidden.shape
    block = 3
    gain = 1.0 + scale[...]
    blank = jnp.zeros((slots - tokens, width), f32)
    copies = [
        pltpu.make_async_copy(w_section.at[kt, ky], held.at[n], sems.at[n])
        for n, (kt, ky) in enumerate(taps[:early])
    ]
    for copy in copies:
        copy.start()

    def out_copy(step):
        at = pl.ds(step * block, block)
        return pltpu.make_async_copy(rows.at[at], modulated.at[at], out_sems.at[step])

    def share(step, carry):
        for frame in range(block):
            for row in range(token_rows):
                normed, _ = normalise(hidden[step * block + frame, row].astype(f32))
                value = jnp.concatenate([normed * gain + shift[...], blank], axis=0)
                rows[step * block + frame, row] = value.astype(bf16)
        out_copy(step).start()
        value = rows[pl.ds(step * block, block)].reshape(-1, width)
        value = dot_turned(value, w_out[...]).astype(bf16)
        value = value.reshape(block, token_rows, slots, value.shape[-1])
        latent[pl.ds(step * block, block)] = jnp.concatenate([value[:, 0], value[:, 1]], axis=-1)
        return carry

    lax.fori_loop(0, frames // block, share, 0)
    for copy in copies:
        copy.wait()
    for step in range(frames // block):
        out_copy(step).wait()


def modulate(hidden, mod_scale, mod_shift, w_out, w_section):
    frames, token_rows, tokens, width = hidden.shape
    token_width = w_out.shape[0]
    out = jax.ShapeDtypeStruct((frames, token_rows, slots, width), bf16)
    return pl.pallas_call(
        modulate_kernel,
        out_shape=[
            out,
            jax.ShapeDtypeStruct((frames, slots, 2 * token_width), bf16),
            jax.ShapeDtypeStruct((early,) + w_section.shape[2:], bf16),
        ],
        in_specs=[whole] * 4 + [far_off],
        out_specs=[far_off, whole, whole],
        scratch_shapes=[
            pltpu.VMEM(out.shape, bf16),
            pltpu.SemaphoreType.DMA((early,)),
            pltpu.SemaphoreType.DMA((frames // 3,)),
        ],
        compiler_params=params(44),
        cost_estimate=pl.CostEstimate(
            flops=2 * frames * 2 * slots * width * token_width,
            bytes_accessed=8 * frames * slots * width,
            transcendentals=0,
        ),
        name="modulate",
    )(hidden, mod_scale.reshape(1, -1), mod_shift.reshape(1, -1), w_out, w_section)


def column_shifts(value):
    cols, channels = value.shape
    wide = value.astype(f32)
    place = lax.broadcasted_iota(jnp.int32, (cols, channels), 0)
    nxt = jnp.where(place == cols - 1, 0.0, pltpu.roll(wide, cols - 1, 0))
    prv = jnp.where(place == 0, 0.0, pltpu.roll(wide, 1, 0))
    return nxt.astype(bf16), prv.astype(bf16)


taps = [(2 - n // 3, (1, 0, 2)[n % 3]) for n in range(9)]


def flat(value):
    return value.reshape(-1, value.shape[-1])


def weight_matrix(held_first, held_rest, n):
    block = held_first[n] if n < early else held_rest[n - early]
    return jnp.concatenate([block[kx] for kx in range(3)], axis=-1)


def pack_kernel(places, ahead, last, grad_ahead, latent, near, far):
    cols, channels = ahead.shape[-2:]
    for side, out in ((0, near), (1, far)):
        row = places[side]
        pieces = [ahead[0, row], ahead[1, row], last[0, row]]
        pieces += [grad_ahead[0, row], grad_ahead[1, row]]
        for n, piece in enumerate(pieces):
            out[n * cols : (n + 1) * cols] = piece
        at = len(pieces) * cols
        tail = flat(latent[...])
        count = tail.shape[0] * lanes // channels
        for lane in range(channels // lanes):
            out[at : at + count, lane * lanes : (lane + 1) * lanes] = tail[
                lane * count : (lane + 1) * count
            ]


def pack_rows(places, ahead, last, grad_ahead, latent):
    cols, channels = ahead.shape[-2:]
    total = 5 * cols + latent.size // channels
    return pl.pallas_call(
        pack_kernel,
        in_specs=[scalars] + [whole] * 4,
        out_specs=[whole] * 2,
        out_shape=[jax.ShapeDtypeStruct((total, channels), bf16)] * 2,
        compiler_params=params(4),
        name="pack_rows",
    )(places, ahead, last, grad_ahead, latent)


def latent_kernel(places, near_rows, far_rows, latent, send):
    even = places[0] != 0
    frames, _, pair = latent.shape
    groups, depth = send.shape[:2]
    block = depth - 2
    channels = near_rows.shape[1]
    count = frames * slots * pair // channels
    start = near_rows.shape[0] - count
    send[0, 0:2] = jnp.zeros_like(send[0, 0:2])
    for frame in range(frames):
        row, lane = frame * slots % count, frame * slots // count * lanes
        ends = [
            ref[start + row : start + row + slots, lane : lane + lanes]
            for ref in (near_rows, far_rows)
        ]
        above = jnp.where(even, ends[1], ends[0])[:, pair // 2 :]
        below = jnp.where(even, ends[0], ends[1])[:, : pair // 2]
        value = jnp.concatenate([latent[frame], below, above], axis=-1)
        for dst in range(groups):
            at = frame + 2 - block * dst
            if 0 <= at < depth:
                send[dst, at] = value


def latent_shares(places, near_rows, far_rows, latent, groups):
    frames, _, pair = latent.shape
    return pl.pallas_call(
        latent_kernel,
        in_specs=[scalars] + [whole] * 3,
        out_specs=whole,
        out_shape=jax.ShapeDtypeStruct((groups, frames // groups + 2, slots, 2 * pair), bf16),
        compiler_params=params(4),
        name="latent_shares",
    )(places, near_rows, far_rows, latent)


def own_kernel(ahead, last, w_section, held_first, total, held_rest, shifts, sems):
    _, rows, cols, channels = ahead.shape
    frames = 3
    copies = [
        pltpu.make_async_copy(w_section.at[kt, ky], held_rest.at[n], sems.at[n])
        for n, (kt, ky) in enumerate(taps[early:])
    ]
    for copy in copies:
        copy.start()
    for frame in range(frames):
        for row in range(rows):
            value = ahead[frame, row] if frame < 2 else last[0, row]
            shifts[0, frame, row], shifts[1, frame, row] = column_shifts(value)
    for n, (kt, ky) in enumerate(taps):
        lo, hi = max(0, ky - 1), rows + min(0, ky - 1)
        at = slice(lo + 1 - ky, hi + 1 - ky)
        src = slice(2 - kt, frames), at
        centre = flat(last[:, at])
        if kt > 0:
            centre = jnp.concatenate([flat(ahead[2 - kt : 2, at]), centre], axis=0)
        window = jnp.concatenate(
            [flat(shifts[(0,) + src]), centre, flat(shifts[(1,) + src])], axis=-1
        )
        if n >= early:
            copies[n - early].wait()
        part = dot_turned(window, weight_matrix(held_first, held_rest, n))
        for lane in range(channels // lanes):
            value = part[:, lane * lanes : (lane + 1) * lanes]
            value = value.reshape(kt + 1, hi - lo, cols, lanes)
            if n == 0:
                total[lane] = value
            else:
                total[lane, 0 : kt + 1, lo:hi] += value


def own_part(ahead, last, w_section, held_first):
    _, rows, cols, channels = ahead.shape
    return pl.pallas_call(
        own_kernel,
        out_shape=[
            jax.ShapeDtypeStruct((channels // lanes, 3, rows, cols, lanes), f32),
            jax.ShapeDtypeStruct((9 - early,) + w_section.shape[2:], bf16),
        ],
        in_specs=[whole, whole, far_off, whole],
        out_specs=[whole] * 2,
        scratch_shapes=[
            pltpu.VMEM((2, 3, rows, cols, channels), bf16),
            pltpu.SemaphoreType.DMA((9 - early,)),
        ],
        compiler_params=params(30),
        cost_estimate=pl.CostEstimate(
            flops=2 * 45 * rows * cols * channels * channels,
            bytes_accessed=2 * w_section.size,
            transcendentals=0,
        ),
        name="own_part",
    )(ahead, last, w_section, held_first)


def edge_kernel(
    places, own, grad_ahead, near_rows, far_rows, held_first, held_rest, w_in,
    total, far, patches, near,
):
    even = places[0] != 0
    blocks, frames, rows, cols, _ = own.shape
    for lane in range(blocks):
        total[lane, :, 0] = own[lane, :, 0]
        total[lane, :, 1] = own[lane, :, rows - 1]
    for frame in range(frames + 2):
        at = slice(frame * cols, (frame + 1) * cols)
        ends = near_rows[at], far_rows[at]
        for side in range(2):
            value = jnp.where(even == (side == 1), ends[0], ends[1])
            shifted = column_shifts(value)
            if frame < frames:
                near[1, side, frame] = value
                near[0, side, frame], near[2, side, frame] = shifted
            else:
                row = side * (rows + 1)
                far[1, frame - frames, row] = value
                far[0, frame - frames, row], far[2, frame - frames, row] = shifted
    for frame in range(2):
        for row in range(rows):
            value = grad_ahead[frame, row]
            far[1, frame, row + 1] = value
            far[0, frame, row + 1], far[2, frame, row + 1] = column_shifts(value)

    patches[...] = jnp.zeros_like(patches)
    lat = w_in.shape[3]
    for n in range(4 * 3 * 2 * 2 * 2 * 2):
        p, q, kt, a, b, pp, qq = [
            n // size % top
            for size, top in ((96, 2), (48, 2), (16, 3), (8, 2), (4, 2), (2, 2), (1, 2))
        ]
        ky, kx = p - 1 + 2 * a + pp, q - 1 + 2 * b + qq
        if 0 <= ky < 3 and 0 <= kx < 3:
            at = (((kt * 2 + a) * 2 + b) * 4 + 2 * pp + qq) * lat
            patches[2 * p + q, at : at + lat] = w_in[kt, ky, kx]

    for n, (kt, ky) in enumerate(taps):
        pieces, places_of = [], []
        if kt < 2:
            for side, row in ((0, 0), (1, rows - 1)):
                pieces.append([far[kx, 0 : 2 - kt, row + 2 - ky] for kx in range(3)])
                places_of.append((slice(kt + 1, frames), side))
        if ky != 1:
            side = 0 if ky == 2 else 1
            pieces.append([near[kx, side, 2 - kt : frames] for kx in range(3)])
            places_of.append((slice(0, kt + 1), side))
        if not pieces:
            continue
        window = jnp.concatenate(
            [jnp.concatenate([flat(v) for v in piece], axis=-1) for piece in pieces], axis=0
        )
        part = dot_turned(window, weight_matrix(held_first, held_rest, n))
        at = 0
        for place, side in places_of:
            count = (place.stop - place.start) * cols
            for lane in range(blocks):
                value = part[at : at + count, lane * lanes : (lane + 1) * lanes]
                total[lane, place, side] += value.reshape(-1, cols, lanes)
            at += count


def edge_part(places, own, grad_ahead, near_rows, far_rows, held_first, held_rest, w_in):
    blocks, frames, rows, cols, _ = own.shape
    channels = blocks * lanes
    pair = 8 * w_in.shape[3]
    return pl.pallas_call(
        edge_kernel,
        out_shape=[
            jax.ShapeDtypeStruct((blocks, frames, 2, cols, lanes), f32),
            jax.ShapeDtypeStruct((3, 2, rows + 2, cols, channels), bf16),
            jax.ShapeDtypeStruct((4, 6 * pair, channels), bf16),
        ],
        in_specs=[scalars] + [whole] * 7,
        out_specs=[whole] * 3,
        scratch_shapes=[pltpu.VMEM((3, 2, frames, cols, channels), bf16)],
        compiler_params=params(12),
        cost_estimate=pl.CostEstimate(
            flops=2 * 5 * own.size * channels, bytes_accessed=0, transcendentals=0
        ),
        name="edge_part",
    )(places, own, grad_ahead, near_rows, far_rows, held_first, held_rest, w_in)


def latent_phase(total, slot_of, row_of, spread_row, windows, patches, spread):
    blocks, frames, _, cols, _ = total.shape
    half = cols // 2
    pair = windows.shape[-1]
    for p in range(2):
        for q in range(2):
            top = row_of[p] + p
            window = jnp.concatenate(
                [
                    flat(windows[q, kt : kt + frames, top + a])
                    for kt in range(3)
                    for a in range(2)
                ],
                axis=-1,
            )
            weight = patches[2 * p + q]
            pre = dot(window, weight)
            back = jnp.concatenate(
                [
                    jnp.concatenate(
                        [
                            total[lane, frame, slot_of[p], pl.ds(q, half, stride=2), :]
                            for lane in range(blocks)
                        ],
                        axis=-1,
                    )
                    for frame in range(frames)
                ],
                axis=0,
            )
            gate = jax.nn.sigmoid(pre)
            act_grad = (back * (gate * (1.0 + pre * (1.0 - gate)))).astype(bf16)
            terms = dot_turned(act_grad, weight)
            for kt in range(3):
                for a in range(2):
                    at = (kt * 2 + a) * pair
                    spread[kt : kt + frames, top + a - spread_row, q : q + half] += terms[
                        :, at : at + pair
                    ].reshape(frames, half, pair)


def shares_of(spread, row, half):
    width = spread.shape[-1] // 2
    return spread[:, row, 1 : half + 1, :width] + spread[:, row, 0:half, width:]


def edge_latent_kernel(
    places, total, latent, patches, near_out, far_out, windows, spread, tokens
):
    even = places[0] != 0
    groups, depth = latent.shape[:2]
    width = latent.shape[-1] // 4
    half = windows.shape[3]
    block = half // groups
    tokens[...] = jnp.zeros_like(tokens)
    for src in range(groups):
        at = slice(8 + src * block, 8 + (src + 1) * block)
        for frame in range(depth):
            value = latent[src, frame].astype(f32)[:block]
            for n, row in enumerate((1, 2, 3, 0)):
                tokens[frame, row, at] = value[:, n * width : (n + 1) * width]
    for q in range(2):
        left = tokens[:, :, 7 + q : 7 + q + half]
        right = tokens[:, :, 8 + q : 8 + q + half]
        windows[q] = jnp.concatenate([left, right], axis=-1).astype(bf16)
    spread[...] = jnp.zeros_like(spread)
    latent_phase(total, (0, 1), (0, 1), 0, windows, patches, spread)
    for n, row in enumerate((0, 3)):
        tokens[:, n, 0:half] = shares_of(spread, row, half)
    none = jnp.zeros((block, width), f32)
    fill = jnp.zeros((slots - block, 2 * width), f32)
    for dst in range(groups):
        at = slice(dst * block, (dst + 1) * block)
        for frame in range(depth):
            up = jnp.concatenate([none, tokens[frame, 0, at]], axis=-1)
            down = jnp.concatenate([tokens[frame, 1, at], none], axis=-1)
            padded = lambda v: jnp.concatenate([v, fill], axis=0).astype(bf16)
            near_out[dst, frame] = padded(jnp.where(even, down, up))
            far_out[dst, frame] = padded(jnp.where(even, up, down))


def edge_latent(places, total, latent, patches):
    groups, depth, _, quad = latent.shape
    cols = total.shape[3]
    out = jax.ShapeDtypeStruct((groups, depth, slots, quad // 2), bf16)
    return pl.pallas_call(
        edge_latent_kernel,
        out_shape=[
            out,
            out,
            jax.ShapeDtypeStruct((2, depth, 4, cols // 2, quad // 2), bf16),
            jax.ShapeDtypeStruct((depth, 4, cols // 2 + 8, quad // 2), f32),
        ],
        in_specs=[scalars] + [whole] * 3,
        out_specs=[whole] * 4,
        scratch_shapes=[pltpu.VMEM((depth, 4, 72, quad // 4), f32)],
        compiler_params=params(10),
        name="edge_latent",
    )(places, total, latent, patches)


def inner_kernel(
    own, far, held_first, held_rest, windows, patches, spread_in, out, total, spread, tokens
):
    blocks, frames, rows, cols, _ = own.shape
    half = windows.shape[3]
    groups, depth = out.shape[:2]
    block = half // groups
    total[...] = own[:, :, 1 : rows - 1]
    spread[...] = spread_in[:, 1:3]
    for n, (kt, ky) in enumerate(taps):
        if kt == 2:
            continue
        src = slice(0, 2 - kt), slice(3 - ky, rows + 1 - ky)
        window = jnp.concatenate([flat(far[(kx,) + src]) for kx in range(3)], axis=-1)
        part = dot_turned(window, weight_matrix(held_first, held_rest, n))
        for lane in range(blocks):
            value = part[:, lane * lanes : (lane + 1) * lanes]
            total[lane, kt + 1 : frames] += value.reshape(2 - kt, rows - 2, cols, lanes)
    latent_phase(total, (1, 0), (1, 0), 1, windows, patches, spread)
    for row in range(2):
        tokens[:, row] = shares_of(spread, row, half)
    fill = jnp.zeros((slots - block, out.shape[-1]), f32)
    for dst in range(groups):
        at = slice(dst * block, (dst + 1) * block)
        for frame in range(depth):
            value = jnp.concatenate([tokens[frame, 0, at], tokens[frame, 1, at]], axis=-1)
            out[dst, frame] = jnp.concatenate([value, fill], axis=0)


def inner_part(own, far, held_first, held_rest, windows, patches, spread, groups):
    blocks, frames, rows, cols, _ = own.shape
    channels = blocks * lanes
    depth, _, wide, pair = spread.shape
    return pl.pallas_call(
        inner_kernel,
        out_shape=jax.ShapeDtypeStruct((groups, depth, slots, pair), f32),
        in_specs=[whole] * 7,
        out_specs=whole,
        scratch_shapes=[
            pltpu.VMEM((blocks, frames, rows - 2, cols, lanes), f32),
            pltpu.VMEM((depth, 2, wide, pair), f32),
            pltpu.VMEM((depth, 2, cols // 2, pair // 2), f32),
        ],
        compiler_params=params(12),
        cost_estimate=pl.CostEstimate(
            flops=2 * 4 * own.size * channels, bytes_accessed=0, transcendentals=own.size
        ),
        name="inner_part",
    )(own, far, held_first, held_rest, windows, patches, spread)


def weight_kernel(shares, modulated, token_grad, send, field):
    groups, depth, _, pair = shares.shape
    width = pair // 2
    frames, token_rows = modulated.shape[:2]
    model = modulated.shape[-1]
    field[...] = jnp.zeros_like(field)
    for src in range(groups):
        at = src * (frames // groups)
        field[at : at + depth] += shares[src].astype(f32)
    values = field[2 : 2 + frames]
    token_grad[:, 0] = values[:, :, :width].astype(bf16)
    token_grad[:, 1] = values[:, :, width:].astype(bf16)
    turned = jnp.transpose(token_grad[...].reshape(-1, width).astype(f32)).astype(bf16)
    weight = dot(turned, modulated[...].reshape(-1, model))
    half = model // (2 * groups)
    for dst in range(groups):
        at = 2 * half * dst
        stacked = jnp.concatenate(
            [weight[:, at : at + half], weight[:, at + half : at + 2 * half]], axis=0
        )
        send[dst] = jnp.transpose(stacked).astype(bf16)


def weight_terms(shares, modulated):
    groups, depth, _, pair = shares.shape
    frames, token_rows, _, model = modulated.shape
    return pl.pallas_call(
        weight_kernel,
        out_shape=[
            jax.ShapeDtypeStruct((frames, token_rows, slots, pair // 2), bf16),
            jax.ShapeDtypeStruct((groups, model // (2 * groups), pair), bf16),
        ],
        in_specs=[whole] * 2,
        out_specs=[whole] * 2,
        scratch_shapes=[pltpu.VMEM((frames + 2, slots, pair), f32)],
        compiler_params=params(12),
        name="weight_terms",
    )(shares, modulated)


def middle_kernel(got, send):
    total = jnp.sum(got[...].astype(f32), axis=0)
    count, rows, width = send.shape
    total = total.reshape(count // 2, rows, 2 * width).astype(bf16)
    send[0 : count // 2] = total[:, :, :width]
    send[count // 2 :] = total[:, :, width:]


def middle_sum(got, count):
    groups, depth, pair = got.shape
    return pl.pallas_call(
        middle_kernel,
        out_shape=jax.ShapeDtypeStruct((count, 2 * depth // count, pair // 2), bf16),
        in_specs=[whole],
        out_specs=whole,
        compiler_params=params(4),
        name="middle_sum",
    )(got)


def hidden_kernel(hidden, token_grad, scale, w_out, grad_hidden):
    frames, token_rows, tokens, width = hidden.shape
    gain = 1.0 + scale[...]
    block = 3

    def share(step, carry):
        rows = token_grad[pl.ds(step * block, block)].reshape(-1, token_grad.shape[-1])
        mod_grad = dot(rows, w_out[...])
        for frame in range(block):
            for row in range(token_rows):
                at = (frame * token_rows + row) * slots
                scaled = mod_grad[at : at + tokens] * gain
                normed, inverse = normalise(hidden[step * block + frame, row].astype(f32))
                first = jnp.mean(scaled, axis=-1, keepdims=True)
                second = jnp.mean(scaled * normed, axis=-1, keepdims=True)
                value = (scaled - first - normed * second) * inverse
                grad_hidden[step * block + frame, row] = value.astype(bf16)
        return carry

    lax.fori_loop(0, frames // block, share, 0)


def hidden_grad(hidden, token_grad, mod_scale, w_out):
    frames, token_rows, tokens, width = hidden.shape
    return pl.pallas_call(
        hidden_kernel,
        out_shape=jax.ShapeDtypeStruct(hidden.shape, bf16),
        in_specs=[whole] * 4,
        out_specs=whole,
        compiler_params=params(8),
        cost_estimate=pl.CostEstimate(
            flops=2 * frames * 2 * slots * width * w_out.shape[0],
            bytes_accessed=8 * frames * slots * width,
            transcendentals=0,
        ),
        name="hidden_grad",
    )(hidden, token_grad, mod_scale.reshape(1, -1), w_out)


def shards(hidden, mod_scale, mod_shift, w_out, w_in, w_section, section_grad):
    groups, strips = lax.axis_size("tm"), lax.axis_size("height")
    rows = section_grad.shape[1]
    swap = lambda a, b: [(a, b), (b, a)]
    near = sum([swap(i, i + 1) for i in range(0, strips - 1, 2)], [])
    far = sum([swap(i, i + 1) for i in range(1, strips - 1, 2)], [])
    odd = lax.rem(lax.axis_index("height"), 2)
    places = jnp.stack([(1 - odd) * (rows - 1), odd * (rows - 1)]).astype(jnp.int32)
    w_out = jnp.transpose(w_out)

    ahead, last = fetch(section_grad)
    grad_ahead = lax.ppermute(ahead, "tm", [(g + 1, g) for g in range(groups - 1)])
    modulated, latent, held_first = modulate(hidden, mod_scale, mod_shift, w_out, w_section)
    near_send, far_send = pack_rows(places, ahead, last, grad_ahead, latent)
    far_rows = lax.ppermute(far_send, "height", far)
    near_rows = lax.ppermute(near_send, "height", near)
    own, held_rest = own_part(ahead, last, w_section, held_first)
    latent_send = latent_shares(places, near_rows, far_rows, latent, groups)
    latent_got = lax.all_to_all(latent_send, "tm", 0, 0, tiled=True)
    edge, far_grad, patches = edge_part(
        places, own, grad_ahead, near_rows, far_rows, held_first, held_rest, w_in
    )
    near_share, far_share, windows, spread = edge_latent(places, edge, latent_got, patches)
    far_share = lax.ppermute(far_share, "height", far)
    near_share = lax.ppermute(near_share, "height", near)
    centre = inner_part(own, far_grad, held_first, held_rest, windows, patches, spread, groups)
    centre = centre + near_share.astype(f32) + far_share.astype(f32)
    shares = lax.all_to_all(centre.astype(bf16), "tm", 0, 0, tiled=True)

    token_grad, send = weight_terms(shares, modulated)
    got = lax.all_to_all(send, "tm", 0, 0, tiled=True)
    grad_hidden = hidden_grad(hidden, token_grad, mod_scale, w_out)
    pieces = lax.all_to_all(middle_sum(got, strips), "height", 0, 0, tiled=True)
    total_tokens = math.prod(hidden.shape[:3]) * groups * strips
    grad_out_weight = jnp.sum(pieces.astype(f32), axis=0) / math.sqrt(total_tokens)
    return (grad_hidden, grad_out_weight)


def solution(mesh):
    placed = (P(None, "height", "tm", None), P(), P(), P(), P(), P(), P("tm", "height", None, None))
    return jax.shard_map(
        shards,
        mesh=mesh,
        in_specs=placed,
        out_specs=(P(None, "height", "tm", None), P(("tm", "height"), None)),
        check_vma=False,
    )
```

```python
import functools
import math

import jax
import jax.numpy as jnp
from jax import lax
from jax.experimental import pallas as pl
from jax.experimental.pallas import tpu as pltpu
from jax.sharding import PartitionSpec as P

epsilon = 1e-05
slots = 16
lanes = 128
f32 = jnp.float32
bf16 = jnp.bfloat16
whole = pl.BlockSpec(memory_space=pltpu.VMEM)
scalars = pl.BlockSpec(memory_space=pltpu.SMEM)
far_off = pl.BlockSpec(memory_space=pltpu.HBM)


def params(mib):
    return pltpu.CompilerParams(vmem_limit_bytes=int(mib * 2**20))


def dot(lhs, rhs):
    return jnp.dot(lhs, rhs, preferred_element_type=f32)


def dot_turned(lhs, rhs):
    return lax.dot_general(lhs, rhs, (((1,), (1,)), ((), ())), preferred_element_type=f32)


def normalise(values):
    center = jnp.mean(values, axis=-1, keepdims=True)
    shifted = values - center
    spread = jnp.mean(shifted * shifted, axis=-1, keepdims=True)
    inverse = lax.rsqrt(spread + epsilon)
    return shifted * inverse, inverse


def modulate_kernel(source, scale, shift, w_out, modulated, send, hidden, rows, in_sems, out_sems):
    frames, token_rows, tokens, width = hidden.shape
    groups = send.shape[0]
    block = frames // groups
    gain = 1.0 + scale[...]
    blank = jnp.zeros((slots - tokens, width), f32)
    send[0, 0:2] = jnp.zeros_like(send[0, 0:2])

    def in_copy(step):
        at = pl.ds(step * block, block)
        return pltpu.make_async_copy(source.at[at], hidden.at[at], in_sems.at[step])

    for step in range(groups):
        in_copy(step).start()

    def out_copy(step):
        at = pl.ds(step * block, block)
        return pltpu.make_async_copy(rows.at[at], modulated.at[at], out_sems.at[step])

    def share(step, carry):
        in_copy(step).wait()
        for frame in range(block):
            for row in range(token_rows):
                normed, _ = normalise(hidden[step * block + frame, row].astype(f32))
                value = jnp.concatenate([normed * gain + shift[...], blank], axis=0)
                rows[step * block + frame, row] = value.astype(bf16)
        out_copy(step).start()
        value = rows[pl.ds(step * block, block)].reshape(-1, width)
        value = dot_turned(value, w_out[...]).astype(bf16)
        value = value.reshape(block, token_rows, slots, value.shape[-1])
        paired = jnp.concatenate([value[:, 0], value[:, 1]], axis=-1)
        for frame in range(block):
            send[step, frame + 2] = paired[frame]

        @pl.when(step < groups - 1)
        def _():
            for frame in range(1, block):
                send[step + 1, frame - 1] = paired[frame]

        return carry

    lax.fori_loop(0, groups, share, 0)
    for step in range(groups):
        out_copy(step).wait()


def modulate(hidden, mod_scale, mod_shift, w_out, groups):
    frames, token_rows, tokens, width = hidden.shape
    token_width = w_out.shape[0]
    out = jax.ShapeDtypeStruct((frames, token_rows, slots, width), bf16)
    return pl.pallas_call(
        modulate_kernel,
        out_shape=[
            out,
            jax.ShapeDtypeStruct((groups, frames // groups + 2, slots, 2 * token_width), bf16),
        ],
        in_specs=[far_off] + [whole] * 3,
        out_specs=[far_off, whole],
        scratch_shapes=[
            pltpu.VMEM(hidden.shape, bf16),
            pltpu.VMEM(out.shape, bf16),
            pltpu.SemaphoreType.DMA((groups,)),
            pltpu.SemaphoreType.DMA((groups,)),
        ],
        compiler_params=params(53),
        cost_estimate=pl.CostEstimate(
            flops=2 * frames * 2 * slots * width * token_width,
            bytes_accessed=8 * frames * slots * width,
            transcendentals=0,
        ),
        name="modulate",
    )(hidden, mod_scale.reshape(1, -1), mod_shift.reshape(1, -1), w_out)


def column_shifts(value):
    cols, channels = value.shape
    wide = value.astype(f32)
    place = lax.broadcasted_iota(jnp.int32, (cols, channels), 0)
    nxt = jnp.where(place == cols - 1, 0.0, pltpu.roll(wide, cols - 1, 0))
    prv = jnp.where(place == 0, 0.0, pltpu.roll(wide, 1, 0))
    return nxt.astype(bf16), prv.astype(bf16)


taps = [(2 - n // 3, (1, 0, 2)[n % 3]) for n in range(9)]


def flat(value):
    return value.reshape(-1, value.shape[-1])


def weight_matrix(held, kt, ky):
    return jnp.concatenate([held[kt, ky, kx] for kx in range(3)], axis=-1)


def pack_kernel(places, grad, grad_ahead, latent, near, far, sems):
    frames, _, cols, channels = grad.shape
    copies = [
        pltpu.make_async_copy(
            grad.at[frame, places[side]],
            out.at[frame * cols : (frame + 1) * cols],
            sems.at[side * frames + frame],
        )
        for side, out in ((0, near), (1, far))
        for frame in range(frames)
    ]
    for copy in copies:
        copy.start()
    for side, out in ((0, near), (1, far)):
        for frame in range(2):
            at = (frames + frame) * cols
            out[at : at + cols] = grad_ahead[frame, places[side]]
        at = (frames + 2) * cols
        tail = flat(latent[...])
        count = tail.shape[0] * lanes // channels
        for lane in range(channels // lanes):
            out[at : at + count, lane * lanes : (lane + 1) * lanes] = tail[
                lane * count : (lane + 1) * count
            ]
    for copy in copies:
        copy.wait()


def pack_rows(places, grad, grad_ahead, latent):
    frames, _, cols, channels = grad.shape
    total = (frames + 2) * cols + latent.size // channels
    return pl.pallas_call(
        pack_kernel,
        in_specs=[scalars, far_off, whole, whole],
        out_specs=[whole] * 2,
        out_shape=[jax.ShapeDtypeStruct((total, channels), bf16)] * 2,
        scratch_shapes=[pltpu.SemaphoreType.DMA((2 * frames,))],
        compiler_params=params(4),
        name="pack_rows",
    )(places, grad, grad_ahead, latent)


def own_kernel(grad, grad_ahead, w_section, total, held, shifts, sems):
    frames, rows, cols, channels = grad.shape
    copies = [
        pltpu.make_async_copy(w_section.at[kt, ky], held.at[kt, ky], sems.at[n])
        for n, (kt, ky) in enumerate(taps)
    ]
    for copy in copies:
        copy.start()
    for frame in range(frames + 2):
        for row in range(rows):
            value = grad[frame, row] if frame < frames else grad_ahead[frame - frames, row]
            shifts[0, frame, row], shifts[1, frame, row] = column_shifts(value)
    for n, (kt, ky) in enumerate(taps):
        lo, hi = max(0, ky - 1), rows + min(0, ky - 1)
        at = slice(lo + 1 - ky, hi + 1 - ky)
        src = slice(2 - kt, frames + 2 - kt), at
        centre = flat(grad[2 - kt :, at])
        if kt < 2:
            centre = jnp.concatenate([centre, flat(grad_ahead[: 2 - kt, at])], axis=0)
        window = jnp.concatenate(
            [flat(shifts[(0,) + src]), centre, flat(shifts[(1,) + src])], axis=-1
        )
        copies[n].wait()
        part = dot_turned(window, weight_matrix(held, kt, ky))
        for lane in range(channels // lanes):
            value = part[:, lane * lanes : (lane + 1) * lanes]
            value = value.reshape(frames, hi - lo, cols, lanes)
            if n == 0:
                total[lane] = value
            else:
                total[lane, :, lo:hi] += value


def own_part(grad, grad_ahead, w_section):
    frames, rows, cols, channels = grad.shape
    return pl.pallas_call(
        own_kernel,
        out_shape=[
            jax.ShapeDtypeStruct((channels // lanes, frames, rows, cols, lanes), f32),
            jax.ShapeDtypeStruct(w_section.shape, bf16),
        ],
        in_specs=[whole, whole, far_off],
        out_specs=[whole] * 2,
        scratch_shapes=[
            pltpu.VMEM((2, frames + 2, rows, cols, channels), bf16),
            pltpu.SemaphoreType.DMA((len(taps),)),
        ],
        compiler_params=params(26),
        cost_estimate=pl.CostEstimate(
            flops=2 * 24 * grad.size * channels,
            bytes_accessed=2 * w_section.size,
            transcendentals=0,
        ),
        name="own_part",
    )(grad, grad_ahead, w_section)


def edge_kernel(places, own, near_rows, far_rows, held, w_in, total, patches, near):
    even = places[0] != 0
    blocks, frames, rows, cols, _ = own.shape
    for lane in range(blocks):
        total[lane, :, 0] = own[lane, :, 0]
        total[lane, :, 1] = own[lane, :, rows - 1]
    for frame in range(frames + 2):
        at = slice(frame * cols, (frame + 1) * cols)
        ends = near_rows[at], far_rows[at]
        for side in range(2):
            value = jnp.where(even == (side == 1), ends[0], ends[1])
            near[1, side, frame] = value
            near[0, side, frame], near[2, side, frame] = column_shifts(value)

    patches[...] = jnp.zeros_like(patches)
    lat = w_in.shape[3]
    for n in range(4 * 3 * 2 * 2 * 2 * 2):
        p, q, kt, a, b, pp, qq = [
            n // size % top
            for size, top in ((96, 2), (48, 2), (16, 3), (8, 2), (4, 2), (2, 2), (1, 2))
        ]
        ky, kx = p - 1 + 2 * a + pp, q - 1 + 2 * b + qq
        if 0 <= ky < 3 and 0 <= kx < 3:
            at = (((kt * 2 + a) * 2 + b) * 4 + 2 * pp + qq) * lat
            patches[2 * p + q, at : at + lat] = w_in[kt, ky, kx]

    for kt, ky in taps:
        if ky == 1:
            continue
        side = 0 if ky == 2 else 1
        window = jnp.concatenate(
            [flat(near[kx, side, 2 - kt : frames + 2 - kt]) for kx in range(3)], axis=-1
        )
        part = dot_turned(window, weight_matrix(held, kt, ky))
        for lane in range(blocks):
            value = part[:, lane * lanes : (lane + 1) * lanes]
            total[lane, :, side] += value.reshape(frames, cols, lanes)


def edge_part(places, own, near_rows, far_rows, held, w_in):
    blocks, frames, _, cols, _ = own.shape
    channels = blocks * lanes
    pair = 8 * w_in.shape[3]
    return pl.pallas_call(
        edge_kernel,
        out_shape=[
            jax.ShapeDtypeStruct((blocks, frames, 2, cols, lanes), f32),
            jax.ShapeDtypeStruct((4, 6 * pair, channels), bf16),
        ],
        in_specs=[scalars] + [whole] * 5,
        out_specs=[whole] * 2,
        scratch_shapes=[pltpu.VMEM((3, 2, frames + 2, cols, channels), bf16)],
        compiler_params=params(10),
        cost_estimate=pl.CostEstimate(
            flops=2 * 4 * own.size * channels, bytes_accessed=0, transcendentals=0
        ),
        name="edge_part",
    )(places, own, near_rows, far_rows, held, w_in)


def latent_phase(total, slot_of, row_of, spread_row, windows, patches, spread):
    blocks, frames, _, cols, _ = total.shape
    half = cols // 2
    pair = windows.shape[-1]
    for p in range(2):
        for q in range(2):
            top = row_of[p] + p
            window = jnp.concatenate(
                [
                    flat(windows[q, kt : kt + frames, top + a])
                    for kt in range(3)
                    for a in range(2)
                ],
                axis=-1,
            )
            weight = patches[2 * p + q]
            pre = dot(window, weight)
            back = jnp.concatenate(
                [
                    jnp.concatenate(
                        [
                            total[lane, frame, slot_of[p], pl.ds(q, half, stride=2), :]
                            for lane in range(blocks)
                        ],
                        axis=-1,
                    )
                    for frame in range(frames)
                ],
                axis=0,
            )
            gate = jax.nn.sigmoid(pre)
            act_grad = (back * (gate * (1.0 + pre * (1.0 - gate)))).astype(bf16)
            terms = dot_turned(act_grad, weight)
            for kt in range(3):
                for a in range(2):
                    at = (kt * 2 + a) * pair
                    spread[kt : kt + frames, top + a - spread_row, q : q + half] += terms[
                        :, at : at + pair
                    ].reshape(frames, half, pair)


def shares_of(spread, row, half):
    width = spread.shape[-1] // 2
    return spread[:, row, 1 : half + 1, :width] + spread[:, row, 0:half, width:]


def edge_latent_kernel(
    places, total, latent, near_rows, far_rows, patches,
    near_out, far_out, windows, spread, tokens,
):
    even = places[0] != 0
    groups, depth, _, pair = latent.shape
    width = pair // 2
    count = groups * depth * slots * lanes // near_rows.shape[1]
    start = near_rows.shape[0] - count
    half = windows.shape[3]
    block = half // groups
    tokens[...] = jnp.zeros_like(tokens)
    for src in range(groups):
        at = slice(8 + src * block, 8 + (src + 1) * block)
        for frame in range(depth):
            value = latent[src, frame].astype(f32)[:block]
            tokens[frame, 1, at] = value[:, :width]
            tokens[frame, 2, at] = value[:, width:]
            row = (src * depth + frame) * slots
            lane = row // count * lanes
            row = start + row % count
            ends = [
                ref[row : row + slots, lane : lane + lanes].astype(f32)[:block]
                for ref in (near_rows, far_rows)
            ]
            tokens[frame, 0, at] = jnp.where(even, ends[1], ends[0])[:, width:]
            tokens[frame, 3, at] = jnp.where(even, ends[0], ends[1])[:, :width]
    for q in range(2):
        left = tokens[:, :, 7 + q : 7 + q + half]
        right = tokens[:, :, 8 + q : 8 + q + half]
        windows[q] = jnp.concatenate([left, right], axis=-1).astype(bf16)
    spread[...] = jnp.zeros_like(spread)
    latent_phase(total, (0, 1), (0, 1), 0, windows, patches, spread)
    for n, row in enumerate((0, 3)):
        tokens[:, n, 0:half] = shares_of(spread, row, half)
    none = jnp.zeros((block, width), f32)
    fill = jnp.zeros((slots - block, 2 * width), f32)
    for dst in range(groups):
        at = slice(dst * block, (dst + 1) * block)
        for frame in range(depth):
            up = jnp.concatenate([none, tokens[frame, 0, at]], axis=-1)
            down = jnp.concatenate([tokens[frame, 1, at], none], axis=-1)
            padded = lambda v: jnp.concatenate([v, fill], axis=0).astype(bf16)
            near_out[dst, frame] = padded(jnp.where(even, down, up))
            far_out[dst, frame] = padded(jnp.where(even, up, down))


def edge_latent(places, total, latent, near_rows, far_rows, patches):
    groups, depth, _, pair = latent.shape
    cols = total.shape[3]
    out = jax.ShapeDtypeStruct(latent.shape, bf16)
    return pl.pallas_call(
        edge_latent_kernel,
        out_shape=[
            out,
            out,
            jax.ShapeDtypeStruct((2, depth, 4, cols // 2, pair), bf16),
            jax.ShapeDtypeStruct((depth, 4, cols // 2 + 8, pair), f32),
        ],
        in_specs=[scalars] + [whole] * 5,
        out_specs=[whole] * 4,
        scratch_shapes=[pltpu.VMEM((depth, 4, 72, pair // 2), f32)],
        compiler_params=params(10),
        name="edge_latent",
    )(places, total, latent, near_rows, far_rows, patches)


def inner_kernel(own, windows, patches, spread_in, out, spread, tokens):
    half = windows.shape[3]
    groups, depth = out.shape[:2]
    block = half // groups
    spread[...] = spread_in[:, 1:3]
    latent_phase(own, (2, 1), (1, 0), 1, windows, patches, spread)
    for row in range(2):
        tokens[:, row] = shares_of(spread, row, half)
    fill = jnp.zeros((slots - block, out.shape[-1]), f32)
    for dst in range(groups):
        at = slice(dst * block, (dst + 1) * block)
        for frame in range(depth):
            value = jnp.concatenate([tokens[frame, 0, at], tokens[frame, 1, at]], axis=-1)
            out[dst, frame] = jnp.concatenate([value, fill], axis=0)


def inner_part(own, windows, patches, spread, groups):
    cols = own.shape[3]
    depth, _, wide, pair = spread.shape
    return pl.pallas_call(
        inner_kernel,
        out_shape=jax.ShapeDtypeStruct((groups, depth, slots, pair), f32),
        in_specs=[whole] * 4,
        out_specs=whole,
        scratch_shapes=[
            pltpu.VMEM((depth, 2, wide, pair), f32),
            pltpu.VMEM((depth, 2, cols // 2, pair // 2), f32),
        ],
        compiler_params=params(10),
        cost_estimate=pl.CostEstimate(
            flops=8 * own.size * 6 * pair, bytes_accessed=0, transcendentals=own.size
        ),
        name="inner_part",
    )(own, windows, patches, spread)


def weight_kernel(shares, modulated, token_grad, send, field):
    groups, depth, _, pair = shares.shape
    width = pair // 2
    frames, token_rows = modulated.shape[:2]
    model = modulated.shape[-1]
    field[...] = jnp.zeros_like(field)
    for src in range(groups):
        at = src * (frames // groups)
        field[at : at + depth] += shares[src].astype(f32)
    values = field[2 : 2 + frames]
    token_grad[:, 0] = values[:, :, :width].astype(bf16)
    token_grad[:, 1] = values[:, :, width:].astype(bf16)
    turned = jnp.transpose(token_grad[...].reshape(-1, width).astype(f32)).astype(bf16)
    weight = dot(turned, modulated[...].reshape(-1, model))
    half = model // (2 * groups)
    for dst in range(groups):
        at = 2 * half * dst
        stacked = jnp.concatenate(
            [weight[:, at : at + half], weight[:, at + half : at + 2 * half]], axis=0
        )
        send[dst] = jnp.transpose(stacked).astype(bf16)


def weight_terms(shares, modulated):
    groups, depth, _, pair = shares.shape
    frames, token_rows, _, model = modulated.shape
    return pl.pallas_call(
        weight_kernel,
        out_shape=[
            jax.ShapeDtypeStruct((frames, token_rows, slots, pair // 2), bf16),
            jax.ShapeDtypeStruct((groups, model // (2 * groups), pair), bf16),
        ],
        in_specs=[whole] * 2,
        out_specs=[whole] * 2,
        scratch_shapes=[pltpu.VMEM((frames + 2, slots, pair), f32)],
        compiler_params=params(12),
        name="weight_terms",
    )(shares, modulated)


def middle_kernel(got, send):
    total = jnp.sum(got[...].astype(f32), axis=0)
    count, rows, width = send.shape
    total = total.reshape(count // 2, rows, 2 * width).astype(bf16)
    send[0 : count // 2] = total[:, :, :width]
    send[count // 2 :] = total[:, :, width:]


def middle_sum(got, count):
    groups, depth, pair = got.shape
    return pl.pallas_call(
        middle_kernel,
        out_shape=jax.ShapeDtypeStruct((count, 2 * depth // count, pair // 2), bf16),
        in_specs=[whole],
        out_specs=whole,
        compiler_params=params(4),
        name="middle_sum",
    )(got)


def hidden_kernel(hidden, token_grad, scale, w_out, grad_hidden):
    frames, token_rows, tokens, width = hidden.shape
    gain = 1.0 + scale[...]
    block = 3

    def share(step, carry):
        rows = token_grad[pl.ds(step * block, block)].reshape(-1, token_grad.shape[-1])
        mod_grad = dot(rows, w_out[...])
        for frame in range(block):
            for row in range(token_rows):
                at = (frame * token_rows + row) * slots
                scaled = mod_grad[at : at + tokens] * gain
                normed, inverse = normalise(hidden[step * block + frame, row].astype(f32))
                first = jnp.mean(scaled, axis=-1, keepdims=True)
                second = jnp.mean(scaled * normed, axis=-1, keepdims=True)
                value = (scaled - first - normed * second) * inverse
                grad_hidden[step * block + frame, row] = value.astype(bf16)
        return carry

    lax.fori_loop(0, frames // block, share, 0)


def hidden_grad(hidden, token_grad, mod_scale, w_out):
    frames, token_rows, tokens, width = hidden.shape
    return pl.pallas_call(
        hidden_kernel,
        out_shape=jax.ShapeDtypeStruct(hidden.shape, bf16),
        in_specs=[whole] * 4,
        out_specs=whole,
        compiler_params=params(8),
        cost_estimate=pl.CostEstimate(
            flops=2 * frames * 2 * slots * width * w_out.shape[0],
            bytes_accessed=8 * frames * slots * width,
            transcendentals=0,
        ),
        name="hidden_grad",
    )(hidden, token_grad, mod_scale.reshape(1, -1), w_out)


def shards(hidden, mod_scale, mod_shift, w_out, w_in, w_section, section_grad):
    groups, strips = lax.axis_size("tm"), lax.axis_size("height")
    rows = section_grad.shape[1]
    swap = lambda a, b: [(a, b), (b, a)]
    near = sum([swap(i, i + 1) for i in range(0, strips - 1, 2)], [])
    far = sum([swap(i, i + 1) for i in range(1, strips - 1, 2)], [])
    odd = lax.rem(lax.axis_index("height"), 2)
    places = jnp.stack([(1 - odd) * (rows - 1), odd * (rows - 1)]).astype(jnp.int32)
    w_out = jnp.transpose(w_out)

    grad_ahead = lax.ppermute(section_grad, "tm", [(g + 1, g) for g in range(groups - 1)])
    modulated, latent_send = modulate(hidden, mod_scale, mod_shift, w_out, groups)
    latent = lax.all_to_all(latent_send, "tm", 0, 0, tiled=True)
    near_send, far_send = pack_rows(places, section_grad, grad_ahead, latent)
    far_rows = lax.ppermute(far_send, "height", far)
    near_rows = lax.ppermute(near_send, "height", near)
    own, held = own_part(section_grad, grad_ahead, w_section)
    edge, patches = edge_part(places, own, near_rows, far_rows, held, w_in)
    near_share, far_share, windows, spread = edge_latent(
        places, edge, latent, near_rows, far_rows, patches
    )
    far_share = lax.ppermute(far_share, "height", far)
    near_share = lax.ppermute(near_share, "height", near)
    centre = inner_part(own, windows, patches, spread, groups)
    centre = centre + near_share.astype(f32) + far_share.astype(f32)
    shares = lax.all_to_all(centre.astype(bf16), "tm", 0, 0, tiled=True)

    token_grad, send = weight_terms(shares, modulated)
    got = lax.all_to_all(send, "tm", 0, 0, tiled=True)
    grad_hidden = hidden_grad(hidden, token_grad, mod_scale, w_out)
    pieces = lax.all_to_all(middle_sum(got, strips), "height", 0, 0, tiled=True)
    total_tokens = math.prod(hidden.shape[:3]) * groups * strips
    grad_out_weight = jnp.sum(pieces.astype(f32), axis=0) / math.sqrt(total_tokens)
    return (grad_hidden, grad_out_weight)


def solution(mesh):
    placed = (P(None, "height", "tm", None), P(), P(), P(), P(), P(), P("tm", "height", None, None))
    return jax.shard_map(
        shards,
        mesh=mesh,
        in_specs=placed,
        out_specs=(P(None, "height", "tm", None), P(("tm", "height"), None)),
        check_vma=False,
    )
```

```python
import functools
import math

import jax
import jax.numpy as jnp
from jax import lax
from jax.experimental import pallas as pl
from jax.experimental.pallas import tpu as pltpu
from jax.sharding import PartitionSpec as P

epsilon = 1e-05
slots = 16
lanes = 128
f32 = jnp.float32
bf16 = jnp.bfloat16
whole = pl.BlockSpec(memory_space=pltpu.VMEM)
scalars = pl.BlockSpec(memory_space=pltpu.SMEM)
far_off = pl.BlockSpec(memory_space=pltpu.HBM)
early = 1


def params(mib):
    return pltpu.CompilerParams(vmem_limit_bytes=int(mib * 2**20))


def dot(lhs, rhs):
    return jnp.dot(lhs, rhs, preferred_element_type=f32)


def dot_turned(lhs, rhs):
    return lax.dot_general(lhs, rhs, (((1,), (1,)), ((), ())), preferred_element_type=f32)


def normalise(values):
    center = jnp.mean(values, axis=-1, keepdims=True)
    shifted = values - center
    spread = jnp.mean(shifted * shifted, axis=-1, keepdims=True)
    inverse = lax.rsqrt(spread + epsilon)
    return shifted * inverse, inverse


def modulate_kernel(places, hidden, scale, shift, w_out, modulated, *rest):
    pieces, latent = rest[:-1], rest[-1]
    frames, token_rows, tokens, width = hidden.shape
    groups = len(pieces)
    block = frames // groups
    gain = 1.0 + scale[...]
    blank = jnp.zeros((slots - tokens, width), f32)
    latent[0:2] = jnp.zeros_like(latent[0:2])

    def share(step, carry):
        for frame in range(block):
            for row in range(token_rows):
                normed, _ = normalise(hidden[step * block + frame, row].astype(f32))
                value = jnp.concatenate([normed * gain + shift[...], blank], axis=0)
                modulated[step * block + frame, row] = value.astype(bf16)
        value = modulated[pl.ds(step * block, block)].reshape(-1, width)
        value = dot_turned(value, w_out[...]).astype(bf16)
        value = value.reshape(block, token_rows, slots, value.shape[-1])
        paired = jnp.concatenate([value[:, 0], value[:, 1]], axis=-1)
        latent[pl.ds(step * block + 2, block)] = paired
        return carry

    lax.fori_loop(0, groups, share, 0)
    for step, piece in enumerate(pieces):
        dst = lax.rem(places[2] + step, groups)
        piece[...] = latent[pl.ds(dst * block, block + 2)]


def modulate(places, hidden, mod_scale, mod_shift, w_out, groups):
    frames, token_rows, tokens, width = hidden.shape
    pair = 2 * w_out.shape[0]
    piece = jax.ShapeDtypeStruct((frames // groups + 2, slots, pair), bf16)
    return pl.pallas_call(
        modulate_kernel,
        out_shape=[jax.ShapeDtypeStruct((frames, token_rows, slots, width), bf16)]
        + [piece] * groups,
        in_specs=[scalars] + [whole] * 4,
        out_specs=[whole] * (1 + groups),
        scratch_shapes=[pltpu.VMEM((frames + 2, slots, pair), bf16)],
        compiler_params=params(8),
        cost_estimate=pl.CostEstimate(
            flops=2 * frames * slots * width * pair,
            bytes_accessed=8 * frames * slots * width,
            transcendentals=0,
        ),
        name="modulate",
    )(places, hidden, mod_scale.reshape(1, -1), mod_shift.reshape(1, -1), w_out)


def column_shifts(value):
    cols, channels = value.shape
    wide = value.astype(f32)
    place = lax.broadcasted_iota(jnp.int32, (cols, channels), 0)
    nxt = jnp.where(place == cols - 1, 0.0, pltpu.roll(wide, cols - 1, 0))
    prv = jnp.where(place == 0, 0.0, pltpu.roll(wide, 1, 0))
    return nxt.astype(bf16), prv.astype(bf16)


taps = [(2 - n // 3, (1, 0, 2)[n % 3]) for n in range(9)]


def flat(value):
    return value.reshape(-1, value.shape[-1])


def weight_matrix(held_first, held_rest, n):
    block = held_first[n] if n < early else held_rest[n - early]
    return jnp.concatenate([block[kx] for kx in range(3)], axis=-1)


def pack_kernel(
    places, grad, grad_ahead, w_section, w_in, *rest
):
    pieces = rest[:4]
    near, far, latent, shifts, patches, held, sems = rest[4:]
    frames, rows, cols, channels = grad.shape
    groups = len(pieces)
    copies = [
        pltpu.make_async_copy(w_section.at[kt, ky], held.at[n], sems.at[n])
        for n, (kt, ky) in enumerate(taps[:early])
    ]
    for copy in copies:
        copy.start()
    for step, piece in enumerate(pieces):
        latent[lax.rem(places[2] + groups - step, groups)] = piece[...]
    for side, out in ((0, near), (1, far)):
        row = places[side]
        for frame in range(frames + 2):
            at = frame * cols
            value = grad[frame, row] if frame < frames else grad_ahead[frame - frames, row]
            out[at : at + cols] = value
        at = (frames + 2) * cols
        tail = flat(latent[...])
        count = tail.shape[0] * lanes // channels
        for lane in range(channels // lanes):
            out[at : at + count, lane * lanes : (lane + 1) * lanes] = tail[
                lane * count : (lane + 1) * count
            ]
    for frame in range(frames + 2):
        for row in range(rows):
            value = grad[frame, row] if frame < frames else grad_ahead[frame - frames, row]
            shifts[0, frame, row], shifts[1, frame, row] = column_shifts(value)

    patches[...] = jnp.zeros_like(patches)
    lat = w_in.shape[3]
    for n in range(4 * 3 * 2 * 2 * 2 * 2):
        p, q, kt, a, b, pp, qq = [
            n // size % top
            for size, top in ((96, 2), (48, 2), (16, 3), (8, 2), (4, 2), (2, 2), (1, 2))
        ]
        ky, kx = p - 1 + 2 * a + pp, q - 1 + 2 * b + qq
        if 0 <= ky < 3 and 0 <= kx < 3:
            at = (((kt * 2 + a) * 2 + b) * 4 + 2 * pp + qq) * lat
            patches[2 * p + q, at : at + lat] = w_in[kt, ky, kx]
    for copy in copies:
        copy.wait()


def pack_rows(places, grad, grad_ahead, w_section, w_in, pieces):
    frames, rows, cols, channels = grad.shape
    groups = len(pieces)
    latent = jax.ShapeDtypeStruct((groups,) + pieces[0].shape, bf16)
    total = (frames + 2) * cols + latent.size // channels
    return pl.pallas_call(
        pack_kernel,
        in_specs=[scalars, whole, whole, far_off, whole] + [whole] * groups,
        out_specs=[whole] * 6,
        out_shape=[
            jax.ShapeDtypeStruct((total, channels), bf16),
            jax.ShapeDtypeStruct((total, channels), bf16),
            latent,
            jax.ShapeDtypeStruct((2, frames + 2, rows, cols, channels), bf16),
            jax.ShapeDtypeStruct((4, 48 * w_in.shape[3], channels), bf16),
            jax.ShapeDtypeStruct((early,) + w_section.shape[2:], bf16),
        ],
        scratch_shapes=[pltpu.SemaphoreType.DMA((early,))],
        compiler_params=params(8),
        name="pack_rows",
    )(places, grad, grad_ahead, w_section, w_in, *pieces)


def own_kernel(grad, grad_ahead, shifts, w_section, held_first, total, held_rest, sems):
    frames, rows, cols, channels = grad.shape
    copies = [
        pltpu.make_async_copy(w_section.at[kt, ky], held_rest.at[n], sems.at[n])
        for n, (kt, ky) in enumerate(taps[early:])
    ]
    for copy in copies:
        copy.start()
    for n, (kt, ky) in enumerate(taps):
        lo, hi = max(0, ky - 1), rows + min(0, ky - 1)
        at = slice(lo + 1 - ky, hi + 1 - ky)
        src = slice(2 - kt, frames + 2 - kt), at
        centre = flat(grad[2 - kt :, at])
        if kt < 2:
            centre = jnp.concatenate([centre, flat(grad_ahead[: 2 - kt, at])], axis=0)
        window = jnp.concatenate(
            [flat(shifts[(0,) + src]), centre, flat(shifts[(1,) + src])], axis=-1
        )
        if n >= early:
            copies[n - early].wait()
        part = dot_turned(window, weight_matrix(held_first, held_rest, n))
        for lane in range(channels // lanes):
            value = part[:, lane * lanes : (lane + 1) * lanes]
            value = value.reshape(frames, hi - lo, cols, lanes)
            if n == 0:
                total[lane] = value
            else:
                total[lane, :, lo:hi] += value


def own_part(grad, grad_ahead, shifts, w_section, held_first):
    frames, rows, cols, channels = grad.shape
    return pl.pallas_call(
        own_kernel,
        out_shape=[
            jax.ShapeDtypeStruct((channels // lanes, frames, rows, cols, lanes), f32),
            jax.ShapeDtypeStruct((len(taps) - early,) + w_section.shape[2:], bf16),
        ],
        in_specs=[whole, whole, whole, far_off, whole],
        out_specs=[whole] * 2,
        scratch_shapes=[pltpu.SemaphoreType.DMA((len(taps) - early,))],
        compiler_params=params(12),
        cost_estimate=pl.CostEstimate(
            flops=2 * 24 * grad.size * channels,
            bytes_accessed=2 * w_section.size,
            transcendentals=0,
        ),
        name="own_part",
    )(grad, grad_ahead, shifts, w_section, held_first)


def edge_kernel(places, own, near_rows, far_rows, held_first, held_rest, total, near):
    even = places[0] != 0
    blocks, frames, rows, cols, _ = own.shape
    for lane in range(blocks):
        total[lane, :, 0] = own[lane, :, 0]
        total[lane, :, 1] = own[lane, :, rows - 1]
    for frame in range(frames + 2):
        at = slice(frame * cols, (frame + 1) * cols)
        ends = near_rows[at], far_rows[at]
        for side in range(2):
            value = jnp.where(even == (side == 1), ends[0], ends[1])
            near[1, side, frame] = value
            near[0, side, frame], near[2, side, frame] = column_shifts(value)

    for n, (kt, ky) in enumerate(taps):
        if ky == 1:
            continue
        side = 0 if ky == 2 else 1
        window = jnp.concatenate(
            [flat(near[kx, side, 2 - kt : frames + 2 - kt]) for kx in range(3)], axis=-1
        )
        part = dot_turned(window, weight_matrix(held_first, held_rest, n))
        for lane in range(blocks):
            value = part[:, lane * lanes : (lane + 1) * lanes]
            total[lane, :, side] += value.reshape(frames, cols, lanes)


def edge_part(places, own, near_rows, far_rows, held_first, held_rest):
    blocks, frames, _, cols, _ = own.shape
    channels = blocks * lanes
    return pl.pallas_call(
        edge_kernel,
        out_shape=jax.ShapeDtypeStruct((blocks, frames, 2, cols, lanes), f32),
        in_specs=[scalars] + [whole] * 5,
        out_specs=whole,
        scratch_shapes=[pltpu.VMEM((3, 2, frames + 2, cols, channels), bf16)],
        compiler_params=params(10),
        cost_estimate=pl.CostEstimate(
            flops=2 * 4 * own.size * channels, bytes_accessed=0, transcendentals=0
        ),
        name="edge_part",
    )(places, own, near_rows, far_rows, held_first, held_rest)


def latent_phase(total, slot_of, row_of, spread_row, windows, patches, spread):
    blocks, frames, _, cols, _ = total.shape
    half = cols // 2
    pair = windows.shape[-1]
    for p in range(2):
        for q in range(2):
            top = row_of[p] + p
            window = jnp.concatenate(
                [
                    flat(windows[q, kt : kt + frames, top + a])
                    for kt in range(3)
                    for a in range(2)
                ],
                axis=-1,
            )
            weight = patches[2 * p + q]
            pre = dot(window, weight)
            back = jnp.concatenate(
                [
                    jnp.concatenate(
                        [
                            total[lane, frame, slot_of[p], pl.ds(q, half, stride=2), :]
                            for lane in range(blocks)
                        ],
                        axis=-1,
                    )
                    for frame in range(frames)
                ],
                axis=0,
            )
            gate = jax.nn.sigmoid(pre)
            act_grad = (back * (gate * (1.0 + pre * (1.0 - gate)))).astype(bf16)
            terms = dot_turned(act_grad, weight)
            for kt in range(3):
                for a in range(2):
                    at = (kt * 2 + a) * pair
                    spread[kt : kt + frames, top + a - spread_row, q : q + half] += terms[
                        :, at : at + pair
                    ].reshape(frames, half, pair)


def shares_of(spread, row, half):
    width = spread.shape[-1] // 2
    return spread[:, row, 1 : half + 1, :width] + spread[:, row, 0:half, width:]


def edge_latent_kernel(
    places, total, latent, near_rows, far_rows, patches,
    near_out, far_out, windows, spread, tokens,
):
    even = places[0] != 0
    groups, depth, _, pair = latent.shape
    width = pair // 2
    count = groups * depth * slots * lanes // near_rows.shape[1]
    start = near_rows.shape[0] - count
    half = windows.shape[3]
    block = half // groups
    tokens[...] = jnp.zeros_like(tokens)
    for src in range(groups):
        at = slice(8 + src * block, 8 + (src + 1) * block)
        for frame in range(depth):
            value = latent[src, frame].astype(f32)[:block]
            tokens[frame, 1, at] = value[:, :width]
            tokens[frame, 2, at] = value[:, width:]
            row = (src * depth + frame) * slots
            lane = row // count * lanes
            row = start + row % count
            ends = [
                ref[row : row + slots, lane : lane + lanes].astype(f32)[:block]
                for ref in (near_rows, far_rows)
            ]
            tokens[frame, 0, at] = jnp.where(even, ends[1], ends[0])[:, width:]
            tokens[frame, 3, at] = jnp.where(even, ends[0], ends[1])[:, :width]
    for q in range(2):
        left = tokens[:, :, 7 + q : 7 + q + half]
        right = tokens[:, :, 8 + q : 8 + q + half]
        windows[q] = jnp.concatenate([left, right], axis=-1).astype(bf16)
    spread[...] = jnp.zeros_like(spread)
    latent_phase(total, (0, 1), (0, 1), 0, windows, patches, spread)
    for n, row in enumerate((0, 3)):
        tokens[:, n, 0:half] = shares_of(spread, row, half)
    none = jnp.zeros((block, width), f32)
    fill = jnp.zeros((slots - block, 2 * width), f32)
    for dst in range(groups):
        at = slice(dst * block, (dst + 1) * block)
        for frame in range(depth):
            up = jnp.concatenate([none, tokens[frame, 0, at]], axis=-1)
            down = jnp.concatenate([tokens[frame, 1, at], none], axis=-1)
            padded = lambda v: jnp.concatenate([v, fill], axis=0).astype(bf16)
            near_out[dst, frame] = padded(jnp.where(even, down, up))
            far_out[dst, frame] = padded(jnp.where(even, up, down))


def edge_latent(places, total, latent, near_rows, far_rows, patches):
    groups, depth, _, pair = latent.shape
    cols = total.shape[3]
    out = jax.ShapeDtypeStruct(latent.shape, bf16)
    return pl.pallas_call(
        edge_latent_kernel,
        out_shape=[
            out,
            out,
            jax.ShapeDtypeStruct((2, depth, 4, cols // 2, pair), bf16),
            jax.ShapeDtypeStruct((depth, 4, cols // 2 + 8, pair), f32),
        ],
        in_specs=[scalars] + [whole] * 5,
        out_specs=[whole] * 4,
        scratch_shapes=[pltpu.VMEM((depth, 4, 72, pair // 2), f32)],
        compiler_params=params(10),
        name="edge_latent",
    )(places, total, latent, near_rows, far_rows, patches)


def inner_kernel(own, windows, patches, spread_in, out, spread, tokens):
    half = windows.shape[3]
    groups, depth = out.shape[:2]
    block = half // groups
    spread[...] = spread_in[:, 1:3]
    latent_phase(own, (2, 1), (1, 0), 1, windows, patches, spread)
    for row in range(2):
        tokens[:, row] = shares_of(spread, row, half)
    fill = jnp.zeros((slots - block, out.shape[-1]), f32)
    for dst in range(groups):
        at = slice(dst * block, (dst + 1) * block)
        for frame in range(depth):
            value = jnp.concatenate([tokens[frame, 0, at], tokens[frame, 1, at]], axis=-1)
            out[dst, frame] = jnp.concatenate([value, fill], axis=0)


def inner_part(own, windows, patches, spread, groups):
    cols = own.shape[3]
    depth, _, wide, pair = spread.shape
    return pl.pallas_call(
        inner_kernel,
        out_shape=jax.ShapeDtypeStruct((groups, depth, slots, pair), f32),
        in_specs=[whole] * 4,
        out_specs=whole,
        scratch_shapes=[
            pltpu.VMEM((depth, 2, wide, pair), f32),
            pltpu.VMEM((depth, 2, cols // 2, pair // 2), f32),
        ],
        compiler_params=params(10),
        cost_estimate=pl.CostEstimate(
            flops=8 * own.size * 6 * pair, bytes_accessed=0, transcendentals=own.size
        ),
        name="inner_part",
    )(own, windows, patches, spread)


def share_kernel(places, centre, near_share, far_share, *pieces):
    groups = len(pieces)
    for step, piece in enumerate(pieces):
        dst = lax.rem(places[2] + step, groups)
        value = centre[dst] + near_share[dst].astype(f32) + far_share[dst].astype(f32)
        piece[...] = value.astype(bf16)


def share_pieces(places, centre, near_share, far_share):
    groups = centre.shape[0]
    return pl.pallas_call(
        share_kernel,
        out_shape=[jax.ShapeDtypeStruct(centre.shape[1:], bf16)] * groups,
        in_specs=[scalars] + [whole] * 3,
        out_specs=[whole] * groups,
        compiler_params=params(4),
        name="share_pieces",
    )(places, centre, near_share, far_share)


def weight_kernel(places, modulated, *rest):
    shares, token_grad, pieces, (field, weight) = rest[:4], rest[4], rest[5:9], rest[9:]
    groups = len(shares)
    depth, _, pair = shares[0].shape
    width = pair // 2
    frames = modulated.shape[0]
    model = modulated.shape[-1]
    field[...] = jnp.zeros_like(field)
    for step, share in enumerate(shares):
        src = lax.rem(places[2] + groups - step, groups)
        field[pl.ds(src * (frames // groups), depth)] += share[...].astype(f32)
    values = field[2 : 2 + frames]
    token_grad[:, 0] = values[:, :, :width].astype(bf16)
    token_grad[:, 1] = values[:, :, width:].astype(bf16)
    turned = jnp.transpose(token_grad[...].reshape(-1, width).astype(f32)).astype(bf16)
    total = dot(turned, modulated[...].reshape(-1, model))
    half = model // (2 * groups)
    for dst in range(groups):
        at = 2 * half * dst
        weight[dst, :width] = total[:, at : at + half]
        weight[dst, width:] = total[:, at + half : at + 2 * half]
    for step, piece in enumerate(pieces):
        dst = lax.rem(places[2] + step, groups)
        piece[...] = jnp.transpose(weight[dst]).astype(bf16)


def weight_terms(places, modulated, shares):
    groups = len(shares)
    depth, _, pair = shares[0].shape
    frames, token_rows, _, model = modulated.shape
    half = model // (2 * groups)
    return pl.pallas_call(
        weight_kernel,
        out_shape=[jax.ShapeDtypeStruct((frames, token_rows, slots, pair // 2), bf16)]
        + [jax.ShapeDtypeStruct((half, pair), bf16)] * groups,
        in_specs=[scalars] + [whole] * (1 + groups),
        out_specs=[whole] * (1 + groups),
        scratch_shapes=[
            pltpu.VMEM((frames + 2, slots, pair), f32),
            pltpu.VMEM((groups, pair, half), f32),
        ],
        compiler_params=params(12),
        name="weight_terms",
    )(places, modulated, *shares)


def middle_kernel(*refs):
    send = refs[-1]
    total = sum(ref[...].astype(f32) for ref in refs[:-1])
    count, rows, width = send.shape
    total = total.reshape(count // 2, rows, 2 * width).astype(bf16)
    send[0 : count // 2] = total[:, :, :width]
    send[count // 2 :] = total[:, :, width:]


def middle_sum(got, count):
    depth, pair = got[0].shape
    return pl.pallas_call(
        middle_kernel,
        out_shape=jax.ShapeDtypeStruct((count, 2 * depth // count, pair // 2), bf16),
        in_specs=[whole] * len(got),
        out_specs=whole,
        compiler_params=params(4),
        name="middle_sum",
    )(*got)


def hidden_kernel(hidden, token_grad, scale, w_out, grad_hidden):
    frames, token_rows, tokens, width = hidden.shape
    gain = 1.0 + scale[...]
    block = 3

    def share(step, carry):
        rows = token_grad[pl.ds(step * block, block)].reshape(-1, token_grad.shape[-1])
        mod_grad = dot(rows, w_out[...])
        for frame in range(block):
            for row in range(token_rows):
                at = (frame * token_rows + row) * slots
                scaled = mod_grad[at : at + tokens] * gain
                normed, inverse = normalise(hidden[step * block + frame, row].astype(f32))
                first = jnp.mean(scaled, axis=-1, keepdims=True)
                second = jnp.mean(scaled * normed, axis=-1, keepdims=True)
                value = (scaled - first - normed * second) * inverse
                grad_hidden[step * block + frame, row] = value.astype(bf16)
        return carry

    lax.fori_loop(0, frames // block, share, 0)


def hidden_grad(hidden, token_grad, mod_scale, w_out):
    frames, token_rows, tokens, width = hidden.shape
    return pl.pallas_call(
        hidden_kernel,
        out_shape=jax.ShapeDtypeStruct(hidden.shape, bf16),
        in_specs=[whole] * 4,
        out_specs=whole,
        compiler_params=params(8),
        cost_estimate=pl.CostEstimate(
            flops=2 * frames * 2 * slots * width * w_out.shape[0],
            bytes_accessed=8 * frames * slots * width,
            transcendentals=0,
        ),
        name="hidden_grad",
    )(hidden, token_grad, mod_scale.reshape(1, -1), w_out)


def shards(hidden, mod_scale, mod_shift, w_out, w_in, w_section, section_grad):
    groups, strips = lax.axis_size("tm"), lax.axis_size("height")
    rows = section_grad.shape[1]
    swap = lambda a, b: [(a, b), (b, a)]
    near = sum([swap(i, i + 1) for i in range(0, strips - 1, 2)], [])
    far = sum([swap(i, i + 1) for i in range(1, strips - 1, 2)], [])
    odd = lax.rem(lax.axis_index("height"), 2)
    places = jnp.stack([(1 - odd) * (rows - 1), odd * (rows - 1), lax.axis_index("tm")])
    places = places.astype(jnp.int32)
    w_out = jnp.transpose(w_out)
    w_section = pltpu.with_memory_space_constraint(w_section, pltpu.HBM)

    def round_tm(pieces):
        hops = lambda k: [(g, (g + k) % groups) for g in range(groups)]
        return [pieces[0]] + [
            lax.ppermute(pieces[k], "tm", hops(k)) for k in range(1, groups)
        ]

    grad_ahead = lax.ppermute(section_grad, "tm", [(g + 1, g) for g in range(groups - 1)])
    modulated, *pieces = modulate(places, hidden, mod_scale, mod_shift, w_out, groups)
    near_send, far_send, latent, shifts, patches, held_first = pack_rows(
        places, section_grad, grad_ahead, w_section, w_in, round_tm(pieces)
    )
    far_rows = lax.ppermute(far_send, "height", far)
    near_rows = lax.ppermute(near_send, "height", near)
    own, held_rest = own_part(section_grad, grad_ahead, shifts, w_section, held_first)
    edge = edge_part(places, own, near_rows, far_rows, held_first, held_rest)
    near_share, far_share, windows, spread = edge_latent(
        places, edge, latent, near_rows, far_rows, patches
    )
    far_share = lax.ppermute(far_share, "height", far)
    near_share = lax.ppermute(near_share, "height", near)
    centre = inner_part(own, windows, patches, spread, groups)
    shares = round_tm(share_pieces(places, centre, near_share, far_share))
    token_grad, *pieces = weight_terms(places, modulated, shares)
    got = round_tm(pieces)
    grad_hidden = hidden_grad(hidden, token_grad, mod_scale, w_out)
    pieces = lax.all_to_all(middle_sum(got, strips), "height", 0, 0, tiled=True)
    total_tokens = math.prod(hidden.shape[:3]) * groups * strips
    grad_out_weight = jnp.sum(pieces.astype(f32), axis=0) / math.sqrt(total_tokens)
    return (grad_hidden, grad_out_weight)


def solution(mesh):
    placed = (P(None, "height", "tm", None), P(), P(), P(), P(), P(), P("tm", "height", None, None))
    return jax.shard_map(
        shards,
        mesh=mesh,
        in_specs=placed,
        out_specs=(P(None, "height", "tm", None), P(("tm", "height"), None)),
        check_vma=False,
    )
```

```python
import functools
import math

import jax
import jax.numpy as jnp
from jax import lax
from jax.experimental import pallas as pl
from jax.experimental.pallas import tpu as pltpu
from jax.sharding import PartitionSpec as P

epsilon = 1e-05
slots = 16
lanes = 128
f32 = jnp.float32
bf16 = jnp.bfloat16
whole = pl.BlockSpec(memory_space=pltpu.VMEM)
scalars = pl.BlockSpec(memory_space=pltpu.SMEM)
far_off = pl.BlockSpec(memory_space=pltpu.HBM)
early = 2
taps = [(2 - n // 3, (1, 0, 2)[n % 3]) for n in range(9)]


def params(mib):
    return pltpu.CompilerParams(vmem_limit_bytes=int(mib * 2**20))


def dot(lhs, rhs):
    return jnp.dot(lhs, rhs, preferred_element_type=f32)


def dot_turned(lhs, rhs):
    return lax.dot_general(lhs, rhs, (((1,), (1,)), ((), ())), preferred_element_type=f32)


def normalise(values):
    center = jnp.mean(values, axis=-1, keepdims=True)
    shifted = values - center
    spread = jnp.mean(shifted * shifted, axis=-1, keepdims=True)
    inverse = lax.rsqrt(spread + epsilon)
    return shifted * inverse, inverse


def fetch_kernel(grad, ahead, sem):
    copy = pltpu.make_async_copy(grad.at[0:2], ahead, sem)
    copy.start()
    copy.wait()


def fetch(grad):
    return pl.pallas_call(
        fetch_kernel,
        out_shape=jax.ShapeDtypeStruct((2,) + grad.shape[1:], bf16),
        in_specs=[far_off],
        out_specs=whole,
        scratch_shapes=[pltpu.SemaphoreType.DMA],
        compiler_params=params(4),
        name="fetch",
    )(grad)


def wide_weight(w_section):
    return w_section.shape[-2], 3 * w_section.shape[-1]


def weight_copies(w_section, held, some, sems):
    channels = w_section.shape[-1]
    return [
        [
            pltpu.make_async_copy(
                w_section.at[kt, ky, kx],
                held.at[n, :, kx * channels : (kx + 1) * channels],
                sems.at[3 * n + kx],
            )
            for kx in range(3)
        ]
        for n, (kt, ky) in enumerate(some)
    ]


def modulate_kernel(places, hidden, scale, shift, w_out, w_section, modulated, held, *rest):
    pieces, latent, sems = rest[:-2], rest[-2], rest[-1]
    copies = sum(weight_copies(w_section, held, taps[:early], sems), [])
    for copy in copies:
        copy.start()
    frames, token_rows, tokens, width = hidden.shape
    groups = len(pieces)
    block = frames // groups
    gain = 1.0 + scale[...]
    blank = jnp.zeros((slots - tokens, width), f32)
    latent[0:2] = jnp.zeros_like(latent[0:2])

    def share(step, carry):
        for frame in range(block):
            for row in range(token_rows):
                normed, _ = normalise(hidden[step * block + frame, row].astype(f32))
                value = jnp.concatenate([normed * gain + shift[...], blank], axis=0)
                modulated[step * block + frame, row] = value.astype(bf16)
        value = modulated[pl.ds(step * block, block)].reshape(-1, width)
        value = dot_turned(value, w_out[...]).astype(bf16)
        value = value.reshape(block, token_rows, slots, value.shape[-1])
        paired = jnp.concatenate([value[:, 0], value[:, 1]], axis=-1)
        latent[pl.ds(step * block + 2, block)] = paired
        return carry

    lax.fori_loop(0, groups, share, 0)
    for step, piece in enumerate(pieces):
        dst = lax.rem(places[2] + step, groups)
        piece[...] = latent[pl.ds(dst * block, block + 2)]
    for copy in copies:
        copy.wait()


def modulate(places, hidden, mod_scale, mod_shift, w_out, w_section, groups):
    frames, token_rows, tokens, width = hidden.shape
    pair = 2 * w_out.shape[0]
    piece = jax.ShapeDtypeStruct((frames // groups + 2, slots, pair), bf16)
    return pl.pallas_call(
        modulate_kernel,
        out_shape=[
            jax.ShapeDtypeStruct((frames, token_rows, slots, width), bf16),
            jax.ShapeDtypeStruct((early,) + wide_weight(w_section), bf16),
        ]
        + [piece] * groups,
        in_specs=[scalars] + [whole] * 4 + [far_off],
        out_specs=[whole] * (2 + groups),
        scratch_shapes=[
            pltpu.VMEM((frames + 2, slots, pair), bf16),
            pltpu.SemaphoreType.DMA((3 * early,)),
        ],
        compiler_params=params(8),
        cost_estimate=pl.CostEstimate(
            flops=2 * frames * slots * width * pair,
            bytes_accessed=8 * frames * slots * width,
            transcendentals=0,
        ),
        name="modulate",
    )(places, hidden, mod_scale.reshape(1, -1), mod_shift.reshape(1, -1), w_out, w_section)


def widened(value):
    cols, channels = value.shape
    wide = value.astype(f32)
    place = lax.broadcasted_iota(jnp.int32, (cols, channels), 0)
    right = jnp.where(place == cols - 1, 0.0, pltpu.roll(wide, cols - 1, 0)).astype(bf16)
    left = jnp.where(place == 0, 0.0, pltpu.roll(wide, 1, 0)).astype(bf16)
    return jnp.concatenate([right, value, left], axis=-1)


def flat(value):
    return value.reshape(-1, value.shape[-1])


def weight_matrix(held_first, held_rest, n):
    return held_first[n] if n < early else held_rest[n - early]


def pack_kernel(places, grad, grad_ahead, w_in, *rest):
    pieces = rest[:4]
    near, far, latent, wide, patches = rest[4:]
    frames, rows, cols, channels = grad.shape
    groups = len(pieces)
    for step, piece in enumerate(pieces):
        latent[lax.rem(places[2] + groups - step, groups)] = piece[...]
    for side, out in ((0, near), (1, far)):
        row = places[side]
        for frame in range(frames + 2):
            at = frame * cols
            value = grad[frame, row] if frame < frames else grad_ahead[frame - frames, row]
            out[at : at + cols] = value
        at = (frames + 2) * cols
        tail = flat(latent[...])
        count = tail.shape[0] * lanes // channels
        for lane in range(channels // lanes):
            out[at : at + count, lane * lanes : (lane + 1) * lanes] = tail[
                lane * count : (lane + 1) * count
            ]
    for frame in range(frames + 2):
        for row in range(rows):
            value = grad[frame, row] if frame < frames else grad_ahead[frame - frames, row]
            wide[frame, row] = widened(value)

    patches[...] = jnp.zeros_like(patches)
    lat = w_in.shape[3]
    for n in range(4 * 3 * 2 * 2 * 2 * 2):
        p, q, kt, a, b, pp, qq = [
            n // size % top
            for size, top in ((96, 2), (48, 2), (16, 3), (8, 2), (4, 2), (2, 2), (1, 2))
        ]
        ky, kx = p - 1 + 2 * a + pp, q - 1 + 2 * b + qq
        if 0 <= ky < 3 and 0 <= kx < 3:
            at = (((kt * 2 + a) * 2 + b) * 4 + 2 * pp + qq) * lat
            patches[2 * p + q, at : at + lat] = w_in[kt, ky, kx]


def pack_rows(places, grad, grad_ahead, w_in, pieces):
    frames, rows, cols, channels = grad.shape
    groups = len(pieces)
    latent = jax.ShapeDtypeStruct((groups,) + pieces[0].shape, bf16)
    total = (frames + 2) * cols + latent.size // channels
    return pl.pallas_call(
        pack_kernel,
        in_specs=[scalars] + [whole] * (3 + groups),
        out_specs=[whole] * 5,
        out_shape=[
            jax.ShapeDtypeStruct((total, channels), bf16),
            jax.ShapeDtypeStruct((total, channels), bf16),
            latent,
            jax.ShapeDtypeStruct((frames + 2, rows, cols, 3 * channels), bf16),
            jax.ShapeDtypeStruct((4, 48 * w_in.shape[3], channels), bf16),
        ],
        compiler_params=params(8),
        name="pack_rows",
    )(places, grad, grad_ahead, w_in, *pieces)


def own_kernel(wide, w_section, held_first, total, held_rest, sems):
    depth, rows, cols, _ = wide.shape
    frames = depth - 2
    copies = weight_copies(w_section, held_rest, taps[early:], sems)
    for copy in sum(copies, []):
        copy.start()
    for n, (kt, ky) in enumerate(taps):
        lo, hi = max(0, ky - 1), rows + min(0, ky - 1)
        window = flat(wide[2 - kt : depth - kt, lo + 1 - ky : hi + 1 - ky])
        if n >= early:
            for copy in copies[n - early]:
                copy.wait()
        part = dot_turned(window, weight_matrix(held_first, held_rest, n))
        for lane in range(total.shape[0]):
            value = part[:, lane * lanes : (lane + 1) * lanes]
            value = value.reshape(frames, hi - lo, cols, lanes)
            if n == 0:
                total[lane] = value
            else:
                total[lane, :, lo:hi] += value


def own_part(wide, w_section, held_first):
    depth, rows, cols, _ = wide.shape
    channels = w_section.shape[-1]
    return pl.pallas_call(
        own_kernel,
        out_shape=[
            jax.ShapeDtypeStruct((channels // lanes, depth - 2, rows, cols, lanes), f32),
            jax.ShapeDtypeStruct((len(taps) - early,) + wide_weight(w_section), bf16),
        ],
        in_specs=[whole, far_off, whole],
        out_specs=[whole] * 2,
        scratch_shapes=[pltpu.SemaphoreType.DMA((3 * (len(taps) - early),))],
        compiler_params=params(12),
        cost_estimate=pl.CostEstimate(
            flops=2 * 14 * wide.size * channels,
            bytes_accessed=2 * w_section.size,
            transcendentals=0,
        ),
        name="own_part",
    )(wide, w_section, held_first)


def edge_conv(even, own, near_rows, far_rows, held_first, held_rest, total, wide):
    blocks, frames, rows, cols, _ = own.shape
    for lane in range(blocks):
        total[lane, :, 0] = own[lane, :, 0]
        total[lane, :, 1] = own[lane, :, rows - 1]
    for frame in range(frames + 2):
        at = slice(frame * cols, (frame + 1) * cols)
        ends = near_rows[at], far_rows[at]
        for side in range(2):
            wide[side, frame] = widened(jnp.where(even == (side == 1), ends[0], ends[1]))
    for n, (kt, ky) in enumerate(taps):
        if ky == 1:
            continue
        side = 0 if ky == 2 else 1
        window = flat(wide[side, 2 - kt : frames + 2 - kt])
        part = dot_turned(window, weight_matrix(held_first, held_rest, n))
        for lane in range(blocks):
            value = part[:, lane * lanes : (lane + 1) * lanes]
            total[lane, :, side] += value.reshape(frames, cols, lanes)


def latent_phase(total, slot_of, row_of, spread_row, windows, patches, spread):
    blocks, frames, _, cols, _ = total.shape
    half = cols // 2
    pair = windows.shape[-1]
    for p in range(2):
        for q in range(2):
            top = row_of[p] + p
            window = jnp.concatenate(
                [
                    flat(windows[q, kt : kt + frames, top + a])
                    for kt in range(3)
                    for a in range(2)
                ],
                axis=-1,
            )
            weight = patches[2 * p + q]
            pre = dot(window, weight)
            back = jnp.concatenate(
                [
                    jnp.concatenate(
                        [
                            total[lane, frame, slot_of[p], pl.ds(q, half, stride=2), :]
                            for lane in range(blocks)
                        ],
                        axis=-1,
                    )
                    for frame in range(frames)
                ],
                axis=0,
            )
            gate = jax.nn.sigmoid(pre)
            act_grad = (back * (gate * (1.0 + pre * (1.0 - gate)))).astype(bf16)
            terms = dot_turned(act_grad, weight)
            for kt in range(3):
                for a in range(2):
                    at = (kt * 2 + a) * pair
                    spread[kt : kt + frames, top + a - spread_row, q : q + half] += terms[
                        :, at : at + pair
                    ].reshape(frames, half, pair)


def shares_of(spread, row, half):
    width = spread.shape[-1] // 2
    return spread[:, row, 1 : half + 1, :width] + spread[:, row, 0:half, width:]


def edge_kernel(
    places, own, latent, near_rows, far_rows, held_first, held_rest, patches,
    near_out, far_out, windows, spread, tokens, total, wide,
):
    even = places[0] != 0
    edge_conv(even, own, near_rows, far_rows, held_first, held_rest, total, wide)
    groups, depth, _, pair = latent.shape
    width = pair // 2
    count = groups * depth * slots * lanes // near_rows.shape[1]
    start = near_rows.shape[0] - count
    half = windows.shape[3]
    block = half // groups
    tokens[...] = jnp.zeros_like(tokens)
    for src in range(groups):
        at = slice(8 + src * block, 8 + (src + 1) * block)
        for frame in range(depth):
            value = latent[src, frame].astype(f32)[:block]
            tokens[frame, 1, at] = value[:, :width]
            tokens[frame, 2, at] = value[:, width:]
            row = (src * depth + frame) * slots
            lane = row // count * lanes
            row = start + row % count
            ends = [
                ref[row : row + slots, lane : lane + lanes].astype(f32)[:block]
                for ref in (near_rows, far_rows)
            ]
            tokens[frame, 0, at] = jnp.where(even, ends[1], ends[0])[:, width:]
            tokens[frame, 3, at] = jnp.where(even, ends[0], ends[1])[:, :width]
    for q in range(2):
        left = tokens[:, :, 7 + q : 7 + q + half]
        right = tokens[:, :, 8 + q : 8 + q + half]
        windows[q] = jnp.concatenate([left, right], axis=-1).astype(bf16)
    spread[...] = jnp.zeros_like(spread)
    latent_phase(total, (0, 1), (0, 1), 0, windows, patches, spread)
    for n, row in enumerate((0, 3)):
        tokens[:, n, 0:half] = shares_of(spread, row, half)
    none = jnp.zeros((block, width), f32)
    fill = jnp.zeros((slots - block, 2 * width), f32)
    for dst in range(groups):
        at = slice(dst * block, (dst + 1) * block)
        for frame in range(depth):
            up = jnp.concatenate([none, tokens[frame, 0, at]], axis=-1)
            down = jnp.concatenate([tokens[frame, 1, at], none], axis=-1)
            padded = lambda v: jnp.concatenate([v, fill], axis=0).astype(bf16)
            near_out[dst, frame] = padded(jnp.where(even, down, up))
            far_out[dst, frame] = padded(jnp.where(even, up, down))


def edge_part(places, own, latent, near_rows, far_rows, held_first, held_rest, patches):
    groups, depth, _, pair = latent.shape
    blocks, frames, _, cols, _ = own.shape
    out = jax.ShapeDtypeStruct(latent.shape, bf16)
    return pl.pallas_call(
        edge_kernel,
        out_shape=[
            out,
            out,
            jax.ShapeDtypeStruct((2, depth, 4, cols // 2, pair), bf16),
            jax.ShapeDtypeStruct((depth, 4, cols // 2 + 8, pair), f32),
        ],
        in_specs=[scalars] + [whole] * 7,
        out_specs=[whole] * 4,
        scratch_shapes=[
            pltpu.VMEM((depth, 4, 72, pair // 2), f32),
            pltpu.VMEM((blocks, frames, 2, cols, lanes), f32),
            pltpu.VMEM((2, depth, cols, 3 * blocks * lanes), bf16),
        ],
        compiler_params=params(14),
        cost_estimate=pl.CostEstimate(
            flops=2 * 6 * own.size * blocks * lanes, bytes_accessed=0, transcendentals=own.size
        ),
        name="edge_part",
    )(places, own, latent, near_rows, far_rows, held_first, held_rest, patches)


def inner_kernel(own, windows, patches, spread_in, out, spread, tokens):
    half = windows.shape[3]
    groups, depth = out.shape[:2]
    block = half // groups
    spread[...] = spread_in[:, 1:3]
    latent_phase(own, (2, 1), (1, 0), 1, windows, patches, spread)
    for row in range(2):
        tokens[:, row] = shares_of(spread, row, half)
    fill = jnp.zeros((slots - block, out.shape[-1]), f32)
    for dst in range(groups):
        at = slice(dst * block, (dst + 1) * block)
        for frame in range(depth):
            value = jnp.concatenate([tokens[frame, 0, at], tokens[frame, 1, at]], axis=-1)
            out[dst, frame] = jnp.concatenate([value, fill], axis=0)


def inner_part(own, windows, patches, spread, groups):
    cols = own.shape[3]
    depth, _, wide, pair = spread.shape
    return pl.pallas_call(
        inner_kernel,
        out_shape=jax.ShapeDtypeStruct((groups, depth, slots, pair), f32),
        in_specs=[whole] * 4,
        out_specs=whole,
        scratch_shapes=[
            pltpu.VMEM((depth, 2, wide, pair), f32),
            pltpu.VMEM((depth, 2, cols // 2, pair // 2), f32),
        ],
        compiler_params=params(10),
        cost_estimate=pl.CostEstimate(
            flops=8 * own.size * 6 * pair, bytes_accessed=0, transcendentals=own.size
        ),
        name="inner_part",
    )(own, windows, patches, spread)


def share_kernel(places, centre, near_share, far_share, *pieces):
    groups = len(pieces)
    for step, piece in enumerate(pieces):
        dst = lax.rem(places[2] + step, groups)
        value = centre[dst] + near_share[dst].astype(f32) + far_share[dst].astype(f32)
        piece[...] = value.astype(bf16)


def share_pieces(places, centre, near_share, far_share):
    groups = centre.shape[0]
    return pl.pallas_call(
        share_kernel,
        out_shape=[jax.ShapeDtypeStruct(centre.shape[1:], bf16)] * groups,
        in_specs=[scalars] + [whole] * 3,
        out_specs=[whole] * groups,
        compiler_params=params(4),
        name="share_pieces",
    )(places, centre, near_share, far_share)


def weight_kernel(places, modulated, *rest):
    shares, token_grad, pieces, (field, weight) = rest[:4], rest[4], rest[5:9], rest[9:]
    groups = len(shares)
    depth, _, pair = shares[0].shape
    width = pair // 2
    frames = modulated.shape[0]
    model = modulated.shape[-1]
    field[...] = jnp.zeros_like(field)
    for step, share in enumerate(shares):
        src = lax.rem(places[2] + groups - step, groups)
        field[pl.ds(src * (frames // groups), depth)] += share[...].astype(f32)
    values = field[2 : 2 + frames]
    token_grad[:, 0] = values[:, :, :width].astype(bf16)
    token_grad[:, 1] = values[:, :, width:].astype(bf16)
    turned = jnp.transpose(token_grad[...].reshape(-1, width).astype(f32)).astype(bf16)
    total = dot(turned, modulated[...].reshape(-1, model))
    half = model // (2 * groups)
    for dst in range(groups):
        at = 2 * half * dst
        weight[dst, :width] = total[:, at : at + half]
        weight[dst, width:] = total[:, at + half : at + 2 * half]
    for step, piece in enumerate(pieces):
        dst = lax.rem(places[2] + step, groups)
        piece[...] = jnp.transpose(weight[dst]).astype(bf16)


def weight_terms(places, modulated, shares):
    groups = len(shares)
    depth, _, pair = shares[0].shape
    frames, token_rows, _, model = modulated.shape
    half = model // (2 * groups)
    return pl.pallas_call(
        weight_kernel,
        out_shape=[jax.ShapeDtypeStruct((frames, token_rows, slots, pair // 2), bf16)]
        + [jax.ShapeDtypeStruct((half, pair), bf16)] * groups,
        in_specs=[scalars] + [whole] * (1 + groups),
        out_specs=[whole] * (1 + groups),
        scratch_shapes=[
            pltpu.VMEM((frames + 2, slots, pair), f32),
            pltpu.VMEM((groups, pair, half), f32),
        ],
        compiler_params=params(12),
        name="weight_terms",
    )(places, modulated, *shares)


def middle_kernel(*refs):
    send = refs[-1]
    total = sum(ref[...].astype(f32) for ref in refs[:-1])
    count, rows, width = send.shape
    total = total.reshape(count // 2, rows, 2 * width).astype(bf16)
    send[0 : count // 2] = total[:, :, :width]
    send[count // 2 :] = total[:, :, width:]


def middle_sum(got, count):
    depth, pair = got[0].shape
    return pl.pallas_call(
        middle_kernel,
        out_shape=jax.ShapeDtypeStruct((count, 2 * depth // count, pair // 2), bf16),
        in_specs=[whole] * len(got),
        out_specs=whole,
        compiler_params=params(4),
        name="middle_sum",
    )(*got)


def hidden_kernel(hidden, token_grad, scale, w_out, grad_hidden):
    frames, token_rows, tokens, width = hidden.shape
    gain = 1.0 + scale[...]
    block = 3

    def share(step, carry):
        rows = token_grad[pl.ds(step * block, block)].reshape(-1, token_grad.shape[-1])
        mod_grad = dot(rows, w_out[...])
        for frame in range(block):
            for row in range(token_rows):
                at = (frame * token_rows + row) * slots
                scaled = mod_grad[at : at + tokens] * gain
                normed, inverse = normalise(hidden[step * block + frame, row].astype(f32))
                first = jnp.mean(scaled, axis=-1, keepdims=True)
                second = jnp.mean(scaled * normed, axis=-1, keepdims=True)
                value = (scaled - first - normed * second) * inverse
                grad_hidden[step * block + frame, row] = value.astype(bf16)
        return carry

    lax.fori_loop(0, frames // block, share, 0)


def hidden_grad(hidden, token_grad, mod_scale, w_out):
    frames, token_rows, tokens, width = hidden.shape
    return pl.pallas_call(
        hidden_kernel,
        out_shape=jax.ShapeDtypeStruct(hidden.shape, bf16),
        in_specs=[whole] * 4,
        out_specs=whole,
        compiler_params=params(8),
        cost_estimate=pl.CostEstimate(
            flops=2 * frames * 2 * slots * width * w_out.shape[0],
            bytes_accessed=8 * frames * slots * width,
            transcendentals=0,
        ),
        name="hidden_grad",
    )(hidden, token_grad, mod_scale.reshape(1, -1), w_out)


def shards(hidden, mod_scale, mod_shift, w_out, w_in, w_section, section_grad):
    groups, strips = lax.axis_size("tm"), lax.axis_size("height")
    rows = section_grad.shape[1]
    swap = lambda a, b: [(a, b), (b, a)]
    near = sum([swap(i, i + 1) for i in range(0, strips - 1, 2)], [])
    far = sum([swap(i, i + 1) for i in range(1, strips - 1, 2)], [])
    odd = lax.rem(lax.axis_index("height"), 2)
    places = jnp.stack([(1 - odd) * (rows - 1), odd * (rows - 1), lax.axis_index("tm")])
    places = places.astype(jnp.int32)
    w_out = jnp.transpose(w_out)
    w_section = pltpu.with_memory_space_constraint(w_section, pltpu.HBM)

    def round_tm(pieces):
        hops = lambda k: [(g, (g + k) % groups) for g in range(groups)]
        return [pieces[0]] + [
            lax.ppermute(pieces[k], "tm", hops(k)) for k in range(1, groups)
        ]

    ahead = fetch(pltpu.with_memory_space_constraint(section_grad, pltpu.HBM))
    grad_ahead = lax.ppermute(ahead, "tm", [(g + 1, g) for g in range(groups - 1)])
    modulated, held_first, *pieces = modulate(
        places, hidden, mod_scale, mod_shift, w_out, w_section, groups
    )
    near_send, far_send, latent, wide, patches = pack_rows(
        places, section_grad, grad_ahead, w_in, round_tm(pieces)
    )
    far_rows = lax.ppermute(far_send, "height", far)
    near_rows = lax.ppermute(near_send, "height", near)
    own, held_rest = own_part(wide, w_section, held_first)
    near_share, far_share, windows, spread = edge_part(
        places, own, latent, near_rows, far_rows, held_first, held_rest, patches
    )
    far_share = lax.ppermute(far_share, "height", far)
    near_share = lax.ppermute(near_share, "height", near)
    centre = inner_part(own, windows, patches, spread, groups)
    shares = round_tm(share_pieces(places, centre, near_share, far_share))
    token_grad, *pieces = weight_terms(places, modulated, shares)
    got = round_tm(pieces)
    grad_hidden = hidden_grad(hidden, token_grad, mod_scale, w_out)
    pieces = lax.all_to_all(middle_sum(got, strips), "height", 0, 0, tiled=True)
    total_tokens = math.prod(hidden.shape[:3]) * groups * strips
    grad_out_weight = jnp.sum(pieces.astype(f32), axis=0) / math.sqrt(total_tokens)
    return (grad_hidden, grad_out_weight)


def solution(mesh):
    placed = (P(None, "height", "tm", None), P(), P(), P(), P(), P(), P("tm", "height", None, None))
    return jax.shard_map(
        shards,
        mesh=mesh,
        in_specs=placed,
        out_specs=(P(None, "height", "tm", None), P(("tm", "height"), None)),
        check_vma=False,
    )
```

```python
import functools
import math

import jax
import jax.numpy as jnp
from jax import lax
from jax.experimental import pallas as pl
from jax.experimental.pallas import tpu as pltpu
from jax.sharding import PartitionSpec as P

epsilon = 1e-05
slots = 16
lanes = 128
f32 = jnp.float32
bf16 = jnp.bfloat16
whole = pl.BlockSpec(memory_space=pltpu.VMEM)
scalars = pl.BlockSpec(memory_space=pltpu.SMEM)
far_off = pl.BlockSpec(memory_space=pltpu.HBM)
early = 3
taps = [(2 - n // 3, (1, 0, 2)[n % 3]) for n in range(9)]


def params(mib):
    return pltpu.CompilerParams(vmem_limit_bytes=int(mib * 2**20))


def dot(lhs, rhs):
    return jnp.dot(lhs, rhs, preferred_element_type=f32)


def dot_turned(lhs, rhs):
    return lax.dot_general(lhs, rhs, (((1,), (1,)), ((), ())), preferred_element_type=f32)


def normalise(values):
    center = jnp.mean(values, axis=-1, keepdims=True)
    shifted = values - center
    spread = jnp.mean(shifted * shifted, axis=-1, keepdims=True)
    inverse = lax.rsqrt(spread + epsilon)
    return shifted * inverse, inverse


def fetch_kernel(grad, ahead, sem):
    copy = pltpu.make_async_copy(grad.at[0:2], ahead, sem)
    copy.start()
    copy.wait()


def fetch(grad):
    return pl.pallas_call(
        fetch_kernel,
        out_shape=jax.ShapeDtypeStruct((2,) + grad.shape[1:], bf16),
        in_specs=[far_off],
        out_specs=whole,
        scratch_shapes=[pltpu.SemaphoreType.DMA],
        compiler_params=params(4),
        name="fetch",
    )(grad)


def wide_weight(w_section):
    return w_section.shape[-2], 3 * w_section.shape[-1]


def weight_copies(w_section, held, some, sems):
    channels = w_section.shape[-1]
    return [
        [
            pltpu.make_async_copy(
                w_section.at[kt, ky, kx],
                held.at[n, :, kx * channels : (kx + 1) * channels],
                sems.at[3 * n + kx],
            )
            for kx in range(3)
        ]
        for n, (kt, ky) in enumerate(some)
    ]


def modulate_kernel(places, hidden, scale, shift, w_out, w_section, modulated, held, *rest):
    pieces, latent, sems = rest[:-2], rest[-2], rest[-1]
    copies = sum(weight_copies(w_section, held, taps[:early], sems), [])
    for copy in copies:
        copy.start()
    frames, token_rows, tokens, width = hidden.shape
    groups = len(pieces)
    block = frames // groups
    gain = 1.0 + scale[...]
    blank = jnp.zeros((slots - tokens, width), f32)
    latent[0:2] = jnp.zeros_like(latent[0:2])

    def share(step, carry):
        for frame in range(block):
            for row in range(token_rows):
                normed, _ = normalise(hidden[step * block + frame, row].astype(f32))
                value = jnp.concatenate([normed * gain + shift[...], blank], axis=0)
                modulated[step * block + frame, row] = value.astype(bf16)
        return carry

    def project(step):
        value = modulated[pl.ds(step * block, block)].reshape(-1, width)
        value = dot_turned(value, w_out[...]).astype(bf16)
        value = value.reshape(block, token_rows, slots, value.shape[-1])
        paired = jnp.concatenate([value[:, 0], value[:, 1]], axis=-1)
        latent[pl.ds(step * block + 2, block)] = paired

    def share_after(step, carry):
        project(step - 1)
        return share(step, carry)

    share(0, 0)
    lax.fori_loop(1, groups, share_after, 0)
    project(groups - 1)
    for step, piece in enumerate(pieces):
        dst = lax.rem(places[2] + step, groups)
        piece[...] = latent[pl.ds(dst * block, block + 2)]
    for copy in copies:
        copy.wait()


def modulate(places, hidden, mod_scale, mod_shift, w_out, w_section, groups):
    frames, token_rows, tokens, width = hidden.shape
    pair = 2 * w_out.shape[0]
    piece = jax.ShapeDtypeStruct((frames // groups + 2, slots, pair), bf16)
    return pl.pallas_call(
        modulate_kernel,
        out_shape=[
            jax.ShapeDtypeStruct((frames, token_rows, slots, width), bf16),
            jax.ShapeDtypeStruct((early,) + wide_weight(w_section), bf16),
        ]
        + [piece] * groups,
        in_specs=[scalars] + [whole] * 4 + [far_off],
        out_specs=[whole] * (2 + groups),
        scratch_shapes=[
            pltpu.VMEM((frames + 2, slots, pair), bf16),
            pltpu.SemaphoreType.DMA((3 * early,)),
        ],
        compiler_params=params(8),
        cost_estimate=pl.CostEstimate(
            flops=2 * frames * slots * width * pair,
            bytes_accessed=8 * frames * slots * width,
            transcendentals=0,
        ),
        name="modulate",
    )(places, hidden, mod_scale.reshape(1, -1), mod_shift.reshape(1, -1), w_out, w_section)


def widened(value):
    cols, channels = value.shape
    wide = value.astype(f32)
    place = lax.broadcasted_iota(jnp.int32, (cols, channels), 0)
    right = jnp.where(place == cols - 1, 0.0, pltpu.roll(wide, cols - 1, 0)).astype(bf16)
    left = jnp.where(place == 0, 0.0, pltpu.roll(wide, 1, 0)).astype(bf16)
    return jnp.concatenate([right, value, left], axis=-1)


def flat(value):
    return value.reshape(-1, value.shape[-1])


def weight_matrix(held_first, held_rest, n):
    return held_first[n] if n < early else held_rest[n - early]


def tail_rows(depth, channels):
    return -(-depth // (channels // lanes)) * slots


def tail_place(frame, start, channels):
    blocks = channels // lanes
    return start + frame // blocks * slots, frame % blocks * lanes


def pack_kernel(places, grad, grad_ahead, w_in, *rest):
    pieces = rest[:4]
    near, far, latent, wide, patches = rest[4:]
    frames, rows, cols, channels = grad.shape
    groups = len(pieces)
    for step, piece in enumerate(pieces):
        latent[lax.rem(places[2] + groups - step, groups)] = piece[...]
    for side, out in ((0, near), (1, far)):
        row = places[side]
        for frame in range(frames + 2):
            at = frame * cols
            value = grad[frame, row] if frame < frames else grad_ahead[frame - frames, row]
            out[at : at + cols] = value
        half = lanes // groups
        for frame in range(frames + 2):
            tops = [latent[src, frame][:, :half] for src in range(groups)]
            ends = [latent[src, frame][:, -half:] for src in range(groups)]
            tops, ends = jnp.concatenate(tops, axis=-1), jnp.concatenate(ends, axis=-1)
            at, lane = tail_place(frame, (frames + 2) * cols, channels)
            out[at : at + slots, lane : lane + lanes] = jnp.where(row == 0, tops, ends)
    for frame in range(frames + 2):
        for row in range(rows):
            value = grad[frame, row] if frame < frames else grad_ahead[frame - frames, row]
            wide[frame, row] = widened(value)

    patches[...] = jnp.zeros_like(patches)
    lat = w_in.shape[3]
    for n in range(4 * 3 * 2 * 2 * 2 * 2):
        p, q, kt, a, b, pp, qq = [
            n // size % top
            for size, top in ((96, 2), (48, 2), (16, 3), (8, 2), (4, 2), (2, 2), (1, 2))
        ]
        ky, kx = p - 1 + 2 * a + pp, q - 1 + 2 * b + qq
        if 0 <= ky < 3 and 0 <= kx < 3:
            at = (((kt * 2 + a) * 2 + b) * 4 + 2 * pp + qq) * lat
            patches[2 * p + q, at : at + lat] = w_in[kt, ky, kx]


def pack_rows(places, grad, grad_ahead, w_in, pieces):
    frames, rows, cols, channels = grad.shape
    groups = len(pieces)
    latent = jax.ShapeDtypeStruct((groups,) + pieces[0].shape, bf16)
    total = (frames + 2) * cols + tail_rows(frames + 2, channels)
    return pl.pallas_call(
        pack_kernel,
        in_specs=[scalars] + [whole] * (3 + groups),
        out_specs=[whole] * 5,
        out_shape=[
            jax.ShapeDtypeStruct((total, channels), bf16),
            jax.ShapeDtypeStruct((total, channels), bf16),
            latent,
            jax.ShapeDtypeStruct((frames + 2, rows, cols, 3 * channels), bf16),
            jax.ShapeDtypeStruct((4, 48 * w_in.shape[3], channels), bf16),
        ],
        compiler_params=params(8),
        name="pack_rows",
    )(places, grad, grad_ahead, w_in, *pieces)


def own_kernel(wide, w_section, held_first, total, held_rest, sems):
    depth, rows, cols, _ = wide.shape
    frames = depth - 2
    copies = weight_copies(w_section, held_rest, taps[early:], sems)
    for copy in sum(copies, []):
        copy.start()
    for n, (kt, ky) in enumerate(taps):
        lo, hi = max(0, ky - 1), rows + min(0, ky - 1)
        window = flat(wide[2 - kt : depth - kt, lo + 1 - ky : hi + 1 - ky])
        if n >= early and n % 3 == 0:
            for copy in sum(copies[n - early : n - early + 3], []):
                copy.wait()
        part = dot_turned(window, weight_matrix(held_first, held_rest, n))
        for lane in range(total.shape[0]):
            value = part[:, lane * lanes : (lane + 1) * lanes]
            value = value.reshape(frames, hi - lo, cols, lanes)
            if n == 0:
                total[lane] = value
            else:
                total[lane, :, lo:hi] += value


def own_part(wide, w_section, held_first):
    depth, rows, cols, _ = wide.shape
    channels = w_section.shape[-1]
    return pl.pallas_call(
        own_kernel,
        out_shape=[
            jax.ShapeDtypeStruct((channels // lanes, depth - 2, rows, cols, lanes), f32),
            jax.ShapeDtypeStruct((len(taps) - early,) + wide_weight(w_section), bf16),
        ],
        in_specs=[whole, far_off, whole],
        out_specs=[whole] * 2,
        scratch_shapes=[pltpu.SemaphoreType.DMA((3 * (len(taps) - early),))],
        compiler_params=params(12),
        cost_estimate=pl.CostEstimate(
            flops=2 * 14 * wide.size * channels,
            bytes_accessed=2 * w_section.size,
            transcendentals=0,
        ),
        name="own_part",
    )(wide, w_section, held_first)


def edge_conv(even, own, near_rows, far_rows, held_first, held_rest, total, wide):
    blocks, frames, rows, cols, _ = own.shape
    for lane in range(blocks):
        total[lane, :, 0] = own[lane, :, 0]
        total[lane, :, 1] = own[lane, :, rows - 1]
    for frame in range(frames + 2):
        at = slice(frame * cols, (frame + 1) * cols)
        ends = near_rows[at], far_rows[at]
        for side in range(2):
            wide[side, frame] = widened(jnp.where(even == (side == 1), ends[0], ends[1]))
    for n, (kt, ky) in enumerate(taps):
        if ky == 1:
            continue
        side = 0 if ky == 2 else 1
        window = flat(wide[side, 2 - kt : frames + 2 - kt])
        part = dot_turned(window, weight_matrix(held_first, held_rest, n))
        for lane in range(blocks):
            value = part[:, lane * lanes : (lane + 1) * lanes]
            total[lane, :, side] += value.reshape(frames, cols, lanes)


def latent_phase(total, slot_of, row_of, spread_row, windows, patches, spread):
    blocks, frames, _, cols, _ = total.shape
    half = cols // 2
    pair = windows.shape[-1]
    for p in range(2):
        for q in range(2):
            top = row_of[p] + p
            window = jnp.concatenate(
                [
                    flat(windows[q, kt : kt + frames, top + a])
                    for kt in range(3)
                    for a in range(2)
                ],
                axis=-1,
            )
            weight = patches[2 * p + q]
            pre = dot(window, weight)
            back = jnp.concatenate(
                [
                    jnp.concatenate(
                        [
                            total[lane, frame, slot_of[p], pl.ds(q, half, stride=2), :]
                            for lane in range(blocks)
                        ],
                        axis=-1,
                    )
                    for frame in range(frames)
                ],
                axis=0,
            )
            gate = jax.nn.sigmoid(pre)
            act_grad = (back * (gate * (1.0 + pre * (1.0 - gate)))).astype(bf16)
            terms = dot_turned(act_grad, weight)
            for kt in range(3):
                for a in range(2):
                    at = (kt * 2 + a) * pair
                    spread[kt : kt + frames, top + a - spread_row, q : q + half] += terms[
                        :, at : at + pair
                    ].reshape(frames, half, pair)


def shares_of(spread, row, half):
    width = spread.shape[-1] // 2
    return spread[:, row, 1 : half + 1, :width] + spread[:, row, 0:half, width:]


def edge_kernel(
    places, own, latent, near_rows, far_rows, held_first, held_rest, patches,
    near_out, far_out, windows, spread, tokens, total, wide,
):
    even = places[0] != 0
    edge_conv(even, own, near_rows, far_rows, held_first, held_rest, total, wide)
    groups, depth, _, pair = latent.shape
    width = pair // 2
    channels = near_rows.shape[1]
    start = depth * own.shape[3]
    part = width // 2
    half = windows.shape[3]
    block = half // groups
    tokens[...] = jnp.zeros_like(tokens)
    for src in range(groups):
        at = slice(8 + src * block, 8 + (src + 1) * block)
        for frame in range(depth):
            value = latent[src, frame].astype(f32)[:block]
            tokens[frame, 1, at] = value[:, :width]
            tokens[frame, 2, at] = value[:, width:]
            row, lane = tail_place(frame, start, channels)
            ends = [
                ref[row : row + slots, lane : lane + lanes].astype(f32)[:block]
                for ref in (near_rows, far_rows)
            ]
            pick = slice(src * part, (src + 1) * part)
            none = jnp.zeros((block, part), f32)
            above = jnp.where(even, ends[1], ends[0])[:, pick]
            below = jnp.where(even, ends[0], ends[1])[:, pick]
            tokens[frame, 0, at] = jnp.concatenate([none, above], axis=-1)
            tokens[frame, 3, at] = jnp.concatenate([below, none], axis=-1)
    for q in range(2):
        left = tokens[:, :, 7 + q : 7 + q + half]
        right = tokens[:, :, 8 + q : 8 + q + half]
        windows[q] = jnp.concatenate([left, right], axis=-1).astype(bf16)
    spread[...] = jnp.zeros_like(spread)
    latent_phase(total, (0, 1), (0, 1), 0, windows, patches, spread)
    for n, row in enumerate((0, 3)):
        tokens[:, n, 0:half] = shares_of(spread, row, half)
    fill = jnp.zeros((slots - block, groups * part), f32)
    for frame in range(depth):
        up, down = [
            jnp.concatenate(
                [
                    tokens[frame, n, dst * block : (dst + 1) * block][:, lo : lo + part]
                    for dst in range(groups)
                ],
                axis=-1,
            )
            for n, lo in ((0, part), (1, 0))
        ]
        padded = lambda v: jnp.concatenate([v, fill], axis=0).astype(bf16)
        near_out[frame] = padded(jnp.where(even, down, up))
        far_out[frame] = padded(jnp.where(even, up, down))


def edge_part(places, own, latent, near_rows, far_rows, held_first, held_rest, patches):
    groups, depth, _, pair = latent.shape
    blocks, frames, _, cols, _ = own.shape
    out = jax.ShapeDtypeStruct((depth, slots, groups * pair // 4), bf16)
    return pl.pallas_call(
        edge_kernel,
        out_shape=[
            out,
            out,
            jax.ShapeDtypeStruct((2, depth, 4, cols // 2, pair), bf16),
            jax.ShapeDtypeStruct((depth, 4, cols // 2 + 8, pair), f32),
        ],
        in_specs=[scalars] + [whole] * 7,
        out_specs=[whole] * 4,
        scratch_shapes=[
            pltpu.VMEM((depth, 4, 72, pair // 2), f32),
            pltpu.VMEM((blocks, frames, 2, cols, lanes), f32),
            pltpu.VMEM((2, depth, cols, 3 * blocks * lanes), bf16),
        ],
        compiler_params=params(14),
        cost_estimate=pl.CostEstimate(
            flops=2 * 6 * own.size * blocks * lanes, bytes_accessed=0, transcendentals=own.size
        ),
        name="edge_part",
    )(places, own, latent, near_rows, far_rows, held_first, held_rest, patches)


def inner_kernel(own, windows, patches, spread_in, out, spread, tokens):
    half = windows.shape[3]
    groups, depth = out.shape[:2]
    block = half // groups
    spread[...] = spread_in[:, 1:3]
    latent_phase(own, (2, 1), (1, 0), 1, windows, patches, spread)
    for row in range(2):
        tokens[:, row] = shares_of(spread, row, half)
    fill = jnp.zeros((slots - block, out.shape[-1]), f32)
    for dst in range(groups):
        at = slice(dst * block, (dst + 1) * block)
        for frame in range(depth):
            value = jnp.concatenate([tokens[frame, 0, at], tokens[frame, 1, at]], axis=-1)
            out[dst, frame] = jnp.concatenate([value, fill], axis=0)


def inner_part(own, windows, patches, spread, groups):
    cols = own.shape[3]
    depth, _, wide, pair = spread.shape
    return pl.pallas_call(
        inner_kernel,
        out_shape=jax.ShapeDtypeStruct((groups, depth, slots, pair), f32),
        in_specs=[whole] * 4,
        out_specs=whole,
        scratch_shapes=[
            pltpu.VMEM((depth, 2, wide, pair), f32),
            pltpu.VMEM((depth, 2, cols // 2, pair // 2), f32),
        ],
        compiler_params=params(10),
        cost_estimate=pl.CostEstimate(
            flops=8 * own.size * 6 * pair, bytes_accessed=0, transcendentals=own.size
        ),
        name="inner_part",
    )(own, windows, patches, spread)


def share_kernel(places, centre, near_share, far_share, *rest):
    pieces, total = rest[:-1], rest[-1]
    even = places[0] != 0
    groups = len(pieces)
    near, far = near_share[...].astype(f32), far_share[...].astype(f32)
    first = jnp.where(even, far, near)
    last = jnp.where(even, near, far)
    part = centre.shape[-1] // 4
    none = jnp.zeros(first.shape[:2] + (2 * part,), f32)
    for dst in range(groups):
        pick = slice(dst * part, (dst + 1) * part)
        terms = jnp.concatenate([first[:, :, pick], none, last[:, :, pick]], axis=-1)
        total[dst] = centre[dst] + terms
    for step, piece in enumerate(pieces):
        piece[...] = total[lax.rem(places[2] + step, groups)].astype(bf16)


def share_pieces(places, centre, near_share, far_share):
    groups = centre.shape[0]
    return pl.pallas_call(
        share_kernel,
        out_shape=[jax.ShapeDtypeStruct(centre.shape[1:], bf16)] * groups,
        in_specs=[scalars] + [whole] * 3,
        out_specs=[whole] * groups,
        scratch_shapes=[pltpu.VMEM(centre.shape, f32)],
        compiler_params=params(4),
        name="share_pieces",
    )(places, centre, near_share, far_share)


def weight_kernel(places, modulated, *rest):
    shares, token_grad, pieces, (field, weight) = rest[:4], rest[4], rest[5:9], rest[9:]
    groups = len(shares)
    depth, _, pair = shares[0].shape
    width = pair // 2
    frames = modulated.shape[0]
    model = modulated.shape[-1]
    field[...] = jnp.zeros_like(field)
    for step, share in enumerate(shares):
        src = lax.rem(places[2] + groups - step, groups)
        field[pl.ds(src * (frames // groups), depth)] += share[...].astype(f32)
    values = field[2 : 2 + frames]
    token_grad[:, 0] = values[:, :, :width].astype(bf16)
    token_grad[:, 1] = values[:, :, width:].astype(bf16)
    turned = jnp.transpose(token_grad[...].reshape(-1, width).astype(f32)).astype(bf16)
    total = dot(turned, modulated[...].reshape(-1, model))
    half = model // (2 * groups)
    for dst in range(groups):
        at = 2 * half * dst
        weight[dst, :width] = total[:, at : at + half]
        weight[dst, width:] = total[:, at + half : at + 2 * half]
    for step, piece in enumerate(pieces):
        dst = lax.rem(places[2] + step, groups)
        piece[...] = jnp.transpose(weight[dst]).astype(bf16)


def weight_terms(places, modulated, shares):
    groups = len(shares)
    depth, _, pair = shares[0].shape
    frames, token_rows, _, model = modulated.shape
    half = model // (2 * groups)
    return pl.pallas_call(
        weight_kernel,
        out_shape=[jax.ShapeDtypeStruct((frames, token_rows, slots, pair // 2), bf16)]
        + [jax.ShapeDtypeStruct((half, pair), bf16)] * groups,
        in_specs=[scalars] + [whole] * (1 + groups),
        out_specs=[whole] * (1 + groups),
        scratch_shapes=[
            pltpu.VMEM((frames + 2, slots, pair), f32),
            pltpu.VMEM((groups, pair, half), f32),
        ],
        compiler_params=params(12),
        name="weight_terms",
    )(places, modulated, *shares)


def middle_kernel(*refs):
    refs, send, total = refs[:-2], refs[-2], refs[-1]
    count = send.shape[0]
    total[...] = sum(ref[...].astype(f32) for ref in refs)
    depth, pair = total.shape
    width = pair // 2
    rows = 2 * depth // count
    half = rows // 2
    fill = jnp.zeros((send.shape[1] - half, pair), f32)
    for n in range(count):
        at, lane = n % (count // 2) * rows, n // (count // 2) * width
        value = total[at : at + rows, lane : lane + width]
        value = jnp.concatenate([value[:half], value[half:]], axis=-1)
        send[n] = jnp.concatenate([value, fill], axis=0).astype(bf16)


def middle_sum(got, count):
    depth, pair = got[0].shape
    rows = -(-depth // count // 16) * 16
    return pl.pallas_call(
        middle_kernel,
        out_shape=jax.ShapeDtypeStruct((count, rows, pair), bf16),
        in_specs=[whole] * len(got),
        out_specs=whole,
        scratch_shapes=[pltpu.VMEM((depth, pair), f32)],
        compiler_params=params(4),
        name="middle_sum",
    )(*got)


def final_kernel(factor, pieces, out):
    half, width = out.shape[0] // 2, out.shape[1]
    total = jnp.sum(pieces[...].astype(f32), axis=0) * factor
    out[:half] = total[:half, :width]
    out[half:] = total[:half, width:]


def final_sum(pieces, rows, factor):
    return pl.pallas_call(
        functools.partial(final_kernel, factor),
        out_shape=jax.ShapeDtypeStruct((rows, pieces.shape[2] // 2), f32),
        in_specs=[whole],
        out_specs=whole,
        compiler_params=params(4),
        name="final_sum",
    )(pieces)


def hidden_kernel(hidden, token_grad, scale, w_out, grad_hidden):
    frames, token_rows, tokens, width = hidden.shape
    gain = 1.0 + scale[...]
    block = 3

    def share(step, carry):
        rows = token_grad[pl.ds(step * block, block)].reshape(-1, token_grad.shape[-1])
        mod_grad = dot(rows, w_out[...])
        for frame in range(block):
            for row in range(token_rows):
                at = (frame * token_rows + row) * slots
                scaled = mod_grad[at : at + tokens] * gain
                normed, inverse = normalise(hidden[step * block + frame, row].astype(f32))
                first = jnp.mean(scaled, axis=-1, keepdims=True)
                second = jnp.mean(scaled * normed, axis=-1, keepdims=True)
                value = (scaled - first - normed * second) * inverse
                grad_hidden[step * block + frame, row] = value.astype(bf16)
        return carry

    lax.fori_loop(0, frames // block, share, 0)


def hidden_grad(hidden, token_grad, mod_scale, w_out):
    frames, token_rows, tokens, width = hidden.shape
    return pl.pallas_call(
        hidden_kernel,
        out_shape=jax.ShapeDtypeStruct(hidden.shape, bf16),
        in_specs=[whole] * 4,
        out_specs=whole,
        compiler_params=params(8),
        cost_estimate=pl.CostEstimate(
            flops=2 * frames * 2 * slots * width * w_out.shape[0],
            bytes_accessed=8 * frames * slots * width,
            transcendentals=0,
        ),
        name="hidden_grad",
    )(hidden, token_grad, mod_scale.reshape(1, -1), w_out)


def shards(hidden, mod_scale, mod_shift, w_out, w_in, w_section, section_grad):
    groups, strips = lax.axis_size("tm"), lax.axis_size("height")
    rows = section_grad.shape[1]
    swap = lambda a, b: [(a, b), (b, a)]
    near = sum([swap(i, i + 1) for i in range(0, strips - 1, 2)], [])
    far = sum([swap(i, i + 1) for i in range(1, strips - 1, 2)], [])
    odd = lax.rem(lax.axis_index("height"), 2)
    places = jnp.stack([(1 - odd) * (rows - 1), odd * (rows - 1), lax.axis_index("tm")])
    places = places.astype(jnp.int32)
    w_out = jnp.transpose(w_out)
    w_section = pltpu.with_memory_space_constraint(w_section, pltpu.HBM)

    def round_tm(pieces):
        hops = lambda k: [(g, (g + k) % groups) for g in range(groups)]
        return [pieces[0]] + [
            lax.ppermute(pieces[k], "tm", hops(k)) for k in range(1, groups)
        ]

    ahead = fetch(pltpu.with_memory_space_constraint(section_grad, pltpu.HBM))
    grad_ahead = lax.ppermute(ahead, "tm", [(g + 1, g) for g in range(groups - 1)])
    modulated, held_first, *pieces = modulate(
        places, hidden, mod_scale, mod_shift, w_out, w_section, groups
    )
    near_send, far_send, latent, wide, patches = pack_rows(
        places, section_grad, grad_ahead, w_in, round_tm(pieces)
    )
    far_rows = lax.ppermute(far_send, "height", far)
    near_rows = lax.ppermute(near_send, "height", near)
    own, held_rest = own_part(wide, w_section, held_first)
    near_share, far_share, windows, spread = edge_part(
        places, own, latent, near_rows, far_rows, held_first, held_rest, patches
    )
    far_share = lax.ppermute(far_share, "height", far)
    near_share = lax.ppermute(near_share, "height", near)
    centre = inner_part(own, windows, patches, spread, groups)
    shares = round_tm(share_pieces(places, centre, near_share, far_share))
    token_grad, *pieces = weight_terms(places, modulated, shares)
    got = round_tm(pieces)
    grad_hidden = hidden_grad(hidden, token_grad, mod_scale, w_out)
    pieces = lax.all_to_all(middle_sum(got, strips), "height", 0, 0, tiled=True)
    total_tokens = math.prod(hidden.shape[:3]) * groups * strips
    model_rows = w_out.shape[1] // (groups * strips)
    grad_out_weight = final_sum(pieces, model_rows, 1.0 / math.sqrt(total_tokens))
    return (grad_hidden, grad_out_weight)


def solution(mesh):
    placed = (P(None, "height", "tm", None), P(), P(), P(), P(), P(), P("tm", "height", None, None))
    return jax.shard_map(
        shards,
        mesh=mesh,
        in_specs=placed,
        out_specs=(P(None, "height", "tm", None), P(("tm", "height"), None)),
        check_vma=False,
    )
```

```python
import functools
import math

import jax
import jax.numpy as jnp
from jax import lax
from jax.experimental import pallas as pl
from jax.experimental.pallas import tpu as pltpu
from jax.sharding import PartitionSpec as P

epsilon = 1e-05
slots = 16
lanes = 128
f32 = jnp.float32
bf16 = jnp.bfloat16
whole = pl.BlockSpec(memory_space=pltpu.VMEM)
scalars = pl.BlockSpec(memory_space=pltpu.SMEM)
far_off = pl.BlockSpec(memory_space=pltpu.HBM)
early = 3
taps = [(2 - n // 3, (1, 0, 2)[n % 3]) for n in range(9)]


def params(mib):
    return pltpu.CompilerParams(vmem_limit_bytes=int(mib * 2**20))


def dot(lhs, rhs):
    return jnp.dot(lhs, rhs, preferred_element_type=f32)


def dot_turned(lhs, rhs):
    return lax.dot_general(lhs, rhs, (((1,), (1,)), ((), ())), preferred_element_type=f32)


def normalise(values):
    center = jnp.mean(values, axis=-1, keepdims=True)
    shifted = values - center
    spread = jnp.mean(shifted * shifted, axis=-1, keepdims=True)
    inverse = lax.rsqrt(spread + epsilon)
    return shifted * inverse, inverse


def fetch_kernel(grad, ahead, sem):
    copy = pltpu.make_async_copy(grad.at[0:2], ahead, sem)
    copy.start()
    copy.wait()


def fetch(grad):
    return pl.pallas_call(
        fetch_kernel,
        out_shape=jax.ShapeDtypeStruct((2,) + grad.shape[1:], bf16),
        in_specs=[far_off],
        out_specs=whole,
        scratch_shapes=[pltpu.SemaphoreType.DMA],
        compiler_params=params(4),
        name="fetch",
    )(grad)


def wide_weight(w_section):
    return w_section.shape[-2], 3 * w_section.shape[-1]


def weight_copies(w_section, held, some, sems):
    channels = w_section.shape[-1]
    return [
        [
            pltpu.make_async_copy(
                w_section.at[kt, ky, kx],
                held.at[n, :, kx * channels : (kx + 1) * channels],
                sems.at[3 * n + kx],
            )
            for kx in range(3)
        ]
        for n, (kt, ky) in enumerate(some)
    ]


def modulate_kernel(
    places, hidden, scale, shift, w_out_far, w_section, modulated, held, *rest
):
    pieces, (latent, w_out, sems, out_sem) = rest[:-4], rest[-4:]
    out_copy = pltpu.make_async_copy(w_out_far, w_out, out_sem)
    out_copy.start()
    copies = sum(weight_copies(w_section, held, taps[:early], sems), [])
    for copy in copies:
        copy.start()
    frames, token_rows, tokens, width = hidden.shape
    groups = len(pieces)
    block = frames // groups
    gain = 1.0 + scale[...]
    blank = jnp.zeros((slots - tokens, width), f32)
    latent[0:2] = jnp.zeros_like(latent[0:2])

    def share(step, carry):
        for frame in range(block):
            for row in range(token_rows):
                normed, _ = normalise(hidden[step * block + frame, row].astype(f32))
                value = jnp.concatenate([normed * gain + shift[...], blank], axis=0)
                modulated[step * block + frame, row] = value.astype(bf16)
        return carry

    def project(step):
        value = modulated[pl.ds(step * block, block)].reshape(-1, width)
        value = dot_turned(value, w_out[...]).astype(bf16)
        value = value.reshape(block, token_rows, slots, value.shape[-1])
        paired = jnp.concatenate([value[:, 0], value[:, 1]], axis=-1)
        latent[pl.ds(step * block + 2, block)] = paired

    def share_after(step, carry):
        project(step - 1)
        return share(step, carry)

    share(0, 0)
    out_copy.wait()
    lax.fori_loop(1, groups, share_after, 0)
    project(groups - 1)
    for step, piece in enumerate(pieces):
        dst = lax.rem(places[2] + step, groups)
        piece[...] = latent[pl.ds(dst * block, block + 2)]
    for copy in copies:
        copy.wait()


def modulate(places, hidden, mod_scale, mod_shift, w_out, w_section, groups):
    frames, token_rows, tokens, width = hidden.shape
    pair = 2 * w_out.shape[0]
    piece = jax.ShapeDtypeStruct((frames // groups + 2, slots, pair), bf16)
    return pl.pallas_call(
        modulate_kernel,
        out_shape=[
            jax.ShapeDtypeStruct((frames, token_rows, slots, width), bf16),
            jax.ShapeDtypeStruct((early,) + wide_weight(w_section), bf16),
        ]
        + [piece] * groups,
        in_specs=[scalars] + [whole] * 3 + [far_off] * 2,
        out_specs=[whole] * (2 + groups),
        scratch_shapes=[
            pltpu.VMEM((frames + 2, slots, pair), bf16),
            pltpu.VMEM(w_out.shape, bf16),
            pltpu.SemaphoreType.DMA((3 * early,)),
            pltpu.SemaphoreType.DMA,
        ],
        compiler_params=params(8),
        cost_estimate=pl.CostEstimate(
            flops=2 * frames * slots * width * pair,
            bytes_accessed=8 * frames * slots * width,
            transcendentals=0,
        ),
        name="modulate",
    )(places, hidden, mod_scale.reshape(1, -1), mod_shift.reshape(1, -1), w_out, w_section)


def widened(value):
    cols, channels = value.shape
    wide = value.astype(f32)
    place = lax.broadcasted_iota(jnp.int32, (cols, channels), 0)
    right = jnp.where(place == cols - 1, 0.0, pltpu.roll(wide, cols - 1, 0)).astype(bf16)
    left = jnp.where(place == 0, 0.0, pltpu.roll(wide, 1, 0)).astype(bf16)
    return jnp.concatenate([right, value, left], axis=-1)


def flat(value):
    return value.reshape(-1, value.shape[-1])


def weight_matrix(held_first, held_rest, n):
    return held_first[n] if n < early else held_rest[n - early]


def tail_rows(depth, channels):
    return -(-depth // (channels // lanes)) * slots


def tail_place(frame, start, channels):
    blocks = channels // lanes
    return start + frame // blocks * slots, frame % blocks * lanes


def widen_kernel(grad, w_in, wide, patches):
    frames, rows, _, _ = grad.shape
    for frame in range(frames):
        for row in range(rows):
            wide[frame, row] = widened(grad[frame, row])
    patches[...] = jnp.zeros_like(patches)
    lat = w_in.shape[3]
    for n in range(4 * 3 * 2 * 2 * 2 * 2):
        p, q, kt, a, b, pp, qq = [
            n // size % top
            for size, top in ((96, 2), (48, 2), (16, 3), (8, 2), (4, 2), (2, 2), (1, 2))
        ]
        ky, kx = p - 1 + 2 * a + pp, q - 1 + 2 * b + qq
        if 0 <= ky < 3 and 0 <= kx < 3:
            at = (((kt * 2 + a) * 2 + b) * 4 + 2 * pp + qq) * lat
            patches[2 * p + q, at : at + lat] = w_in[kt, ky, kx]


def widen_rows(grad, w_in):
    frames, rows, cols, channels = grad.shape
    return pl.pallas_call(
        widen_kernel,
        in_specs=[whole] * 2,
        out_specs=[whole] * 2,
        out_shape=[
            jax.ShapeDtypeStruct((frames, rows, cols, 3 * channels), bf16),
            jax.ShapeDtypeStruct((4, 48 * w_in.shape[3], channels), bf16),
        ],
        compiler_params=params(4),
        cost_estimate=pl.CostEstimate(
            flops=20 * grad.size, bytes_accessed=12 * grad.size, transcendentals=0
        ),
        name="widen_rows",
    )(grad, w_in)


def pack_kernel(places, grad, grad_ahead, *rest):
    pieces = rest[:4]
    near, far, latent = rest[4:]
    frames, rows, cols, channels = grad.shape
    groups = len(pieces)
    for step, piece in enumerate(pieces):
        latent[lax.rem(places[2] + groups - step, groups)] = piece[...]
    for side, out in ((0, near), (1, far)):
        row = places[side]
        for frame in range(frames + 2):
            at = frame * cols
            value = grad[frame, row] if frame < frames else grad_ahead[frame - frames, row]
            out[at : at + cols] = value
        half = lanes // groups
        for frame in range(frames + 2):
            tops = [latent[src, frame][:, :half] for src in range(groups)]
            ends = [latent[src, frame][:, -half:] for src in range(groups)]
            tops, ends = jnp.concatenate(tops, axis=-1), jnp.concatenate(ends, axis=-1)
            at, lane = tail_place(frame, (frames + 2) * cols, channels)
            out[at : at + slots, lane : lane + lanes] = jnp.where(row == 0, tops, ends)


def pack_rows(places, grad, grad_ahead, pieces):
    frames, _, cols, channels = grad.shape
    groups = len(pieces)
    total = (frames + 2) * cols + tail_rows(frames + 2, channels)
    return pl.pallas_call(
        pack_kernel,
        in_specs=[scalars] + [whole] * (2 + groups),
        out_specs=[whole] * 3,
        out_shape=[
            jax.ShapeDtypeStruct((total, channels), bf16),
            jax.ShapeDtypeStruct((total, channels), bf16),
            jax.ShapeDtypeStruct((groups,) + pieces[0].shape, bf16),
        ],
        compiler_params=params(4),
        name="pack_rows",
    )(places, grad, grad_ahead, *pieces)


def own_kernel(wide, grad_ahead, w_section, held_first, total, held_rest, beyond, sems):
    frames, rows, cols, _ = wide.shape
    copies = weight_copies(w_section, held_rest, taps[early:], sems)
    for copy in sum(copies, []):
        copy.start()
    for frame in range(2):
        for row in range(rows):
            beyond[frame, row] = widened(grad_ahead[frame, row])
    for n, (kt, ky) in enumerate(taps):
        lo, hi = max(0, ky - 1), rows + min(0, ky - 1)
        at = slice(lo + 1 - ky, hi + 1 - ky)
        if n >= early and n % 3 == 0:
            for copy in sum(copies[n - early : n - early + 3], []):
                copy.wait()
        weight = weight_matrix(held_first, held_rest, n)
        for source, first, last in (
            (wide[2 - kt :, at], 0, kt + 1),
            (beyond[: 2 - kt, at], kt + 1, frames),
        ):
            if first == last:
                continue
            part = dot_turned(flat(source), weight)
            for lane in range(total.shape[0]):
                value = part[:, lane * lanes : (lane + 1) * lanes]
                value = value.reshape(last - first, hi - lo, cols, lanes)
                if n == 0:
                    total[lane] = value
                else:
                    total[lane, first:last, lo:hi] += value


def own_part(wide, grad_ahead, w_section, held_first):
    frames, rows, cols, _ = wide.shape
    channels = w_section.shape[-1]
    return pl.pallas_call(
        own_kernel,
        out_shape=[
            jax.ShapeDtypeStruct((channels // lanes, frames, rows, cols, lanes), f32),
            jax.ShapeDtypeStruct((len(taps) - early,) + wide_weight(w_section), bf16),
        ],
        in_specs=[whole, whole, far_off, whole],
        out_specs=[whole] * 2,
        scratch_shapes=[
            pltpu.VMEM((2, rows, cols, 3 * channels), bf16),
            pltpu.SemaphoreType.DMA((3 * (len(taps) - early),)),
        ],
        compiler_params=params(14),
        cost_estimate=pl.CostEstimate(
            flops=2 * 24 * wide.size * channels,
            bytes_accessed=2 * w_section.size,
            transcendentals=0,
        ),
        name="own_part",
    )(wide, grad_ahead, w_section, held_first)


def edge_conv(even, own, near_rows, far_rows, held_first, held_rest, total, wide):
    blocks, frames, rows, cols, _ = own.shape
    for lane in range(blocks):
        total[lane, :, 0] = own[lane, :, 0]
        total[lane, :, 1] = own[lane, :, rows - 1]
    for frame in range(frames + 2):
        at = slice(frame * cols, (frame + 1) * cols)
        ends = near_rows[at], far_rows[at]
        for side in range(2):
            wide[side, frame] = widened(jnp.where(even == (side == 1), ends[0], ends[1]))
    for n, (kt, ky) in enumerate(taps):
        if ky == 1:
            continue
        side = 0 if ky == 2 else 1
        window = flat(wide[side, 2 - kt : frames + 2 - kt])
        part = dot_turned(window, weight_matrix(held_first, held_rest, n))
        for lane in range(blocks):
            value = part[:, lane * lanes : (lane + 1) * lanes]
            total[lane, :, side] += value.reshape(frames, cols, lanes)


def latent_phase(total, slot_of, row_of, spread_row, windows, patches, spread):
    blocks, frames, _, cols, _ = total.shape
    half = cols // 2
    pair = windows.shape[-1]
    for p in range(2):
        for q in range(2):
            top = row_of[p] + p
            window = jnp.concatenate(
                [
                    flat(windows[q, kt : kt + frames, top + a])
                    for kt in range(3)
                    for a in range(2)
                ],
                axis=-1,
            )
            weight = patches[2 * p + q]
            pre = dot(window, weight)
            back = jnp.concatenate(
                [
                    jnp.concatenate(
                        [
                            total[lane, frame, slot_of[p], pl.ds(q, half, stride=2), :]
                            for lane in range(blocks)
                        ],
                        axis=-1,
                    )
                    for frame in range(frames)
                ],
                axis=0,
            )
            gate = jax.nn.sigmoid(pre)
            act_grad = (back * (gate * (1.0 + pre * (1.0 - gate)))).astype(bf16)
            terms = dot_turned(act_grad, weight)
            for kt in range(3):
                for a in range(2):
                    at = (kt * 2 + a) * pair
                    spread[kt : kt + frames, top + a - spread_row, q : q + half] += terms[
                        :, at : at + pair
                    ].reshape(frames, half, pair)


def shares_of(spread, row, half):
    width = spread.shape[-1] // 2
    return spread[:, row, 1 : half + 1, :width] + spread[:, row, 0:half, width:]


def edge_kernel(
    places, own, latent, near_rows, far_rows, held_first, held_rest, patches,
    near_out, far_out, windows, spread, tokens, total, wide,
):
    even = places[0] != 0
    edge_conv(even, own, near_rows, far_rows, held_first, held_rest, total, wide)
    groups, depth, _, pair = latent.shape
    width = pair // 2
    channels = near_rows.shape[1]
    start = depth * own.shape[3]
    part = width // 2
    half = windows.shape[3]
    block = half // groups
    tokens[...] = jnp.zeros_like(tokens)
    for src in range(groups):
        at = slice(8 + src * block, 8 + (src + 1) * block)
        for frame in range(depth):
            value = latent[src, frame].astype(f32)[:block]
            tokens[frame, 1, at] = value[:, :width]
            tokens[frame, 2, at] = value[:, width:]
            row, lane = tail_place(frame, start, channels)
            ends = [
                ref[row : row + slots, lane : lane + lanes].astype(f32)[:block]
                for ref in (near_rows, far_rows)
            ]
            pick = slice(src * part, (src + 1) * part)
            none = jnp.zeros((block, part), f32)
            above = jnp.where(even, ends[1], ends[0])[:, pick]
            below = jnp.where(even, ends[0], ends[1])[:, pick]
            tokens[frame, 0, at] = jnp.concatenate([none, above], axis=-1)
            tokens[frame, 3, at] = jnp.concatenate([below, none], axis=-1)
    for q in range(2):
        left = tokens[:, :, 7 + q : 7 + q + half]
        right = tokens[:, :, 8 + q : 8 + q + half]
        windows[q] = jnp.concatenate([left, right], axis=-1).astype(bf16)
    spread[...] = jnp.zeros_like(spread)
    latent_phase(total, (0, 1), (0, 1), 0, windows, patches, spread)
    for n, row in enumerate((0, 3)):
        tokens[:, n, 0:half] = shares_of(spread, row, half)
    fill = jnp.zeros((slots - block, groups * part), f32)
    for frame in range(depth):
        up, down = [
            jnp.concatenate(
                [
                    tokens[frame, n, dst * block : (dst + 1) * block][:, lo : lo + part]
                    for dst in range(groups)
                ],
                axis=-1,
            )
            for n, lo in ((0, part), (1, 0))
        ]
        padded = lambda v: jnp.concatenate([v, fill], axis=0).astype(bf16)
        near_out[frame] = padded(jnp.where(even, down, up))
        far_out[frame] = padded(jnp.where(even, up, down))


def edge_part(places, own, latent, near_rows, far_rows, held_first, held_rest, patches):
    groups, depth, _, pair = latent.shape
    blocks, frames, _, cols, _ = own.shape
    out = jax.ShapeDtypeStruct((depth, slots, groups * pair // 4), bf16)
    return pl.pallas_call(
        edge_kernel,
        out_shape=[
            out,
            out,
            jax.ShapeDtypeStruct((2, depth, 4, cols // 2, pair), bf16),
            jax.ShapeDtypeStruct((depth, 4, cols // 2 + 8, pair), f32),
        ],
        in_specs=[scalars] + [whole] * 7,
        out_specs=[whole] * 4,
        scratch_shapes=[
            pltpu.VMEM((depth, 4, 72, pair // 2), f32),
            pltpu.VMEM((blocks, frames, 2, cols, lanes), f32),
            pltpu.VMEM((2, depth, cols, 3 * blocks * lanes), bf16),
        ],
        compiler_params=params(14),
        cost_estimate=pl.CostEstimate(
            flops=2 * 6 * own.size * blocks * lanes, bytes_accessed=0, transcendentals=own.size
        ),
        name="edge_part",
    )(places, own, latent, near_rows, far_rows, held_first, held_rest, patches)


def inner_kernel(own, windows, patches, spread_in, out, spread, tokens):
    half = windows.shape[3]
    groups, depth = out.shape[:2]
    block = half // groups
    spread[...] = spread_in[:, 1:3]
    latent_phase(own, (2, 1), (1, 0), 1, windows, patches, spread)
    for row in range(2):
        tokens[:, row] = shares_of(spread, row, half)
    fill = jnp.zeros((slots - block, out.shape[-1]), f32)
    for dst in range(groups):
        at = slice(dst * block, (dst + 1) * block)
        for frame in range(depth):
            value = jnp.concatenate([tokens[frame, 0, at], tokens[frame, 1, at]], axis=-1)
            out[dst, frame] = jnp.concatenate([value, fill], axis=0)


def inner_part(own, windows, patches, spread, groups):
    cols = own.shape[3]
    depth, _, wide, pair = spread.shape
    return pl.pallas_call(
        inner_kernel,
        out_shape=jax.ShapeDtypeStruct((groups, depth, slots, pair), f32),
        in_specs=[whole] * 4,
        out_specs=whole,
        scratch_shapes=[
            pltpu.VMEM((depth, 2, wide, pair), f32),
            pltpu.VMEM((depth, 2, cols // 2, pair // 2), f32),
        ],
        compiler_params=params(10),
        cost_estimate=pl.CostEstimate(
            flops=8 * own.size * 6 * pair, bytes_accessed=0, transcendentals=own.size
        ),
        name="inner_part",
    )(own, windows, patches, spread)


def share_kernel(places, centre, near_share, far_share, *rest):
    pieces, total = rest[:-1], rest[-1]
    even = places[0] != 0
    groups = len(pieces)
    near, far = near_share[...].astype(f32), far_share[...].astype(f32)
    first = jnp.where(even, far, near)
    last = jnp.where(even, near, far)
    part = centre.shape[-1] // 4
    none = jnp.zeros(first.shape[:2] + (2 * part,), f32)
    for dst in range(groups):
        pick = slice(dst * part, (dst + 1) * part)
        terms = jnp.concatenate([first[:, :, pick], none, last[:, :, pick]], axis=-1)
        total[dst] = centre[dst] + terms
    for step, piece in enumerate(pieces):
        piece[...] = total[lax.rem(places[2] + step, groups)].astype(bf16)


def share_pieces(places, centre, near_share, far_share):
    groups = centre.shape[0]
    return pl.pallas_call(
        share_kernel,
        out_shape=[jax.ShapeDtypeStruct(centre.shape[1:], bf16)] * groups,
        in_specs=[scalars] + [whole] * 3,
        out_specs=[whole] * groups,
        scratch_shapes=[pltpu.VMEM(centre.shape, f32)],
        compiler_params=params(4),
        name="share_pieces",
    )(places, centre, near_share, far_share)


def weight_kernel(places, modulated, *rest):
    shares, token_grad, pieces, (field, weight) = rest[:4], rest[4], rest[5:9], rest[9:]
    groups = len(shares)
    depth, _, pair = shares[0].shape
    width = pair // 2
    frames = modulated.shape[0]
    model = modulated.shape[-1]
    field[...] = jnp.zeros_like(field)
    for step, share in enumerate(shares):
        src = lax.rem(places[2] + groups - step, groups)
        field[pl.ds(src * (frames // groups), depth)] += share[...].astype(f32)
    values = field[2 : 2 + frames]
    token_grad[:, 0] = values[:, :, :width].astype(bf16)
    token_grad[:, 1] = values[:, :, width:].astype(bf16)
    turned = jnp.transpose(token_grad[...].reshape(-1, width).astype(f32)).astype(bf16)
    total = dot(turned, modulated[...].reshape(-1, model))
    half = model // (2 * groups)
    for dst in range(groups):
        at = 2 * half * dst
        weight[dst, :width] = total[:, at : at + half]
        weight[dst, width:] = total[:, at + half : at + 2 * half]
    for step, piece in enumerate(pieces):
        dst = lax.rem(places[2] + step, groups)
        piece[...] = jnp.transpose(weight[dst]).astype(bf16)


def weight_terms(places, modulated, shares):
    groups = len(shares)
    depth, _, pair = shares[0].shape
    frames, token_rows, _, model = modulated.shape
    half = model // (2 * groups)
    return pl.pallas_call(
        weight_kernel,
        out_shape=[jax.ShapeDtypeStruct((frames, token_rows, slots, pair // 2), bf16)]
        + [jax.ShapeDtypeStruct((half, pair), bf16)] * groups,
        in_specs=[scalars] + [whole] * (1 + groups),
        out_specs=[whole] * (1 + groups),
        scratch_shapes=[
            pltpu.VMEM((frames + 2, slots, pair), f32),
            pltpu.VMEM((groups, pair, half), f32),
        ],
        compiler_params=params(12),
        name="weight_terms",
    )(places, modulated, *shares)


def middle_kernel(*refs):
    refs, send, total = refs[:-2], refs[-2], refs[-1]
    count = send.shape[0]
    total[...] = sum(ref[...].astype(f32) for ref in refs)
    depth, pair = total.shape
    width = pair // 2
    rows = 2 * depth // count
    half = rows // 2
    fill = jnp.zeros((send.shape[1] - half, pair), f32)
    for n in range(count):
        at, lane = n % (count // 2) * rows, n // (count // 2) * width
        value = total[at : at + rows, lane : lane + width]
        value = jnp.concatenate([value[:half], value[half:]], axis=-1)
        send[n] = jnp.concatenate([value, fill], axis=0).astype(bf16)


def middle_sum(got, count):
    depth, pair = got[0].shape
    rows = -(-depth // count // 16) * 16
    return pl.pallas_call(
        middle_kernel,
        out_shape=jax.ShapeDtypeStruct((count, rows, pair), bf16),
        in_specs=[whole] * len(got),
        out_specs=whole,
        scratch_shapes=[pltpu.VMEM((depth, pair), f32)],
        compiler_params=params(4),
        name="middle_sum",
    )(*got)


def final_kernel(factor, pieces, out):
    half, width = out.shape[0] // 2, out.shape[1]
    total = jnp.sum(pieces[...].astype(f32), axis=0) * factor
    out[:half] = total[:half, :width]
    out[half:] = total[:half, width:]


def final_sum(pieces, rows, factor):
    return pl.pallas_call(
        functools.partial(final_kernel, factor),
        out_shape=jax.ShapeDtypeStruct((rows, pieces.shape[2] // 2), f32),
        in_specs=[whole],
        out_specs=whole,
        compiler_params=params(4),
        name="final_sum",
    )(pieces)


def hidden_kernel(hidden, token_grad, scale, w_out, grad_hidden):
    frames, token_rows, tokens, width = hidden.shape
    gain = 1.0 + scale[...]
    block = 3

    def share(step, carry):
        rows = token_grad[pl.ds(step * block, block)].reshape(-1, token_grad.shape[-1])
        mod_grad = dot(rows, w_out[...])
        for frame in range(block):
            for row in range(token_rows):
                at = (frame * token_rows + row) * slots
                scaled = mod_grad[at : at + tokens] * gain
                normed, inverse = normalise(hidden[step * block + frame, row].astype(f32))
                first = jnp.mean(scaled, axis=-1, keepdims=True)
                second = jnp.mean(scaled * normed, axis=-1, keepdims=True)
                value = (scaled - first - normed * second) * inverse
                grad_hidden[step * block + frame, row] = value.astype(bf16)
        return carry

    lax.fori_loop(0, frames // block, share, 0)


def hidden_grad(hidden, token_grad, mod_scale, w_out):
    frames, token_rows, tokens, width = hidden.shape
    return pl.pallas_call(
        hidden_kernel,
        out_shape=jax.ShapeDtypeStruct(hidden.shape, bf16),
        in_specs=[whole] * 4,
        out_specs=whole,
        compiler_params=params(8),
        cost_estimate=pl.CostEstimate(
            flops=2 * frames * 2 * slots * width * w_out.shape[0],
            bytes_accessed=8 * frames * slots * width,
            transcendentals=0,
        ),
        name="hidden_grad",
    )(hidden, token_grad, mod_scale.reshape(1, -1), w_out)


def shards(hidden, mod_scale, mod_shift, w_out, w_in, w_section, section_grad):
    groups, strips = lax.axis_size("tm"), lax.axis_size("height")
    rows = section_grad.shape[1]
    swap = lambda a, b: [(a, b), (b, a)]
    near = sum([swap(i, i + 1) for i in range(0, strips - 1, 2)], [])
    far = sum([swap(i, i + 1) for i in range(1, strips - 1, 2)], [])
    odd = lax.rem(lax.axis_index("height"), 2)
    places = jnp.stack([(1 - odd) * (rows - 1), odd * (rows - 1), lax.axis_index("tm")])
    places = places.astype(jnp.int32)
    w_out = jnp.transpose(w_out)
    w_section = pltpu.with_memory_space_constraint(w_section, pltpu.HBM)

    def round_tm(pieces):
        hops = lambda k: [(g, (g + k) % groups) for g in range(groups)]
        return [pieces[0]] + [
            lax.ppermute(pieces[k], "tm", hops(k)) for k in range(1, groups)
        ]

    ahead = fetch(pltpu.with_memory_space_constraint(section_grad, pltpu.HBM))
    ahead, hidden = lax.optimization_barrier((ahead, hidden))
    grad_ahead = lax.ppermute(ahead, "tm", [(g + 1, g) for g in range(groups - 1)])
    modulated, held_first, *pieces = modulate(
        places,
        hidden,
        mod_scale,
        mod_shift,
        pltpu.with_memory_space_constraint(w_out, pltpu.HBM),
        w_section,
        groups,
    )
    section_grad, pieces = lax.optimization_barrier((section_grad, pieces))
    wide, patches = widen_rows(section_grad, w_in)
    near_send, far_send, latent = pack_rows(places, section_grad, grad_ahead, round_tm(pieces))
    far_rows = lax.ppermute(far_send, "height", far)
    near_rows = lax.ppermute(near_send, "height", near)
    own, held_rest = own_part(wide, grad_ahead, w_section, held_first)
    near_share, far_share, windows, spread = edge_part(
        places, own, latent, near_rows, far_rows, held_first, held_rest, patches
    )
    far_share = lax.ppermute(far_share, "height", far)
    near_share = lax.ppermute(near_share, "height", near)
    centre = inner_part(own, windows, patches, spread, groups)
    shares = round_tm(share_pieces(places, centre, near_share, far_share))
    token_grad, *pieces = weight_terms(places, modulated, shares)
    got = round_tm(pieces)
    grad_hidden = hidden_grad(hidden, token_grad, mod_scale, w_out)
    pieces = lax.all_to_all(middle_sum(got, strips), "height", 0, 0, tiled=True)
    total_tokens = math.prod(hidden.shape[:3]) * groups * strips
    model_rows = w_out.shape[1] // (groups * strips)
    grad_out_weight = final_sum(pieces, model_rows, 1.0 / math.sqrt(total_tokens))
    return (grad_hidden, grad_out_weight)


def solution(mesh):
    placed = (P(None, "height", "tm", None), P(), P(), P(), P(), P(), P("tm", "height", None, None))
    return jax.shard_map(
        shards,
        mesh=mesh,
        in_specs=placed,
        out_specs=(P(None, "height", "tm", None), P(("tm", "height"), None)),
        check_vma=False,
    )
```

```python
import functools
import math

import jax
import jax.numpy as jnp
from jax import lax
from jax.experimental import pallas as pl
from jax.experimental.pallas import tpu as pltpu
from jax.sharding import PartitionSpec as P

epsilon = 1e-05
slots = 16
lanes = 128
f32 = jnp.float32
bf16 = jnp.bfloat16
whole = pl.BlockSpec(memory_space=pltpu.VMEM)
scalars = pl.BlockSpec(memory_space=pltpu.SMEM)
far_off = pl.BlockSpec(memory_space=pltpu.HBM)
early = 3
taps = [(2 - n // 3, (1, 0, 2)[n % 3]) for n in range(9)]


def params(mib):
    return pltpu.CompilerParams(vmem_limit_bytes=int(mib * 2**20))


def dot(lhs, rhs):
    return jnp.dot(lhs, rhs, preferred_element_type=f32)


def dot_turned(lhs, rhs):
    return lax.dot_general(lhs, rhs, (((1,), (1,)), ((), ())), preferred_element_type=f32)


def normalise(values):
    center = jnp.mean(values, axis=-1, keepdims=True)
    shifted = values - center
    spread = jnp.mean(shifted * shifted, axis=-1, keepdims=True)
    inverse = lax.rsqrt(spread + epsilon)
    return shifted * inverse, inverse


def fetch_kernel(grad, ends, between, sems):
    rows = grad.shape[1]
    copies = [
        pltpu.make_async_copy(grad.at[0:2, 0:1], ends.at[:, 0:1], sems.at[0]),
        pltpu.make_async_copy(grad.at[0:2, rows - 1 : rows], ends.at[:, 1:2], sems.at[1]),
        pltpu.make_async_copy(grad.at[0:2, 1 : rows - 1], between, sems.at[2]),
    ]
    for copy in copies:
        copy.start()
    for copy in copies:
        copy.wait()


def fetch(grad):
    _, rows, cols, channels = grad.shape
    return pl.pallas_call(
        fetch_kernel,
        out_shape=[
            jax.ShapeDtypeStruct((2, 2, cols, channels), bf16),
            jax.ShapeDtypeStruct((2, rows - 2, cols, channels), bf16),
        ],
        in_specs=[far_off],
        out_specs=[whole] * 2,
        scratch_shapes=[pltpu.SemaphoreType.DMA((3,))],
        compiler_params=params(4),
        name="fetch",
    )(grad)


def wide_weight(w_section):
    return w_section.shape[-2], 3 * w_section.shape[-1]


def weight_copies(w_section, held, some, sems):
    channels = w_section.shape[-1]
    return [
        [
            pltpu.make_async_copy(
                w_section.at[kt, ky, kx],
                held.at[n, :, kx * channels : (kx + 1) * channels],
                sems.at[3 * n + kx],
            )
            for kx in range(3)
        ]
        for n, (kt, ky) in enumerate(some)
    ]


def modulate_kernel(
    places, hidden, scale, shift, w_out_far, w_section, modulated, held, *rest
):
    pieces, (latent, w_out, sems, out_sem) = rest[:-4], rest[-4:]
    out_copy = pltpu.make_async_copy(w_out_far, w_out, out_sem)
    out_copy.start()
    copies = sum(weight_copies(w_section, held, taps[:early], sems), [])
    for copy in copies:
        copy.start()
    frames, token_rows, tokens, width = hidden.shape
    groups = len(pieces)
    block = frames // groups
    gain = 1.0 + scale[...]
    blank = jnp.zeros((slots - tokens, width), f32)
    latent[0:2] = jnp.zeros_like(latent[0:2])

    def share(step, carry):
        for frame in range(block):
            for row in range(token_rows):
                normed, _ = normalise(hidden[step * block + frame, row].astype(f32))
                value = jnp.concatenate([normed * gain + shift[...], blank], axis=0)
                modulated[step * block + frame, row] = value.astype(bf16)
        return carry

    def project(step):
        value = modulated[pl.ds(step * block, block)].reshape(-1, width)
        value = dot_turned(value, w_out[...]).astype(bf16)
        value = value.reshape(block, token_rows, slots, value.shape[-1])
        paired = jnp.concatenate([value[:, 0], value[:, 1]], axis=-1)
        latent[pl.ds(step * block + 2, block)] = paired

    def share_after(step, carry):
        project(step - 1)
        return share(step, carry)

    share(0, 0)
    out_copy.wait()
    lax.fori_loop(1, groups, share_after, 0)
    project(groups - 1)
    for step, piece in enumerate(pieces):
        dst = lax.rem(places[2] + step, groups)
        piece[...] = latent[pl.ds(dst * block, block + 2)]
    for copy in copies:
        copy.wait()


def modulate(places, hidden, mod_scale, mod_shift, w_out, w_section, groups):
    frames, token_rows, tokens, width = hidden.shape
    pair = 2 * w_out.shape[0]
    piece = jax.ShapeDtypeStruct((frames // groups + 2, slots, pair), bf16)
    return pl.pallas_call(
        modulate_kernel,
        out_shape=[
            jax.ShapeDtypeStruct((frames, token_rows, slots, width), bf16),
            jax.ShapeDtypeStruct((early,) + wide_weight(w_section), bf16),
        ]
        + [piece] * groups,
        in_specs=[scalars] + [whole] * 3 + [far_off] * 2,
        out_specs=[whole] * (2 + groups),
        scratch_shapes=[
            pltpu.VMEM((frames + 2, slots, pair), bf16),
            pltpu.VMEM(w_out.shape, bf16),
            pltpu.SemaphoreType.DMA((3 * early,)),
            pltpu.SemaphoreType.DMA,
        ],
        compiler_params=params(8),
        cost_estimate=pl.CostEstimate(
            flops=2 * frames * slots * width * pair,
            bytes_accessed=8 * frames * slots * width,
            transcendentals=0,
        ),
        name="modulate",
    )(places, hidden, mod_scale.reshape(1, -1), mod_shift.reshape(1, -1), w_out, w_section)


def widened(value):
    cols, channels = value.shape
    wide = value.astype(f32)
    place = lax.broadcasted_iota(jnp.int32, (cols, channels), 0)
    right = jnp.where(place == cols - 1, 0.0, pltpu.roll(wide, cols - 1, 0)).astype(bf16)
    left = jnp.where(place == 0, 0.0, pltpu.roll(wide, 1, 0)).astype(bf16)
    return jnp.concatenate([right, value, left], axis=-1)


def flat(value):
    return value.reshape(-1, value.shape[-1])


def weight_matrix(held_first, held_rest, n):
    return held_first[n] if n < early else held_rest[n - early]


def tail_rows(depth, channels):
    return -(-depth // (channels // lanes)) * slots


def tail_place(frame, start, channels):
    blocks = channels // lanes
    return start + frame // blocks * slots, frame % blocks * lanes


def widen_kernel(grad, w_in, wide, patches):
    frames, rows, _, _ = grad.shape
    for frame in range(frames):
        for row in range(rows):
            wide[frame, row] = widened(grad[frame, row])
    patches[...] = jnp.zeros_like(patches)
    lat = w_in.shape[3]
    for n in range(4 * 3 * 2 * 2 * 2 * 2):
        p, q, kt, a, b, pp, qq = [
            n // size % top
            for size, top in ((96, 2), (48, 2), (16, 3), (8, 2), (4, 2), (2, 2), (1, 2))
        ]
        ky, kx = p - 1 + 2 * a + pp, q - 1 + 2 * b + qq
        if 0 <= ky < 3 and 0 <= kx < 3:
            at = (((kt * 2 + a) * 2 + b) * 4 + 2 * pp + qq) * lat
            patches[2 * p + q, at : at + lat] = w_in[kt, ky, kx]


def widen_rows(grad, w_in):
    frames, rows, cols, channels = grad.shape
    return pl.pallas_call(
        widen_kernel,
        in_specs=[whole] * 2,
        out_specs=[whole] * 2,
        out_shape=[
            jax.ShapeDtypeStruct((frames, rows, cols, 3 * channels), bf16),
            jax.ShapeDtypeStruct((4, 48 * w_in.shape[3], channels), bf16),
        ],
        compiler_params=params(4),
        cost_estimate=pl.CostEstimate(
            flops=20 * grad.size, bytes_accessed=12 * grad.size, transcendentals=0
        ),
        name="widen_rows",
    )(grad, w_in)


def pack_kernel(places, grad, ends_ahead, *rest):
    pieces = rest[:4]
    near, far, latent = rest[4:]
    frames, rows, cols, channels = grad.shape
    groups = len(pieces)
    for step, piece in enumerate(pieces):
        latent[lax.rem(places[2] + groups - step, groups)] = piece[...]
    for side, out in ((0, near), (1, far)):
        row = places[side]
        for frame in range(frames):
            out[frame * cols : (frame + 1) * cols] = grad[frame, row]
        for frame in range(2):
            at = (frames + frame) * cols
            out[at : at + cols] = ends_ahead[frame, jnp.minimum(row, 1)]
        half = lanes // groups
        for frame in range(frames + 2):
            tops = [latent[src, frame][:, :half] for src in range(groups)]
            ends = [latent[src, frame][:, -half:] for src in range(groups)]
            tops, ends = jnp.concatenate(tops, axis=-1), jnp.concatenate(ends, axis=-1)
            at, lane = tail_place(frame, (frames + 2) * cols, channels)
            out[at : at + slots, lane : lane + lanes] = jnp.where(row == 0, tops, ends)


def pack_rows(places, grad, ends_ahead, pieces):
    frames, _, cols, channels = grad.shape
    groups = len(pieces)
    total = (frames + 2) * cols + tail_rows(frames + 2, channels)
    return pl.pallas_call(
        pack_kernel,
        in_specs=[scalars] + [whole] * (2 + groups),
        out_specs=[whole] * 3,
        out_shape=[
            jax.ShapeDtypeStruct((total, channels), bf16),
            jax.ShapeDtypeStruct((total, channels), bf16),
            jax.ShapeDtypeStruct((groups,) + pieces[0].shape, bf16),
        ],
        compiler_params=params(4),
        name="pack_rows",
    )(places, grad, ends_ahead, *pieces)


def own_kernel(
    wide, ends, between, w_section, held_first, total, held_rest, beyond, sems
):
    frames, rows, cols, _ = wide.shape
    copies = weight_copies(w_section, held_rest, taps[early:], sems)
    for copy in sum(copies, []):
        copy.start()
    for frame in range(2):
        beyond[frame, 0] = widened(ends[frame, 0])
        for row in range(1, rows - 1):
            beyond[frame, row] = widened(between[frame, row - 1])
        beyond[frame, rows - 1] = widened(ends[frame, 1])
    for n, (kt, ky) in enumerate(taps):
        lo, hi = max(0, ky - 1), rows + min(0, ky - 1)
        at = slice(lo + 1 - ky, hi + 1 - ky)
        if n >= early and n % 3 == 0:
            for copy in sum(copies[n - early : n - early + 3], []):
                copy.wait()
        weight = weight_matrix(held_first, held_rest, n)
        for frame in range(frames):
            src = frame + 2 - kt
            source = wide[src, at] if src < frames else beyond[src - frames, at]
            part = dot_turned(flat(source), weight)
            for lane in range(total.shape[0]):
                value = part[:, lane * lanes : (lane + 1) * lanes]
                value = value.reshape(hi - lo, cols, lanes)
                if n == 0:
                    total[lane, frame] = value
                else:
                    total[lane, frame, lo:hi] += value


def own_part(wide, ends, between, w_section, held_first):
    frames, rows, cols, _ = wide.shape
    channels = w_section.shape[-1]
    return pl.pallas_call(
        own_kernel,
        out_shape=[
            jax.ShapeDtypeStruct((channels // lanes, frames, rows, cols, lanes), f32),
            jax.ShapeDtypeStruct((len(taps) - early,) + wide_weight(w_section), bf16),
        ],
        in_specs=[whole, whole, whole, far_off, whole],
        out_specs=[whole] * 2,
        scratch_shapes=[
            pltpu.VMEM((2, rows, cols, 3 * channels), bf16),
            pltpu.SemaphoreType.DMA((3 * (len(taps) - early),)),
        ],
        compiler_params=params(14),
        cost_estimate=pl.CostEstimate(
            flops=2 * 24 * wide.size * channels,
            bytes_accessed=2 * w_section.size,
            transcendentals=0,
        ),
        name="own_part",
    )(wide, ends, between, w_section, held_first)


def edge_conv(even, own, near_rows, far_rows, held_first, held_rest, total, wide):
    blocks, frames, rows, cols, _ = own.shape
    for lane in range(blocks):
        total[lane, :, 0] = own[lane, :, 0]
        total[lane, :, 1] = own[lane, :, rows - 1]
    for frame in range(frames + 2):
        at = slice(frame * cols, (frame + 1) * cols)
        ends = near_rows[at], far_rows[at]
        for side in range(2):
            wide[side, frame] = widened(jnp.where(even == (side == 1), ends[0], ends[1]))
    for n, (kt, ky) in enumerate(taps):
        if ky == 1:
            continue
        side = 0 if ky == 2 else 1
        window = flat(wide[side, 2 - kt : frames + 2 - kt])
        part = dot_turned(window, weight_matrix(held_first, held_rest, n))
        for lane in range(blocks):
            value = part[:, lane * lanes : (lane + 1) * lanes]
            total[lane, :, side] += value.reshape(frames, cols, lanes)


def latent_phase(total, slot_of, row_of, spread_row, windows, patches, spread):
    blocks, frames, _, cols, _ = total.shape
    half = cols // 2
    pair = windows.shape[-1]
    for p in range(2):
        for q in range(2):
            top = row_of[p] + p
            window = jnp.concatenate(
                [
                    flat(windows[q, kt : kt + frames, top + a])
                    for kt in range(3)
                    for a in range(2)
                ],
                axis=-1,
            )
            weight = patches[2 * p + q]
            pre = dot(window, weight)
            back = jnp.concatenate(
                [
                    jnp.concatenate(
                        [
                            total[lane, frame, slot_of[p], pl.ds(q, half, stride=2), :]
                            for lane in range(blocks)
                        ],
                        axis=-1,
                    )
                    for frame in range(frames)
                ],
                axis=0,
            )
            gate = jax.nn.sigmoid(pre)
            act_grad = (back * (gate * (1.0 + pre * (1.0 - gate)))).astype(bf16)
            terms = dot_turned(act_grad, weight)
            for kt in range(3):
                for a in range(2):
                    at = (kt * 2 + a) * pair
                    spread[kt : kt + frames, top + a - spread_row, q : q + half] += terms[
                        :, at : at + pair
                    ].reshape(frames, half, pair)


def shares_of(spread, row, half):
    width = spread.shape[-1] // 2
    return spread[:, row, 1 : half + 1, :width] + spread[:, row, 0:half, width:]


def edge_kernel(
    places, own, latent, near_rows, far_rows, held_first, held_rest, patches,
    near_out, far_out, windows, spread, tokens, total, wide,
):
    even = places[0] != 0
    edge_conv(even, own, near_rows, far_rows, held_first, held_rest, total, wide)
    groups, depth, _, pair = latent.shape
    width = pair // 2
    channels = near_rows.shape[1]
    start = depth * own.shape[3]
    part = width // 2
    half = windows.shape[3]
    block = half // groups
    tokens[...] = jnp.zeros_like(tokens)
    for src in range(groups):
        at = slice(8 + src * block, 8 + (src + 1) * block)
        for frame in range(depth):
            value = latent[src, frame].astype(f32)[:block]
            tokens[frame, 1, at] = value[:, :width]
            tokens[frame, 2, at] = value[:, width:]
            row, lane = tail_place(frame, start, channels)
            ends = [
                ref[row : row + slots, lane : lane + lanes].astype(f32)[:block]
                for ref in (near_rows, far_rows)
            ]
            pick = slice(src * part, (src + 1) * part)
            none = jnp.zeros((block, part), f32)
            above = jnp.where(even, ends[1], ends[0])[:, pick]
            below = jnp.where(even, ends[0], ends[1])[:, pick]
            tokens[frame, 0, at] = jnp.concatenate([none, above], axis=-1)
            tokens[frame, 3, at] = jnp.concatenate([below, none], axis=-1)
    for q in range(2):
        left = tokens[:, :, 7 + q : 7 + q + half]
        right = tokens[:, :, 8 + q : 8 + q + half]
        windows[q] = jnp.concatenate([left, right], axis=-1).astype(bf16)
    spread[...] = jnp.zeros_like(spread)
    latent_phase(total, (0, 1), (0, 1), 0, windows, patches, spread)
    for n, row in enumerate((0, 3)):
        tokens[:, n, 0:half] = shares_of(spread, row, half)
    fill = jnp.zeros((slots - block, groups * part), f32)
    for frame in range(depth):
        up, down = [
            jnp.concatenate(
                [
                    tokens[frame, n, dst * block : (dst + 1) * block][:, lo : lo + part]
                    for dst in range(groups)
                ],
                axis=-1,
            )
            for n, lo in ((0, part), (1, 0))
        ]
        padded = lambda v: jnp.concatenate([v, fill], axis=0).astype(bf16)
        near_out[frame] = padded(jnp.where(even, down, up))
        far_out[frame] = padded(jnp.where(even, up, down))


def edge_part(places, own, latent, near_rows, far_rows, held_first, held_rest, patches):
    groups, depth, _, pair = latent.shape
    blocks, frames, _, cols, _ = own.shape
    out = jax.ShapeDtypeStruct((depth, slots, groups * pair // 4), bf16)
    return pl.pallas_call(
        edge_kernel,
        out_shape=[
            out,
            out,
            jax.ShapeDtypeStruct((2, depth, 4, cols // 2, pair), bf16),
            jax.ShapeDtypeStruct((depth, 4, cols // 2 + 8, pair), f32),
        ],
        in_specs=[scalars] + [whole] * 7,
        out_specs=[whole] * 4,
        scratch_shapes=[
            pltpu.VMEM((depth, 4, 72, pair // 2), f32),
            pltpu.VMEM((blocks, frames, 2, cols, lanes), f32),
            pltpu.VMEM((2, depth, cols, 3 * blocks * lanes), bf16),
        ],
        compiler_params=params(14),
        cost_estimate=pl.CostEstimate(
            flops=2 * 6 * own.size * blocks * lanes, bytes_accessed=0, transcendentals=own.size
        ),
        name="edge_part",
    )(places, own, latent, near_rows, far_rows, held_first, held_rest, patches)


def inner_kernel(own, windows, patches, spread_in, out, spread, tokens):
    half = windows.shape[3]
    groups, depth = out.shape[:2]
    block = half // groups
    spread[...] = spread_in[:, 1:3]
    latent_phase(own, (2, 1), (1, 0), 1, windows, patches, spread)
    for row in range(2):
        tokens[:, row] = shares_of(spread, row, half)
    fill = jnp.zeros((slots - block, out.shape[-1]), f32)
    for dst in range(groups):
        at = slice(dst * block, (dst + 1) * block)
        for frame in range(depth):
            value = jnp.concatenate([tokens[frame, 0, at], tokens[frame, 1, at]], axis=-1)
            out[dst, frame] = jnp.concatenate([value, fill], axis=0)


def inner_part(own, windows, patches, spread, groups):
    cols = own.shape[3]
    depth, _, wide, pair = spread.shape
    return pl.pallas_call(
        inner_kernel,
        out_shape=jax.ShapeDtypeStruct((groups, depth, slots, pair), f32),
        in_specs=[whole] * 4,
        out_specs=whole,
        scratch_shapes=[
            pltpu.VMEM((depth, 2, wide, pair), f32),
            pltpu.VMEM((depth, 2, cols // 2, pair // 2), f32),
        ],
        compiler_params=params(10),
        cost_estimate=pl.CostEstimate(
            flops=8 * own.size * 6 * pair, bytes_accessed=0, transcendentals=own.size
        ),
        name="inner_part",
    )(own, windows, patches, spread)


def share_kernel(places, centre, near_share, far_share, *rest):
    pieces, total = rest[:-1], rest[-1]
    even = places[0] != 0
    groups = len(pieces)
    near, far = near_share[...].astype(f32), far_share[...].astype(f32)
    first = jnp.where(even, far, near)
    last = jnp.where(even, near, far)
    part = centre.shape[-1] // 4
    none = jnp.zeros(first.shape[:2] + (2 * part,), f32)
    for dst in range(groups):
        pick = slice(dst * part, (dst + 1) * part)
        terms = jnp.concatenate([first[:, :, pick], none, last[:, :, pick]], axis=-1)
        total[dst] = centre[dst] + terms
    for step, piece in enumerate(pieces):
        piece[...] = total[lax.rem(places[2] + step, groups)].astype(bf16)


def share_pieces(places, centre, near_share, far_share):
    groups = centre.shape[0]
    return pl.pallas_call(
        share_kernel,
        out_shape=[jax.ShapeDtypeStruct(centre.shape[1:], bf16)] * groups,
        in_specs=[scalars] + [whole] * 3,
        out_specs=[whole] * groups,
        scratch_shapes=[pltpu.VMEM(centre.shape, f32)],
        compiler_params=params(4),
        name="share_pieces",
    )(places, centre, near_share, far_share)


def weight_kernel(places, modulated, *rest):
    shares, token_grad, pieces, (field, weight) = rest[:4], rest[4], rest[5:9], rest[9:]
    groups = len(shares)
    depth, _, pair = shares[0].shape
    width = pair // 2
    frames = modulated.shape[0]
    model = modulated.shape[-1]
    field[...] = jnp.zeros_like(field)
    for step, share in enumerate(shares):
        src = lax.rem(places[2] + groups - step, groups)
        field[pl.ds(src * (frames // groups), depth)] += share[...].astype(f32)
    values = field[2 : 2 + frames]
    token_grad[:, 0] = values[:, :, :width].astype(bf16)
    token_grad[:, 1] = values[:, :, width:].astype(bf16)
    turned = jnp.transpose(token_grad[...].reshape(-1, width).astype(f32)).astype(bf16)
    total = dot(turned, modulated[...].reshape(-1, model))
    half = model // (2 * groups)
    for dst in range(groups):
        at = 2 * half * dst
        weight[dst, :width] = total[:, at : at + half]
        weight[dst, width:] = total[:, at + half : at + 2 * half]
    for step, piece in enumerate(pieces):
        dst = lax.rem(places[2] + step, groups)
        piece[...] = jnp.transpose(weight[dst]).astype(bf16)


def weight_terms(places, modulated, shares):
    groups = len(shares)
    depth, _, pair = shares[0].shape
    frames, token_rows, _, model = modulated.shape
    half = model // (2 * groups)
    return pl.pallas_call(
        weight_kernel,
        out_shape=[jax.ShapeDtypeStruct((frames, token_rows, slots, pair // 2), bf16)]
        + [jax.ShapeDtypeStruct((half, pair), bf16)] * groups,
        in_specs=[scalars] + [whole] * (1 + groups),
        out_specs=[whole] * (1 + groups),
        scratch_shapes=[
            pltpu.VMEM((frames + 2, slots, pair), f32),
            pltpu.VMEM((groups, pair, half), f32),
        ],
        compiler_params=params(12),
        name="weight_terms",
    )(places, modulated, *shares)


def middle_kernel(*refs):
    refs, send, total = refs[:-2], refs[-2], refs[-1]
    count = send.shape[0]
    total[...] = sum(ref[...].astype(f32) for ref in refs)
    depth, pair = total.shape
    width = pair // 2
    rows = 2 * depth // count
    half = rows // 2
    fill = jnp.zeros((send.shape[1] - half, pair), f32)
    for n in range(count):
        at, lane = n % (count // 2) * rows, n // (count // 2) * width
        value = total[at : at + rows, lane : lane + width]
        value = jnp.concatenate([value[:half], value[half:]], axis=-1)
        send[n] = jnp.concatenate([value, fill], axis=0).astype(bf16)


def middle_sum(got, count):
    depth, pair = got[0].shape
    rows = -(-depth // count // 16) * 16
    return pl.pallas_call(
        middle_kernel,
        out_shape=jax.ShapeDtypeStruct((count, rows, pair), bf16),
        in_specs=[whole] * len(got),
        out_specs=whole,
        scratch_shapes=[pltpu.VMEM((depth, pair), f32)],
        compiler_params=params(4),
        name="middle_sum",
    )(*got)


def final_kernel(factor, pieces, out):
    half, width = out.shape[0] // 2, out.shape[1]
    total = jnp.sum(pieces[...].astype(f32), axis=0) * factor
    out[:half] = total[:half, :width]
    out[half:] = total[:half, width:]


def final_sum(pieces, rows, factor):
    return pl.pallas_call(
        functools.partial(final_kernel, factor),
        out_shape=jax.ShapeDtypeStruct((rows, pieces.shape[2] // 2), f32),
        in_specs=[whole],
        out_specs=whole,
        compiler_params=params(4),
        name="final_sum",
    )(pieces)


def hidden_kernel(hidden, token_grad, scale, w_out, grad_hidden):
    frames, token_rows, tokens, width = hidden.shape
    gain = 1.0 + scale[...]
    block = 3

    def share(step, carry):
        rows = token_grad[pl.ds(step * block, block)].reshape(-1, token_grad.shape[-1])
        mod_grad = dot(rows, w_out[...])
        for frame in range(block):
            for row in range(token_rows):
                at = (frame * token_rows + row) * slots
                scaled = mod_grad[at : at + tokens] * gain
                normed, inverse = normalise(hidden[step * block + frame, row].astype(f32))
                first = jnp.mean(scaled, axis=-1, keepdims=True)
                second = jnp.mean(scaled * normed, axis=-1, keepdims=True)
                value = (scaled - first - normed * second) * inverse
                grad_hidden[step * block + frame, row] = value.astype(bf16)
        return carry

    lax.fori_loop(0, frames // block, share, 0)


def hidden_grad(hidden, token_grad, mod_scale, w_out):
    frames, token_rows, tokens, width = hidden.shape
    return pl.pallas_call(
        hidden_kernel,
        out_shape=jax.ShapeDtypeStruct(hidden.shape, bf16),
        in_specs=[whole] * 4,
        out_specs=whole,
        compiler_params=params(8),
        cost_estimate=pl.CostEstimate(
            flops=2 * frames * 2 * slots * width * w_out.shape[0],
            bytes_accessed=8 * frames * slots * width,
            transcendentals=0,
        ),
        name="hidden_grad",
    )(hidden, token_grad, mod_scale.reshape(1, -1), w_out)


def shards(hidden, mod_scale, mod_shift, w_out, w_in, w_section, section_grad):
    groups, strips = lax.axis_size("tm"), lax.axis_size("height")
    rows = section_grad.shape[1]
    swap = lambda a, b: [(a, b), (b, a)]
    near = sum([swap(i, i + 1) for i in range(0, strips - 1, 2)], [])
    far = sum([swap(i, i + 1) for i in range(1, strips - 1, 2)], [])
    odd = lax.rem(lax.axis_index("height"), 2)
    places = jnp.stack([(1 - odd) * (rows - 1), odd * (rows - 1), lax.axis_index("tm")])
    places = places.astype(jnp.int32)
    w_out = jnp.transpose(w_out)
    w_section = pltpu.with_memory_space_constraint(w_section, pltpu.HBM)

    def round_tm(pieces):
        hops = lambda k: [(g, (g + k) % groups) for g in range(groups)]
        return [pieces[0]] + [
            lax.ppermute(pieces[k], "tm", hops(k)) for k in range(1, groups)
        ]

    ends, between = fetch(pltpu.with_memory_space_constraint(section_grad, pltpu.HBM))
    earlier = [(g + 1, g) for g in range(groups - 1)]
    ends = lax.ppermute(ends, "tm", earlier)
    modulated, held_first, *pieces = modulate(
        places,
        hidden,
        mod_scale,
        mod_shift,
        pltpu.with_memory_space_constraint(w_out, pltpu.HBM),
        w_section,
        groups,
    )
    section_grad, pieces = lax.optimization_barrier((section_grad, pieces))
    wide, patches = widen_rows(section_grad, w_in)
    pieces = round_tm(pieces)
    between, pieces[1] = lax.optimization_barrier((between, pieces[1]))
    between = lax.ppermute(between, "tm", earlier)
    near_send, far_send, latent = pack_rows(places, section_grad, ends, pieces)
    far_rows = lax.ppermute(far_send, "height", far)
    near_rows = lax.ppermute(near_send, "height", near)
    own, held_rest = own_part(wide, ends, between, w_section, held_first)
    near_share, far_share, windows, spread = edge_part(
        places, own, latent, near_rows, far_rows, held_first, held_rest, patches
    )
    far_share = lax.ppermute(far_share, "height", far)
    near_share = lax.ppermute(near_share, "height", near)
    centre = inner_part(own, windows, patches, spread, groups)
    shares = round_tm(share_pieces(places, centre, near_share, far_share))
    token_grad, *pieces = weight_terms(places, modulated, shares)
    got = round_tm(pieces)
    grad_hidden = hidden_grad(hidden, token_grad, mod_scale, w_out)
    pieces = lax.all_to_all(middle_sum(got, strips), "height", 0, 0, tiled=True)
    total_tokens = math.prod(hidden.shape[:3]) * groups * strips
    model_rows = w_out.shape[1] // (groups * strips)
    grad_out_weight = final_sum(pieces, model_rows, 1.0 / math.sqrt(total_tokens))
    return (grad_hidden, grad_out_weight)


def solution(mesh):
    placed = (P(None, "height", "tm", None), P(), P(), P(), P(), P(), P("tm", "height", None, None))
    return jax.shard_map(
        shards,
        mesh=mesh,
        in_specs=placed,
        out_specs=(P(None, "height", "tm", None), P(("tm", "height"), None)),
        check_vma=False,
    )
```

```python
import functools
import math

import jax
import jax.numpy as jnp
from jax import lax
from jax.experimental import pallas as pl
from jax.experimental.pallas import tpu as pltpu
from jax.sharding import PartitionSpec as P

epsilon = 1e-05
slots = 16
lanes = 128
f32 = jnp.float32
bf16 = jnp.bfloat16
whole = pl.BlockSpec(memory_space=pltpu.VMEM)
scalars = pl.BlockSpec(memory_space=pltpu.SMEM)
far_off = pl.BlockSpec(memory_space=pltpu.HBM)
early = 3
taps = [(2 - n // 3, (1, 0, 2)[n % 3]) for n in range(9)]


def params(mib):
    return pltpu.CompilerParams(vmem_limit_bytes=int(mib * 2**20))


def dot(lhs, rhs):
    return jnp.dot(lhs, rhs, preferred_element_type=f32)


def dot_turned(lhs, rhs):
    return lax.dot_general(lhs, rhs, (((1,), (1,)), ((), ())), preferred_element_type=f32)


def normalise(values):
    center = jnp.mean(values, axis=-1, keepdims=True)
    shifted = values - center
    spread = jnp.mean(shifted * shifted, axis=-1, keepdims=True)
    inverse = lax.rsqrt(spread + epsilon)
    return shifted * inverse, inverse


def fetch_kernel(grad, ends, between, sems):
    rows = grad.shape[1]
    copies = [
        pltpu.make_async_copy(grad.at[0:2, 0:1], ends.at[:, 0:1], sems.at[0]),
        pltpu.make_async_copy(grad.at[0:2, rows - 1 : rows], ends.at[:, 1:2], sems.at[1]),
        pltpu.make_async_copy(grad.at[0:2, 1:2], ends.at[:, 2:3], sems.at[2]),
        pltpu.make_async_copy(grad.at[0:2, 2 : rows - 1], between, sems.at[3]),
    ]
    for copy in copies:
        copy.start()
    for copy in copies:
        copy.wait()


def fetch(grad):
    _, rows, cols, channels = grad.shape
    return pl.pallas_call(
        fetch_kernel,
        out_shape=[
            jax.ShapeDtypeStruct((2, 3, cols, channels), bf16),
            jax.ShapeDtypeStruct((2, rows - 3, cols, channels), bf16),
        ],
        in_specs=[far_off],
        out_specs=[whole] * 2,
        scratch_shapes=[pltpu.SemaphoreType.DMA((4,))],
        compiler_params=params(4),
        name="fetch",
    )(grad)


def wide_weight(w_section):
    return w_section.shape[-2], 3 * w_section.shape[-1]


def weight_copies(w_section, held, some, sems):
    channels = w_section.shape[-1]
    return [
        [
            pltpu.make_async_copy(
                w_section.at[kt, ky, kx],
                held.at[n, :, kx * channels : (kx + 1) * channels],
                sems.at[3 * n + kx],
            )
            for kx in range(3)
        ]
        for n, (kt, ky) in enumerate(some)
    ]


def modulate_kernel(
    places, hidden, scale, shift, w_out, w_section, modulated, held, *rest
):
    pieces, latent, sems = rest[:-2], rest[-2], rest[-1]
    copies = sum(weight_copies(w_section, held, taps[:early], sems), [])
    for copy in copies:
        copy.start()
    frames, token_rows, tokens, width = hidden.shape
    groups = len(pieces)
    block = frames // groups
    gain = 1.0 + scale[...]
    blank = jnp.zeros((slots - tokens, width), f32)
    latent[0:2] = jnp.zeros_like(latent[0:2])

    def share(step, carry):
        for frame in range(block):
            for row in range(token_rows):
                normed, _ = normalise(hidden[step * block + frame, row].astype(f32))
                value = jnp.concatenate([normed * gain + shift[...], blank], axis=0)
                modulated[step * block + frame, row] = value.astype(bf16)
        return carry

    def project(step):
        value = modulated[pl.ds(step * block, block)].reshape(-1, width)
        value = dot_turned(value, w_out[...]).astype(bf16)
        value = value.reshape(block, token_rows, slots, value.shape[-1])
        paired = jnp.concatenate([value[:, 0], value[:, 1]], axis=-1)
        latent[pl.ds(step * block + 2, block)] = paired

    def share_after(step, carry):
        project(step - 1)
        return share(step, carry)

    share(0, 0)
    lax.fori_loop(1, groups, share_after, 0)
    project(groups - 1)
    for step, piece in enumerate(pieces):
        dst = lax.rem(places[2] + step, groups)
        piece[...] = latent[pl.ds(dst * block, block + 2)]
    for copy in copies:
        copy.wait()


def modulate(places, hidden, mod_scale, mod_shift, w_out, w_section, groups):
    frames, token_rows, tokens, width = hidden.shape
    pair = 2 * w_out.shape[0]
    piece = jax.ShapeDtypeStruct((frames // groups + 2, slots, pair), bf16)
    return pl.pallas_call(
        modulate_kernel,
        out_shape=[
            jax.ShapeDtypeStruct((frames, token_rows, slots, width), bf16),
            jax.ShapeDtypeStruct((early,) + wide_weight(w_section), bf16),
        ]
        + [piece] * groups,
        in_specs=[scalars] + [whole] * 4 + [far_off],
        out_specs=[whole] * (2 + groups),
        scratch_shapes=[
            pltpu.VMEM((frames + 2, slots, pair), bf16),
            pltpu.SemaphoreType.DMA((3 * early,)),
        ],
        compiler_params=params(8),
        cost_estimate=pl.CostEstimate(flops=1, bytes_accessed=1, transcendentals=0),
        name="modulate",
    )(places, hidden, mod_scale.reshape(1, -1), mod_shift.reshape(1, -1), w_out, w_section)


def widened(value):
    cols, channels = value.shape
    wide = value.astype(f32)
    place = lax.broadcasted_iota(jnp.int32, (cols, channels), 0)
    right = jnp.where(place == cols - 1, 0.0, pltpu.roll(wide, cols - 1, 0)).astype(bf16)
    left = jnp.where(place == 0, 0.0, pltpu.roll(wide, 1, 0)).astype(bf16)
    return jnp.concatenate([right, value, left], axis=-1)


def flat(value):
    return value.reshape(-1, value.shape[-1])


def weight_matrix(held_first, held_rest, n):
    return held_first[n] if n < early else held_rest[n - early]


def tail_rows(depth, channels):
    return -(-depth // (channels // lanes)) * slots


def tail_place(frame, start, channels):
    blocks = channels // lanes
    return start + frame // blocks * slots, frame % blocks * lanes


def widen_kernel(grad, w_in, wide, patches):
    frames, rows, _, _ = grad.shape
    for frame in range(frames):
        for row in range(rows):
            wide[frame, row] = widened(grad[frame, row])
    patches[...] = jnp.zeros_like(patches)
    lat = w_in.shape[3]
    for n in range(4 * 3 * 2 * 2 * 2 * 2):
        p, q, kt, a, b, pp, qq = [
            n // size % top
            for size, top in ((96, 2), (48, 2), (16, 3), (8, 2), (4, 2), (2, 2), (1, 2))
        ]
        ky, kx = p - 1 + 2 * a + pp, q - 1 + 2 * b + qq
        if 0 <= ky < 3 and 0 <= kx < 3:
            at = (((kt * 2 + a) * 2 + b) * 4 + 2 * pp + qq) * lat
            patches[2 * p + q, at : at + lat] = w_in[kt, ky, kx]


def widen_rows(grad, w_in):
    frames, rows, cols, channels = grad.shape
    return pl.pallas_call(
        widen_kernel,
        in_specs=[whole] * 2,
        out_specs=[whole] * 2,
        out_shape=[
            jax.ShapeDtypeStruct((frames, rows, cols, 3 * channels), bf16),
            jax.ShapeDtypeStruct((4, 48 * w_in.shape[3], channels), bf16),
        ],
        compiler_params=params(4),
        cost_estimate=pl.CostEstimate(
            flops=20 * grad.size, bytes_accessed=12 * grad.size, transcendentals=0
        ),
        name="widen_rows",
    )(grad, w_in)


def pack_kernel(places, grad, ends_ahead, *rest):
    pieces = rest[:4]
    near, far, latent = rest[4:]
    frames, rows, cols, channels = grad.shape
    groups = len(pieces)
    for step, piece in enumerate(pieces):
        latent[lax.rem(places[2] + groups - step, groups)] = piece[...]
    for side, out in ((0, near), (1, far)):
        row = places[side]
        for frame in range(frames):
            out[frame * cols : (frame + 1) * cols] = grad[frame, row]
        for frame in range(2):
            at = (frames + frame) * cols
            out[at : at + cols] = ends_ahead[frame, jnp.minimum(row, 1)]
        half = lanes // groups
        for frame in range(frames + 2):
            tops = [latent[src, frame][:, :half] for src in range(groups)]
            ends = [latent[src, frame][:, -half:] for src in range(groups)]
            tops, ends = jnp.concatenate(tops, axis=-1), jnp.concatenate(ends, axis=-1)
            at, lane = tail_place(frame, (frames + 2) * cols, channels)
            out[at : at + slots, lane : lane + lanes] = jnp.where(row == 0, tops, ends)


def pack_rows(places, grad, ends_ahead, pieces):
    frames, _, cols, channels = grad.shape
    groups = len(pieces)
    total = (frames + 2) * cols + tail_rows(frames + 2, channels)
    return pl.pallas_call(
        pack_kernel,
        in_specs=[scalars] + [whole] * (2 + groups),
        out_specs=[whole] * 3,
        out_shape=[
            jax.ShapeDtypeStruct((total, channels), bf16),
            jax.ShapeDtypeStruct((total, channels), bf16),
            jax.ShapeDtypeStruct((groups,) + pieces[0].shape, bf16),
        ],
        compiler_params=params(4),
        name="pack_rows",
    )(places, grad, ends_ahead, *pieces)


def own_kernel(
    wide, ends, between, w_section, held_first, total, held_rest, beyond, sems
):
    frames, rows, cols, _ = wide.shape
    copies = weight_copies(w_section, held_rest, taps[early:], sems)
    for copy in sum(copies, []):
        copy.start()
    for frame in range(2):
        beyond[frame, 0] = widened(ends[frame, 0])
        beyond[frame, 1] = widened(ends[frame, 2])
        for row in range(2, rows - 1):
            beyond[frame, row] = widened(between[frame, row - 2])
        beyond[frame, rows - 1] = widened(ends[frame, 1])
    for n, (kt, ky) in enumerate(taps):
        lo, hi = max(0, ky - 1), rows + min(0, ky - 1)
        at = slice(lo + 1 - ky, hi + 1 - ky)
        if n >= early and n % 3 == 0:
            for copy in sum(copies[n - early : n - early + 3], []):
                copy.wait()
        weight = weight_matrix(held_first, held_rest, n)
        for source, first, last in (
            (wide[2 - kt :, at], 0, kt + 1),
            (beyond[: 2 - kt, at], kt + 1, frames),
        ):
            if first == last:
                continue
            part = dot_turned(flat(source), weight)
            for lane in range(total.shape[0]):
                value = part[:, lane * lanes : (lane + 1) * lanes]
                value = value.reshape(last - first, hi - lo, cols, lanes)
                if n == 0:
                    total[lane] = value
                else:
                    total[lane, first:last, lo:hi] += value


def own_part(wide, ends, between, w_section, held_first):
    frames, rows, cols, _ = wide.shape
    channels = w_section.shape[-1]
    return pl.pallas_call(
        own_kernel,
        out_shape=[
            jax.ShapeDtypeStruct((channels // lanes, frames, rows, cols, lanes), f32),
            jax.ShapeDtypeStruct((len(taps) - early,) + wide_weight(w_section), bf16),
        ],
        in_specs=[whole, whole, whole, far_off, whole],
        out_specs=[whole] * 2,
        scratch_shapes=[
            pltpu.VMEM((2, rows, cols, 3 * channels), bf16),
            pltpu.SemaphoreType.DMA((3 * (len(taps) - early),)),
        ],
        compiler_params=params(14),
        cost_estimate=pl.CostEstimate(
            flops=2 * 24 * wide.size * channels,
            bytes_accessed=2 * w_section.size,
            transcendentals=0,
        ),
        name="own_part",
    )(wide, ends, between, w_section, held_first)


def edge_conv(even, own, near_rows, far_rows, held_first, held_rest, total, wide):
    blocks, frames, rows, cols, _ = own.shape
    for lane in range(blocks):
        total[lane, :, 0] = own[lane, :, 0]
        total[lane, :, 1] = own[lane, :, rows - 1]
    for frame in range(frames + 2):
        at = slice(frame * cols, (frame + 1) * cols)
        ends = near_rows[at], far_rows[at]
        for side in range(2):
            wide[side, frame] = widened(jnp.where(even == (side == 1), ends[0], ends[1]))
    for n, (kt, ky) in enumerate(taps):
        if ky == 1:
            continue
        side = 0 if ky == 2 else 1
        window = flat(wide[side, 2 - kt : frames + 2 - kt])
        part = dot_turned(window, weight_matrix(held_first, held_rest, n))
        for lane in range(blocks):
            value = part[:, lane * lanes : (lane + 1) * lanes]
            total[lane, :, side] += value.reshape(frames, cols, lanes)


def latent_phase(total, slot_of, row_of, spread_row, windows, patches, spread):
    blocks, frames, _, cols, _ = total.shape
    half = cols // 2
    pair = windows.shape[-1]
    for p in range(2):
        for q in range(2):
            top = row_of[p] + p
            window = jnp.concatenate(
                [
                    flat(windows[q, kt : kt + frames, top + a])
                    for kt in range(3)
                    for a in range(2)
                ],
                axis=-1,
            )
            weight = patches[2 * p + q]
            pre = dot(window, weight)
            back = jnp.concatenate(
                [
                    jnp.concatenate(
                        [
                            total[lane, frame, slot_of[p], pl.ds(q, half, stride=2), :]
                            for lane in range(blocks)
                        ],
                        axis=-1,
                    )
                    for frame in range(frames)
                ],
                axis=0,
            )
            gate = jax.nn.sigmoid(pre)
            act_grad = (back * (gate * (1.0 + pre * (1.0 - gate)))).astype(bf16)
            terms = dot_turned(act_grad, weight)
            for kt in range(3):
                for a in range(2):
                    at = (kt * 2 + a) * pair
                    spread[kt : kt + frames, top + a - spread_row, q : q + half] += terms[
                        :, at : at + pair
                    ].reshape(frames, half, pair)


def shares_of(spread, row, half):
    width = spread.shape[-1] // 2
    return spread[:, row, 1 : half + 1, :width] + spread[:, row, 0:half, width:]


def edge_kernel(
    places, own, latent, near_rows, far_rows, held_first, held_rest, patches,
    near_out, far_out, windows, spread, tokens, total, wide,
):
    even = places[0] != 0
    edge_conv(even, own, near_rows, far_rows, held_first, held_rest, total, wide)
    groups, depth, _, pair = latent.shape
    width = pair // 2
    channels = near_rows.shape[1]
    start = depth * own.shape[3]
    part = width // 2
    half = windows.shape[3]
    block = half // groups
    tokens[...] = jnp.zeros_like(tokens)
    for src in range(groups):
        at = slice(8 + src * block, 8 + (src + 1) * block)
        for frame in range(depth):
            value = latent[src, frame].astype(f32)[:block]
            tokens[frame, 1, at] = value[:, :width]
            tokens[frame, 2, at] = value[:, width:]
            row, lane = tail_place(frame, start, channels)
            ends = [
                ref[row : row + slots, lane : lane + lanes].astype(f32)[:block]
                for ref in (near_rows, far_rows)
            ]
            pick = slice(src * part, (src + 1) * part)
            none = jnp.zeros((block, part), f32)
            above = jnp.where(even, ends[1], ends[0])[:, pick]
            below = jnp.where(even, ends[0], ends[1])[:, pick]
            tokens[frame, 0, at] = jnp.concatenate([none, above], axis=-1)
            tokens[frame, 3, at] = jnp.concatenate([below, none], axis=-1)
    for q in range(2):
        left = tokens[:, :, 7 + q : 7 + q + half]
        right = tokens[:, :, 8 + q : 8 + q + half]
        windows[q] = jnp.concatenate([left, right], axis=-1).astype(bf16)
    spread[...] = jnp.zeros_like(spread)
    latent_phase(total, (0, 1), (0, 1), 0, windows, patches, spread)
    for n, row in enumerate((0, 3)):
        tokens[:, n, 0:half] = shares_of(spread, row, half)
    fill = jnp.zeros((slots - block, groups * part), f32)
    for frame in range(depth):
        up, down = [
            jnp.concatenate(
                [
                    tokens[frame, n, dst * block : (dst + 1) * block][:, lo : lo + part]
                    for dst in range(groups)
                ],
                axis=-1,
            )
            for n, lo in ((0, part), (1, 0))
        ]
        padded = lambda v: jnp.concatenate([v, fill], axis=0).astype(bf16)
        near_out[frame] = padded(jnp.where(even, down, up))
        far_out[frame] = padded(jnp.where(even, up, down))


def edge_part(places, own, latent, near_rows, far_rows, held_first, held_rest, patches):
    groups, depth, _, pair = latent.shape
    blocks, frames, _, cols, _ = own.shape
    out = jax.ShapeDtypeStruct((depth, slots, groups * pair // 4), bf16)
    return pl.pallas_call(
        edge_kernel,
        out_shape=[
            out,
            out,
            jax.ShapeDtypeStruct((2, depth, 4, cols // 2, pair), bf16),
            jax.ShapeDtypeStruct((depth, 4, cols // 2 + 8, pair), f32),
        ],
        in_specs=[scalars] + [whole] * 7,
        out_specs=[whole] * 4,
        scratch_shapes=[
            pltpu.VMEM((depth, 4, 72, pair // 2), f32),
            pltpu.VMEM((blocks, frames, 2, cols, lanes), f32),
            pltpu.VMEM((2, depth, cols, 3 * blocks * lanes), bf16),
        ],
        compiler_params=params(14),
        cost_estimate=pl.CostEstimate(
            flops=2 * 6 * own.size * blocks * lanes, bytes_accessed=0, transcendentals=own.size
        ),
        name="edge_part",
    )(places, own, latent, near_rows, far_rows, held_first, held_rest, patches)


def inner_kernel(own, windows, patches, spread_in, out, spread, tokens):
    half = windows.shape[3]
    groups, depth = out.shape[:2]
    block = half // groups
    spread[...] = spread_in[:, 1:3]
    latent_phase(own, (2, 1), (1, 0), 1, windows, patches, spread)
    for row in range(2):
        tokens[:, row] = shares_of(spread, row, half)
    fill = jnp.zeros((slots - block, out.shape[-1]), f32)
    for dst in range(groups):
        at = slice(dst * block, (dst + 1) * block)
        for frame in range(depth):
            value = jnp.concatenate([tokens[frame, 0, at], tokens[frame, 1, at]], axis=-1)
            out[dst, frame] = jnp.concatenate([value, fill], axis=0)


def inner_part(own, windows, patches, spread, groups):
    cols = own.shape[3]
    depth, _, wide, pair = spread.shape
    return pl.pallas_call(
        inner_kernel,
        out_shape=jax.ShapeDtypeStruct((groups, depth, slots, pair), f32),
        in_specs=[whole] * 4,
        out_specs=whole,
        scratch_shapes=[
            pltpu.VMEM((depth, 2, wide, pair), f32),
            pltpu.VMEM((depth, 2, cols // 2, pair // 2), f32),
        ],
        compiler_params=params(10),
        cost_estimate=pl.CostEstimate(
            flops=8 * own.size * 6 * pair, bytes_accessed=0, transcendentals=own.size
        ),
        name="inner_part",
    )(own, windows, patches, spread)


def share_kernel(places, centre, near_share, far_share, *rest):
    pieces, total = rest[:-1], rest[-1]
    even = places[0] != 0
    groups = len(pieces)
    near, far = near_share[...].astype(f32), far_share[...].astype(f32)
    first = jnp.where(even, far, near)
    last = jnp.where(even, near, far)
    part = centre.shape[-1] // 4
    none = jnp.zeros(first.shape[:2] + (2 * part,), f32)
    for dst in range(groups):
        pick = slice(dst * part, (dst + 1) * part)
        terms = jnp.concatenate([first[:, :, pick], none, last[:, :, pick]], axis=-1)
        total[dst] = centre[dst] + terms
    for step, piece in enumerate(pieces):
        piece[...] = total[lax.rem(places[2] + step, groups)].astype(bf16)


def share_pieces(places, centre, near_share, far_share):
    groups = centre.shape[0]
    return pl.pallas_call(
        share_kernel,
        out_shape=[jax.ShapeDtypeStruct(centre.shape[1:], bf16)] * groups,
        in_specs=[scalars] + [whole] * 3,
        out_specs=[whole] * groups,
        scratch_shapes=[pltpu.VMEM(centre.shape, f32)],
        compiler_params=params(4),
        name="share_pieces",
    )(places, centre, near_share, far_share)


def weight_kernel(places, modulated, *rest):
    shares, token_grad, pieces, (field, weight) = rest[:4], rest[4], rest[5:9], rest[9:]
    groups = len(shares)
    depth, _, pair = shares[0].shape
    width = pair // 2
    frames = modulated.shape[0]
    model = modulated.shape[-1]
    field[...] = jnp.zeros_like(field)
    for step, share in enumerate(shares):
        src = lax.rem(places[2] + groups - step, groups)
        field[pl.ds(src * (frames // groups), depth)] += share[...].astype(f32)
    values = field[2 : 2 + frames]
    token_grad[:, 0] = values[:, :, :width].astype(bf16)
    token_grad[:, 1] = values[:, :, width:].astype(bf16)
    turned = jnp.transpose(token_grad[...].reshape(-1, width).astype(f32)).astype(bf16)
    total = dot(turned, modulated[...].reshape(-1, model))
    half = model // (2 * groups)
    for dst in range(groups):
        at = 2 * half * dst
        weight[dst, :width] = total[:, at : at + half]
        weight[dst, width:] = total[:, at + half : at + 2 * half]
    for step, piece in enumerate(pieces):
        dst = lax.rem(places[2] + step, groups)
        piece[...] = jnp.transpose(weight[dst]).astype(bf16)


def weight_terms(places, modulated, shares):
    groups = len(shares)
    depth, _, pair = shares[0].shape
    frames, token_rows, _, model = modulated.shape
    half = model // (2 * groups)
    return pl.pallas_call(
        weight_kernel,
        out_shape=[jax.ShapeDtypeStruct((frames, token_rows, slots, pair // 2), bf16)]
        + [jax.ShapeDtypeStruct((half, pair), bf16)] * groups,
        in_specs=[scalars] + [whole] * (1 + groups),
        out_specs=[whole] * (1 + groups),
        scratch_shapes=[
            pltpu.VMEM((frames + 2, slots, pair), f32),
            pltpu.VMEM((groups, pair, half), f32),
        ],
        compiler_params=params(12),
        name="weight_terms",
    )(places, modulated, *shares)


def middle_kernel(*refs):
    refs, send, total = refs[:-2], refs[-2], refs[-1]
    count = send.shape[0]
    total[...] = sum(ref[...].astype(f32) for ref in refs)
    depth, pair = total.shape
    width = pair // 2
    rows = 2 * depth // count
    half = rows // 2
    fill = jnp.zeros((send.shape[1] - half, pair), f32)
    for n in range(count):
        at, lane = n % (count // 2) * rows, n // (count // 2) * width
        value = total[at : at + rows, lane : lane + width]
        value = jnp.concatenate([value[:half], value[half:]], axis=-1)
        send[n] = jnp.concatenate([value, fill], axis=0).astype(bf16)


def middle_sum(got, count):
    depth, pair = got[0].shape
    rows = -(-depth // count // 16) * 16
    return pl.pallas_call(
        middle_kernel,
        out_shape=jax.ShapeDtypeStruct((count, rows, pair), bf16),
        in_specs=[whole] * len(got),
        out_specs=whole,
        scratch_shapes=[pltpu.VMEM((depth, pair), f32)],
        compiler_params=params(4),
        name="middle_sum",
    )(*got)


def final_kernel(factor, pieces, out):
    half, width = out.shape[0] // 2, out.shape[1]
    total = jnp.sum(pieces[...].astype(f32), axis=0) * factor
    out[:half] = total[:half, :width]
    out[half:] = total[:half, width:]


def final_sum(pieces, rows, factor):
    return pl.pallas_call(
        functools.partial(final_kernel, factor),
        out_shape=jax.ShapeDtypeStruct((rows, pieces.shape[2] // 2), f32),
        in_specs=[whole],
        out_specs=whole,
        compiler_params=params(4),
        name="final_sum",
    )(pieces)


def hidden_kernel(hidden, token_grad, scale, w_out, grad_hidden):
    frames, token_rows, tokens, width = hidden.shape
    gain = 1.0 + scale[...]
    block = 3

    def share(step, carry):
        rows = token_grad[pl.ds(step * block, block)].reshape(-1, token_grad.shape[-1])
        mod_grad = dot(rows, w_out[...])
        for frame in range(block):
            for row in range(token_rows):
                at = (frame * token_rows + row) * slots
                scaled = mod_grad[at : at + tokens] * gain
                normed, inverse = normalise(hidden[step * block + frame, row].astype(f32))
                first = jnp.mean(scaled, axis=-1, keepdims=True)
                second = jnp.mean(scaled * normed, axis=-1, keepdims=True)
                value = (scaled - first - normed * second) * inverse
                grad_hidden[step * block + frame, row] = value.astype(bf16)
        return carry

    lax.fori_loop(0, frames // block, share, 0)


def hidden_grad(hidden, token_grad, mod_scale, w_out):
    frames, token_rows, tokens, width = hidden.shape
    return pl.pallas_call(
        hidden_kernel,
        out_shape=jax.ShapeDtypeStruct(hidden.shape, bf16),
        in_specs=[whole] * 4,
        out_specs=whole,
        compiler_params=params(8),
        cost_estimate=pl.CostEstimate(
            flops=2 * frames * 2 * slots * width * w_out.shape[0],
            bytes_accessed=8 * frames * slots * width,
            transcendentals=0,
        ),
        name="hidden_grad",
    )(hidden, token_grad, mod_scale.reshape(1, -1), w_out)


def shards(hidden, mod_scale, mod_shift, w_out, w_in, w_section, section_grad):
    groups, strips = lax.axis_size("tm"), lax.axis_size("height")
    rows = section_grad.shape[1]
    swap = lambda a, b: [(a, b), (b, a)]
    near = sum([swap(i, i + 1) for i in range(0, strips - 1, 2)], [])
    far = sum([swap(i, i + 1) for i in range(1, strips - 1, 2)], [])
    odd = lax.rem(lax.axis_index("height"), 2)
    places = jnp.stack([(1 - odd) * (rows - 1), odd * (rows - 1), lax.axis_index("tm")])
    places = places.astype(jnp.int32)
    w_out = jnp.transpose(w_out)
    w_section = pltpu.with_memory_space_constraint(w_section, pltpu.HBM)

    def round_tm(pieces):
        hops = lambda k: [(g, (g + k) % groups) for g in range(groups)]
        return [pieces[0]] + [
            lax.ppermute(pieces[k], "tm", hops(k)) for k in range(1, groups)
        ]

    ends, between = fetch(pltpu.with_memory_space_constraint(section_grad, pltpu.HBM))
    ends, hidden = lax.optimization_barrier((ends, hidden))
    earlier = [(g + 1, g) for g in range(groups - 1)]
    ends = lax.ppermute(ends, "tm", earlier)
    modulated, held_first, *pieces = modulate(
        places,
        hidden,
        mod_scale,
        mod_shift,
        w_out,
        w_section,
        groups,
    )
    section_grad, pieces = lax.optimization_barrier((section_grad, pieces))
    wide, patches = widen_rows(section_grad, w_in)
    pieces = round_tm(pieces)
    between, pieces, wide = lax.optimization_barrier((between, pieces, wide))
    between = lax.ppermute(between, "tm", earlier)
    near_send, far_send, latent = pack_rows(places, section_grad, ends, pieces)
    far_rows = lax.ppermute(far_send, "height", far)
    near_rows = lax.ppermute(near_send, "height", near)
    own, held_rest = own_part(wide, ends, between, w_section, held_first)
    near_share, far_share, windows, spread = edge_part(
        places, own, latent, near_rows, far_rows, held_first, held_rest, patches
    )
    far_share = lax.ppermute(far_share, "height", far)
    near_share = lax.ppermute(near_share, "height", near)
    centre = inner_part(own, windows, patches, spread, groups)
    shares = round_tm(share_pieces(places, centre, near_share, far_share))
    token_grad, *pieces = weight_terms(places, modulated, shares)
    got = round_tm(pieces)
    grad_hidden = hidden_grad(hidden, token_grad, mod_scale, w_out)
    pieces = lax.all_to_all(middle_sum(got, strips), "height", 0, 0, tiled=True)
    total_tokens = math.prod(hidden.shape[:3]) * groups * strips
    model_rows = w_out.shape[1] // (groups * strips)
    grad_out_weight = final_sum(pieces, model_rows, 1.0 / math.sqrt(total_tokens))
    return (grad_hidden, grad_out_weight)


def solution(mesh):
    placed = (P(None, "height", "tm", None), P(), P(), P(), P(), P(), P("tm", "height", None, None))
    return jax.shard_map(
        shards,
        mesh=mesh,
        in_specs=placed,
        out_specs=(P(None, "height", "tm", None), P(("tm", "height"), None)),
        check_vma=False,
    )
```
